32 devices in a mesh: rep: 2 (over y), tok: 4 (over x, core), col: 4 (over z).
Axes of the slice: x: 2, y: 2, z: 4, core: 2. Of those that a mesh axis runs over, the one named last changes fastest.
Arguments:
- request_rows: bfloat16 [64, 10240], P(('rep', 'tok', 'col')), parts along dimension 0, may hold values from -100 to 100
- key_cache: bfloat16 [96, 16, 2048], P(('rep', 'tok', 'col')), parts along dimension 0, may hold values from -3 to 3
- route_list: int32 [8, 4, 3], P('rep', 'col'), parts along dimension 0, may hold values from 0 to 7, as said below
- route_count: int32 [8, 4], P('rep', 'col'), parts along dimension 0, may hold values from 1 to 3, as said below
- norm_gain: float32 [8192], replicated, may hold values from 0.1 to 1.9
- gate_weight: bfloat16 [8192, 16384], P('tok', 'col'), may hold values from -0.0625 to 0.0625
- up_weight: bfloat16 [8192, 16384], P('tok', 'col'), may hold values from -0.0625 to 0.0625
- down_weight: bfloat16 [16384, 8192], P('col', 'tok'), may hold values from -0.046875 to 0.046875
- gate_delta: bfloat16 [4, 4, 4, 128, 128], P('tok', 'col'), may hold values from -0.29882812 to 0.29882812
- up_delta: bfloat16 [4, 4, 4, 128, 128], P('tok', 'col'), may hold values from -0.29882812 to 0.29882812
- down_delta: bfloat16 [4, 4, 4, 128, 128], P('tok', 'col'), may hold values from -0.29882812 to 0.29882812
- tile_index: int32 [4, 4, 3, 4, 3], P('tok', 'col'), may hold values from 0 to 31, as said below
Outputs:
- attended: bfloat16 [96, 8192], P(('rep', 'tok', 'col')), parts along dimension 0
- ffn_out: bfloat16 [96, 8192], P(('rep', 'col'), 'tok'), parts along dimension 0
The draws below stay inside these ranges and needn't reach their ends.
There are 2 independent parts, one for each index of `rep`. The reference program is written for one: setup_inputs(seed, part) draws one part's arguments, and reference() takes and returns one part's arrays. A program takes and returns all parts, laid end to end along the dimension named above; an argument that names none is the same for every part. Nothing has to cross between parts.
Inputs may be any that keep to these rules, and one draw needn't show every extreme that they name: `route_list`: every request is placed in exactly one live slot of its own lane; each source device places at most one request with each owner of its lane; some owner of every lane holds 3 requests; entries of empty slots are 0. `route_count`: the counts of a lane sum to 8; some count of every lane is 3. `tile_index`: variant ids are below 2; row and column blocks of gate and up tiles are below 16 and 32, of down tiles the other way round; tiles may repeat.
All inputs are finite; a program needn't handle non-finite values.
Results may differ from the reference program's by a relative error of at most 0.025.
Values may be sent and summed in bfloat16 or wider, within the bound.
No kernel may reach another device: no remote copies, remote signals or barrier semaphores. Data moves between devices by JAX's collectives and lax.ppermute only.
A program may use at most 128 MiB of HBM per device.

```python
import jax
import jax.numpy as jnp
from jax import lax

D = 8192
HEADS = 64
KV_HEADS = 8
HEAD_DIM = 128
FFW = 16384
BLOCK = 128
CTX = 16
REQ_DEV = 2
TILE_DEV = 4
CAP = 3
VARIANTS = 2
SLOTS = 48
REQS = 32
WIDTH = 10240
N_TOK = 4
N_COL = 4


def lane_table(lane_key):
    owner_key, shift_key, source_key = jax.random.split(lane_key, 3)
    owners = jax.random.permutation(owner_key, N_TOK)
    shifts = jax.random.randint(shift_key, (N_TOK // 2,), -1, 2)
    shifts = shifts.at[0].set(1)
    ordered = jnp.stack([REQ_DEV + shifts, REQ_DEV - shifts], axis=1).reshape(N_TOK)
    loads = jnp.zeros((N_TOK,), jnp.int32).at[owners].set(ordered.astype(jnp.int32))
    sources = jax.random.permutation(source_key, N_TOK)
    starts = jnp.cumsum(loads) - loads
    places = jnp.arange(CAP, dtype=jnp.int32)
    flat = starts[:, None] + places[None, :]
    entries = sources[flat % N_TOK] * REQ_DEV + flat // N_TOK
    entries = jnp.where(places[None, :] < loads[:, None], entries, 0)
    return (entries.astype(jnp.int32), loads.astype(jnp.int32))


def route_tables(key):
    table_key = jax.random.fold_in(key, 11)
    entries, loads = jax.vmap(lane_table)(jax.random.split(table_key, N_COL))
    return (jnp.transpose(entries, (1, 0, 2)), jnp.transpose(loads, (1, 0)))


def request_base(key):
    row_key = jax.random.fold_in(key, 23)
    return jnp.clip(jax.random.normal(row_key, (REQS, WIDTH), jnp.float32), -3.0, 3.0)


def draw_route_list(key, part):
    entries, loads = route_tables(key)
    return entries


def draw_route_count(key, part):
    entries, loads = route_tables(key)
    return loads


def draw_request_rows(key, part):
    base_rows = request_base(key)
    return base_rows.astype(jnp.bfloat16)


def draw_key_cache(key, part):
    key = jax.random.fold_in(key, 2)
    cached = jnp.clip(jax.random.normal(key, (SLOTS, CTX, 2 * KV_HEADS * HEAD_DIM), jnp.float32), -3.0, 3.0)
    return cached.astype(jnp.bfloat16)


def draw_tile_index(key, part):
    key = jax.random.fold_in(key, 5)
    variant_key, row_key, col_key = jax.random.split(key, 3)
    tile_shape = (N_TOK, N_COL, 3, TILE_DEV)
    variants = jax.random.randint(variant_key, tile_shape, 0, VARIANTS)
    d_blocks = D // (N_TOK * BLOCK)
    f_blocks = FFW // (N_COL * BLOCK)
    row_limit = jnp.array([d_blocks, d_blocks, f_blocks], jnp.int32)[None, None, :, None]
    col_limit = jnp.array([f_blocks, f_blocks, d_blocks], jnp.int32)[None, None, :, None]
    rows_drawn = jax.random.randint(row_key, tile_shape, 0, 1 << 20) % row_limit
    cols_drawn = jax.random.randint(col_key, tile_shape, 0, 1 << 20) % col_limit
    return jnp.stack([variants, rows_drawn, cols_drawn], axis=-1).astype(jnp.int32)


def steps_of(key, shape, pieces, least, largest):
    gain, own = 1.0, jax.random.fold_in(key, 6)
    for dim, blocks in pieces:
        steps = jnp.exp(jax.random.uniform(jax.random.fold_in(own, dim), (blocks,), jnp.float32, least / len(pieces), largest / len(pieces)))
        gain = gain * jnp.repeat(steps, shape[dim] // blocks).reshape([-1 if axis == dim else 1 for axis in range(len(shape))])
    return gain


def normal_values(key, dims, scale, most, cuts=(), held_as=jnp.bfloat16):
    drawn = jax.random.normal(key, dims, jnp.float32) * scale
    if len(cuts) > 0:
        drawn = steps_of(key, dims, cuts, -0.22, 0.18) * drawn
    return jnp.clip(drawn, min=-most, max=most).astype(held_as)


def setup_inputs(seed: int = 0, part: int = 0) -> dict:
    key_of = jax.random.split(jax.random.key(seed), 13)
    part_keys = jax.random.split(jax.random.fold_in(key_of[12], part), 13)
    request_rows = draw_request_rows(jax.random.fold_in(jax.random.fold_in(key_of[12], part), 71), part)
    key_cache = draw_key_cache(jax.random.fold_in(jax.random.fold_in(key_of[12], part), 71), part)
    route_list = draw_route_list(jax.random.fold_in(jax.random.fold_in(key_of[12], part), 71), part)
    route_count = draw_route_count(jax.random.fold_in(jax.random.fold_in(key_of[12], part), 71), part)
    norm_gain = jnp.clip(1.0 + 0.18 * jax.random.normal(key_of[4], (D,), jnp.float32), 0.1, 1.9)
    gate_weight = normal_values(key_of[5], (D, FFW), D ** -0.5, 0.0625, ((0, 4), (1, 4)))
    up_weight = normal_values(key_of[6], (D, FFW), D ** -0.5, 0.0625, ((0, 4), (1, 4)))
    down_weight = normal_values(key_of[7], (FFW, D), FFW ** -0.5, 0.046875, ((0, 4), (1, 4)))
    gate_delta = normal_values(key_of[8], (N_TOK, N_COL, TILE_DEV, BLOCK, BLOCK), 0.05, 0.29882812, ((0, 4), (1, 4)))
    up_delta = normal_values(key_of[9], (N_TOK, N_COL, TILE_DEV, BLOCK, BLOCK), 0.05, 0.29882812, ((0, 4), (1, 4)))
    down_delta = normal_values(key_of[10], (N_TOK, N_COL, TILE_DEV, BLOCK, BLOCK), 0.05, 0.29882812, ((0, 4), (1, 4)))
    tile_index = draw_tile_index(jax.random.fold_in(key_of[12], 71), part)
    return {"request_rows": request_rows, "key_cache": key_cache, "route_list": route_list, "route_count": route_count, "norm_gain": norm_gain, "gate_weight": gate_weight, "up_weight": up_weight, "down_weight": down_weight, "gate_delta": gate_delta, "up_delta": up_delta, "down_delta": down_delta, "tile_index": tile_index}


def attend(slot_rows, key_cache, live_mask):
    slot_count = slot_rows.shape[0]
    group_size = HEADS // KV_HEADS
    query_width = HEADS * HEAD_DIM
    pair_width = KV_HEADS * HEAD_DIM
    queries = slot_rows[:, :query_width].astype(jnp.float32).reshape(slot_count, KV_HEADS, group_size, HEAD_DIM)
    own_keys = slot_rows[:, query_width:query_width + pair_width].astype(jnp.float32).reshape(slot_count, KV_HEADS, HEAD_DIM)
    own_values = slot_rows[:, query_width + pair_width:].astype(jnp.float32).reshape(slot_count, KV_HEADS, HEAD_DIM)
    cached_keys = key_cache[:, :, :pair_width].astype(jnp.float32).reshape(slot_count, -1, KV_HEADS, HEAD_DIM)
    cached_values = key_cache[:, :, pair_width:].astype(jnp.float32).reshape(slot_count, -1, KV_HEADS, HEAD_DIM)
    score_scale = HEAD_DIM ** (-0.5)
    past_scores = jnp.einsum('skgd,sjkd->skgj', queries, cached_keys) * score_scale
    own_scores = jnp.einsum('skgd,skd->skg', queries, own_keys) * score_scale
    row_top = jnp.maximum(lax.optimization_barrier(jnp.max(past_scores, axis=-1)), own_scores)
    past_exp = jnp.exp(past_scores - row_top[..., None])
    own_exp = jnp.exp(own_scores - row_top)
    weight_total = lax.optimization_barrier(jnp.sum(past_exp, axis=-1)) + own_exp
    past_weights = lax.optimization_barrier((past_exp / weight_total[..., None]).astype(jnp.bfloat16)).astype(jnp.float32)
    own_weights = lax.optimization_barrier((own_exp / weight_total).astype(jnp.bfloat16)).astype(jnp.float32)
    mixed = jnp.einsum('skgj,sjkd->skgd', past_weights, cached_values)
    mixed = mixed + own_weights[..., None] * own_values[:, :, None, :]
    return (mixed.reshape(slot_count, query_width) * live_mask[:, None].astype(jnp.float32)).astype(jnp.bfloat16)

def normalize(attended, norm_gain):
    values = attended.astype(jnp.float32)
    spread = lax.optimization_barrier(jnp.mean(values * values, axis=-1, keepdims=True))
    return (values * lax.rsqrt(spread + 1e-06) * norm_gain.astype(jnp.float32)).astype(jnp.bfloat16)

def add_tiles(partial_value, source, delta_tiles, tile_list, per_variant, out_base):
    block_width = delta_tiles.shape[-1]
    for slot_tile in range(delta_tiles.shape[0]):
        first_row = tile_list[slot_tile, 0] * per_variant
        block_in = lax.dynamic_slice(source, (first_row, tile_list[slot_tile, 1] * block_width), (per_variant, block_width))
        product = jnp.dot(block_in, delta_tiles[slot_tile], preferred_element_type=jnp.float32)
        position = (first_row, out_base + tile_list[slot_tile, 2] * block_width)
        current = lax.dynamic_slice(partial_value, position, (per_variant, block_width))
        partial_value = lax.dynamic_update_slice(partial_value, current + product, position)
    return partial_value

def reference(request_rows, key_cache, route_list, route_count, norm_gain, gate_weight, up_weight, down_weight, gate_delta, up_delta, down_delta, tile_index):
    lanes = request_rows.reshape(N_TOK, N_COL, REQ_DEV, -1).transpose(1, 0, 2, 3).reshape(N_COL, N_TOK * REQ_DEV, -1)
    picked = jax.vmap(lambda lane_rows, lane_list: jnp.take(lane_rows, lane_list, axis=0), in_axes=(0, 1), out_axes=1)(lanes, route_list)
    live_mask = (jnp.arange(CAP, dtype=jnp.int32)[None, None, :] < route_count[:, :, None]).reshape(SLOTS)
    slot_rows = jnp.where(live_mask[:, None], picked.reshape(SLOTS, -1), jnp.zeros((), request_rows.dtype))
    attended = attend(slot_rows, key_cache, live_mask)
    normed = normalize(attended, norm_gain)
    feature_width = D // N_TOK
    hidden_width = FFW // N_COL
    per_variant = 2 * N_COL * CAP

    def gate_step(carry, tok_shard):
        rows_part = lax.dynamic_slice_in_dim(normed, tok_shard * feature_width, feature_width, 1)
        gate_part = jnp.dot(rows_part, lax.dynamic_slice_in_dim(gate_weight, tok_shard * feature_width, feature_width, 0), preferred_element_type=jnp.float32)
        up_part = jnp.dot(rows_part, lax.dynamic_slice_in_dim(up_weight, tok_shard * feature_width, feature_width, 0), preferred_element_type=jnp.float32)
        for lane_index in range(N_COL):
            gate_part = add_tiles(gate_part, rows_part, gate_delta[tok_shard, lane_index], tile_index[tok_shard, lane_index, 0], per_variant, lane_index * hidden_width)
            up_part = add_tiles(up_part, rows_part, up_delta[tok_shard, lane_index], tile_index[tok_shard, lane_index, 1], per_variant, lane_index * hidden_width)
        gate_round = lax.optimization_barrier(gate_part.astype(jnp.bfloat16)).astype(jnp.float32)
        up_round = lax.optimization_barrier(up_part.astype(jnp.bfloat16)).astype(jnp.float32)
        return ((carry[0] + gate_round, carry[1] + up_round), None)
    empty = jnp.zeros((SLOTS, FFW), jnp.float32)
    (gate_sum, up_sum), unused = lax.scan(gate_step, (empty, empty), jnp.arange(N_TOK, dtype=jnp.int32))
    hidden = (jax.nn.silu(gate_sum) * up_sum).astype(jnp.bfloat16)

    def down_step(carry, lane_index):
        hidden_part = lax.dynamic_slice_in_dim(hidden, lane_index * hidden_width, hidden_width, 1)
        down_part = jnp.dot(hidden_part, lax.dynamic_slice_in_dim(down_weight, lane_index * hidden_width, hidden_width, 0), preferred_element_type=jnp.float32)
        for tok_shard in range(N_TOK):
            down_part = add_tiles(down_part, hidden_part, down_delta[tok_shard, lane_index], tile_index[tok_shard, lane_index, 2], per_variant, tok_shard * feature_width)
        return (carry + lax.optimization_barrier(down_part.astype(jnp.bfloat16)).astype(jnp.float32), None)
    down_sum, unused = lax.scan(down_step, jnp.zeros((SLOTS, D), jnp.float32), jnp.arange(N_COL, dtype=jnp.int32))
    return (attended, down_sum.astype(jnp.bfloat16))
```

```python
import functools

import jax
import jax.numpy as jnp
from jax import lax
from jax.experimental import pallas as pl
from jax.experimental.pallas import tpu as pltpu
from jax.sharding import PartitionSpec as P

HEADS = 64
KV_HEADS = 8
HEAD_DIM = 128
GROUP = HEADS // KV_HEADS
MIB = 1 << 20
BF16 = jnp.bfloat16
F32 = jnp.float32
VMEM = pltpu.VMEM
HBM = pltpu.HBM
SMEM = pltpu.SMEM


def call(kernel, name, ins, outs, scratch=(), limit=8, cost=None):
    arrays = [pltpu.with_memory_space_constraint(a, s) if s is not SMEM else a for a, s in ins]
    return pl.pallas_call(
        kernel,
        name=name,
        in_specs=[pl.BlockSpec(memory_space=s) for _, s in ins],
        out_specs=[pl.BlockSpec(memory_space=VMEM) for _ in outs],
        out_shape=[VMEM(shape, dtype) for shape, dtype in outs],
        scratch_shapes=list(scratch),
        cost_estimate=cost,
        compiler_params=pltpu.CompilerParams(vmem_limit_bytes=limit * MIB),
    )(*arrays)


class Sizes:
    def __init__(self, toks, cols, cap):
        self.toks, self.cols, self.cap = toks, cols, cap
        self.heads = HEADS // toks
        self.kvs = max(1, self.heads // GROUP)
        self.group = self.heads // self.kvs
        self.lane_slots = toks * cap
        self.rows = toks * cols * cap
        self.req_rows = -(-(self.heads + 2 * self.kvs) // 16) * 16
        self.blocks = 2 * self.kvs
        self.pieces = 2 * self.req_rows // 16
        self.cache_rows = None

    def first_kv(self, tok):
        return tok * self.heads // GROUP


def pack_kernel(z, ctx, req_ref, cache_ref, *rest):
    outs, (wide, rows, sems) = rest[: z.toks], rest[z.toks :]
    tok = lax.axis_index("tok")
    width = z.kvs * HEAD_DIM
    cache_rows = z.cap * ctx
    pairs = KV_HEADS * HEAD_DIM
    copies = []
    for s in range(z.toks):
        first = pl.multiple_of(z.first_kv(tok ^ s) * HEAD_DIM, HEAD_DIM)
        for half in range(2):
            for k in range(z.cap):
                copy = pltpu.make_async_copy(
                    cache_ref.at[k, :, pl.ds(half * pairs + first, width)],
                    outs[s].at[pl.ds(k * ctx, ctx), pl.ds(half * width, width)],
                    sems.at[s, half, k],
                )
                copy.start()
                copies.append(copy)
    wide[...] = req_ref[...].astype(F32)
    rows[...] = jnp.zeros_like(rows)
    for s in range(z.toks):
        to = tok ^ s
        starts = [(to * z.heads + h) * HEAD_DIM for h in range(z.heads)]
        for half in range(2):
            starts += [
                HEADS * HEAD_DIM + half * pairs + (z.first_kv(to) + j) * HEAD_DIM
                for j in range(z.kvs)
            ]
        for r in range(2):
            for n, start in enumerate(starts):
                rows[r * z.req_rows + n : r * z.req_rows + n + 1, :] = wide[
                    r : r + 1, pl.ds(pl.multiple_of(start, HEAD_DIM), HEAD_DIM)
                ]
        for p in range(z.pieces):
            at, lane = cache_rows + p // z.blocks * 16, p % z.blocks * HEAD_DIM
            outs[s][at : at + 16, lane : lane + HEAD_DIM] = rows[p * 16 : p * 16 + 16, :].astype(BF16)
    for copy in copies:
        copy.wait()


def attend_kernel(z, ctx, list_ref, count_ref, gain_ref, *rest):
    pieces, rest = rest[: z.toks], rest[z.toks :]
    send_ref, back_refs = rest[0], rest[1 : 1 + z.toks]
    cache, req, query, own_key, own_value, alive, mixed_all = rest[1 + z.toks :]
    tok = lax.axis_index("tok")
    cache_rows = z.cap * ctx
    for s in range(z.toks):
        source = tok ^ s
        cache[source] = pieces[s][:cache_rows, :]
        for p in range(z.pieces):
            at, lane = cache_rows + p // z.blocks * 16, p % z.blocks * HEAD_DIM
            r, part = p * 16 // z.req_rows, p * 16 % z.req_rows
            req[source * 2 + r, part : part + 16, :] = pieces[s][
                at : at + 16, lane : lane + HEAD_DIM
            ].astype(F32)
    for g in range(z.toks):
        for k in range(z.cap):
            live = (k < count_ref[g, 0]).astype(F32)
            rows = req[list_ref[g, 0, k]] * live
            at = (g * z.cap + k) * z.group
            for j in range(z.kvs):
                query[j, at : at + z.group, :] = rows[j * z.group : (j + 1) * z.group, :]
                key, value = z.heads + j, z.heads + z.kvs + j
                own_key[j, at : at + z.group, :] = jnp.broadcast_to(
                    rows[key : key + 1, :], (z.group, HEAD_DIM)
                )
                own_value[j, at : at + z.group, :] = jnp.broadcast_to(
                    rows[value : value + 1, :], (z.group, HEAD_DIM)
                )
            alive[at : at + z.group, :] = jnp.full((z.group, HEAD_DIM), live, F32)
    many, keys = z.lane_slots * z.group, z.toks * cache_rows
    row_slot = lax.broadcasted_iota(jnp.int32, (many, keys), 0) // z.group
    key_slot = lax.broadcasted_iota(jnp.int32, (many, keys), 1) // ctx
    same = row_slot == key_slot
    scale = HEAD_DIM ** (-0.5)
    for j in range(z.kvs):
        cached_keys = cache[:, :, j * HEAD_DIM : (j + 1) * HEAD_DIM].reshape(keys, HEAD_DIM)
        at = (z.kvs + j) * HEAD_DIM
        cached_values = cache[:, :, at : at + HEAD_DIM].reshape(keys, HEAD_DIM)
        past = (
            lax.dot_general(
                query[j].astype(BF16),
                cached_keys,
                (((1,), (1,)), ((), ())),
                preferred_element_type=F32,
            )
            * scale
        )
        own = jnp.sum(query[j] * own_key[j], axis=-1, keepdims=True) * scale
        top = jnp.maximum(jnp.max(jnp.where(same, past, -jnp.inf), axis=-1, keepdims=True), own)
        past_exp = jnp.where(same, jnp.exp(jnp.where(same, past - top, 0.0)), 0.0)
        own_exp = jnp.exp(own - top)
        total = jnp.sum(past_exp, axis=-1, keepdims=True) + own_exp
        weights = (past_exp / total).astype(BF16)
        own_weight = (own_exp / total).astype(BF16).astype(F32)
        mixed = jnp.dot(weights, cached_values, preferred_element_type=F32)
        mixed = (mixed + own_weight * own_value[j]) * alive[...]
        mixed_all[j * many : (j + 1) * many, :] = mixed.astype(BF16).astype(F32)
    block = z.cap * z.group
    for s in range(z.toks):
        for j in range(z.kvs):
            at = pl.multiple_of(j * many + (tok ^ s) * block, block if block % 8 == 0 else 4)
            back_refs[s][j * block : (j + 1) * block, :] = mixed_all[pl.ds(at, block), :].astype(BF16)
    count = z.kvs * z.lane_slots
    wide = z.group * HEAD_DIM
    row_kv = lax.broadcasted_iota(jnp.int32, (count, HEAD_DIM), 0) // z.lane_slots
    squares = jnp.zeros((count, HEAD_DIM), F32)
    for h in range(z.group):
        values = mixed_all[pl.ds(h, count, stride=z.group), :]
        squares = squares + values * values
        gain = jnp.zeros((count, HEAD_DIM), F32)
        for j in range(z.kvs):
            at = pl.multiple_of(tok * z.heads * HEAD_DIM, HEAD_DIM) + (j * z.group + h) * HEAD_DIM
            gain = jnp.where(row_kv == j, gain_ref[:, pl.ds(at, HEAD_DIM)], gain)
        send_ref[:, h * HEAD_DIM : (h + 1) * HEAD_DIM] = (values * gain).astype(BF16)
    high, low = halves(jnp.sum(squares, axis=-1, keepdims=True))
    send_ref[:, wide:] = two_lanes(high, low, count)


def halves(value):
    high = value.astype(BF16).astype(F32)
    return high, value - high


def two_lanes(high, low, rows):
    lane = lax.broadcasted_iota(jnp.int32, (rows, HEAD_DIM), 1)
    return jnp.where(lane == 0, high, jnp.where(lane == 1, low, 0.0)).astype(BF16)


def slot_of_row(z, col, shape):
    row = lax.broadcasted_iota(jnp.int32, shape, 0)
    return ((row // z.lane_slots) ^ col) * z.lane_slots + row % z.lane_slots


def tile_terms(z, col, source, delta_ref, index_ref, matrix, extra, out_base):
    side = delta_ref.shape[-1]
    variant = slot_of_row(z, col, (z.rows, side)) // (2 * z.cols * z.cap)
    for n in range(delta_ref.shape[2]):
        at = pl.multiple_of(index_ref[0, 0, matrix, n, 1] * side, side)
        to = pl.multiple_of(out_base + index_ref[0, 0, matrix, n, 2] * side, side)
        rows = jnp.where(variant == index_ref[0, 0, matrix, n, 0], source[:, pl.ds(at, side)], 0)
        extra[:, pl.ds(to, side)] += jnp.dot(
            rows.astype(BF16), delta_ref[0, 0, n], preferred_element_type=F32
        )


def project_kernel(z, step, index_ref, gate_delta, up_delta, gate_ref, up_ref, *rest):
    pieces, rest = rest[: z.cols], rest[z.cols :]
    send_ref, keep_ref, source, extra, weights, sems = rest
    col, core = lax.axis_index("col"), lax.axis_index("tok") % 2
    units = gate_ref.shape[1]
    half = units // 2
    jobs = []
    for out_ref, side in ((send_ref, 1 - core), (keep_ref, core)):
        for m, ref in enumerate((gate_ref, up_ref)):
            for at in range(0, half, step):
                jobs.append((out_ref, m, ref, pl.multiple_of(side * half, half) + at, m * half + at))
    copies = []
    for n, (_, m, ref, at, _) in enumerate(jobs):
        copy = pltpu.make_async_copy(ref.at[:, pl.ds(at, step)], weights.at[n], sems.at[n])
        copy.start()
        copies.append(copy)
    extra[...] = jnp.zeros_like(extra)
    count = z.kvs * z.lane_slots
    wide = z.group * HEAD_DIM
    slot = slot_of_row(z, col, (z.rows, count))
    lane_of, owner = slot // z.cap % z.cols, slot // (z.cols * z.cap)
    column = lax.broadcasted_iota(jnp.int32, (z.rows, count), 1)
    totals = jnp.zeros((z.rows, HEAD_DIM), F32)
    for j in range(z.kvs):
        place = j * z.lane_slots + owner * z.cap + slot % z.cap
        found = jnp.zeros((z.rows, wide + HEAD_DIM), F32)
        for s in range(z.cols):
            pick = ((lane_of == (col ^ s)) & (column == place)).astype(F32).astype(BF16)
            found += jnp.dot(pick, pieces[s][...], preferred_element_type=F32)
        source[:, j * wide : (j + 1) * wide] = found[:, :wide].astype(BF16)
        totals += found[:, wide:]
    high, low = halves(jnp.sum(totals, axis=-1, keepdims=True))
    send_ref[:, units:] = two_lanes(high, low, z.rows)
    keep_ref[:, units:] = two_lanes(high, low, z.rows)
    tile_terms(z, col, source, gate_delta, index_ref, 0, extra, 0)
    tile_terms(z, col, source, up_delta, index_ref, 1, extra, units)
    for n, (out_ref, m, _, at, to) in enumerate(jobs):
        copies[n].wait()
        value = jnp.dot(source[...], weights[n], preferred_element_type=F32)
        value += extra[:, pl.ds(m * units + at, step)]
        out_ref[:, to : to + step] = value.astype(BF16)


def add_kernel(z, mine, other, out_ref):
    units = mine.shape[1] - HEAD_DIM
    out_ref[:, :units] = (mine[:, :units].astype(F32) + other[:, :units].astype(F32)).astype(BF16)
    total = mine[:, units:].astype(F32) + other[:, units:].astype(F32)
    out_ref[:, units:] = two_lanes(*halves(jnp.sum(total, axis=-1, keepdims=True)), z.rows)


def hidden_kernel(z, width, *refs):
    parts, out_ref = refs[:-1], refs[-1]
    units = out_ref.shape[1]
    squares = sum(ref[:, 2 * units :].astype(F32) for ref in parts)
    squares = jnp.sum(squares, axis=-1, keepdims=True)
    scale = lax.rsqrt(squares * (1.0 / width) + 1e-06)
    step = min(units, 512)
    for at in range(0, units, step):
        gate = sum(ref[:, at : at + step].astype(F32) for ref in parts) * scale
        up = sum(ref[:, units + at : units + at + step].astype(F32) for ref in parts) * scale
        out_ref[:, at : at + step] = (jax.nn.silu(gate) * up).astype(BF16)


def down_kernel(z, step, index_ref, delta_ref, weight_ref, mine, other, *rest):
    outs, (source, extra, fold, weights, sems) = rest[: z.cols], rest[z.cols :]
    col, core = lax.axis_index("col"), lax.axis_index("tok") % 2
    width = weight_ref.shape[1]
    copies = []
    for n in range(width // step):
        copy = pltpu.make_async_copy(
            weight_ref.at[:, pl.ds(n * step, step)], weights.at[n], sems.at[n]
        )
        copy.start()
        copies.append(copy)
    half = mine.shape[1]
    source[:, pl.ds(pl.multiple_of(core * half, half), half)] = mine[...]
    source[:, pl.ds(pl.multiple_of((1 - core) * half, half), half)] = other[...]
    extra[...] = jnp.zeros_like(extra)
    tile_terms(z, col, source, delta_ref, index_ref, 2, extra, 0)
    for n in range(width // step):
        copies[n].wait()
        extra[:, n * step : (n + 1) * step] += jnp.dot(
            source[...], weights[n], preferred_element_type=F32
        )
    for s in range(z.cols):
        rows = slice(s * z.lane_slots, (s + 1) * z.lane_slots)
        fold[: z.lane_slots, :] = extra[rows, : width // 2]
        fold[z.lane_slots :, :] = extra[rows, width // 2 :]
        outs[s][...] = fold[...].astype(BF16)


def finish_kernel(z, *refs):
    parts, out_ref = refs[: z.cols], refs[z.cols]
    total = sum(ref[...].astype(F32) for ref in parts)
    half = total.shape[1]
    out_ref[:, :half] = total[: z.lane_slots].astype(BF16)
    out_ref[:, half:] = total[z.lane_slots :].astype(BF16)


def return_kernel(z, *refs):
    parts, out_ref, rows = refs[: z.toks], refs[z.toks], refs[z.toks + 1]
    tok = lax.axis_index("tok")
    block = z.cap * z.group
    for s in range(z.toks):
        rows[...] = parts[s][...].astype(F32)
        first = pl.multiple_of((tok ^ s) * z.heads * HEAD_DIM, HEAD_DIM)
        for j in range(z.kvs):
            for h in range(z.group):
                to = first + (j * z.group + h) * HEAD_DIM
                out_ref[:, pl.ds(to, HEAD_DIM)] = rows[
                    pl.ds(j * block + h, z.cap, stride=z.group), :
                ].astype(BF16)


def swap(array, axis, size, distance):
    return lax.ppermute(array, axis, [(i, i ^ distance) for i in range(size)])


def local(
    request_rows,
    key_cache,
    route_list,
    route_count,
    norm_gain,
    gate_weight,
    up_weight,
    down_weight,
    gate_delta,
    up_delta,
    down_delta,
    tile_index,
):
    toks, cols = lax.axis_size("tok"), lax.axis_size("col")
    cap, ctx = key_cache.shape[0], key_cache.shape[1]
    z = Sizes(toks, cols, cap)
    width = norm_gain.shape[0]
    cache_rows = cap * ctx
    lanes = 2 * z.kvs * HEAD_DIM
    piece_rows = cache_rows + -(-z.pieces // z.blocks) * 16
    many = z.lane_slots * z.group

    pieces = call(
        functools.partial(pack_kernel, z, ctx),
        "pack",
        [(request_rows, VMEM), (key_cache, HBM)],
        [((piece_rows, lanes), BF16)] * toks,
        [
            pltpu.VMEM(request_rows.shape, F32),
            pltpu.VMEM((2 * z.req_rows, HEAD_DIM), F32),
            pltpu.SemaphoreType.DMA((toks, 2, cap)),
        ],
    )
    pieces = [pieces[0]] + [swap(pieces[s], "tok", toks, s) for s in range(1, toks)]
    block = z.kvs * cap * z.group
    send, *back = call(
        functools.partial(attend_kernel, z, ctx),
        "attend",
        [(route_list, SMEM), (route_count, SMEM), (norm_gain.reshape(1, width), VMEM)]
        + [(p, VMEM) for p in pieces],
        [((z.kvs * z.lane_slots, (z.group + 1) * HEAD_DIM), BF16)]
        + [((block, HEAD_DIM), BF16)] * toks,
        [
            pltpu.VMEM((toks, cache_rows, lanes), BF16),
            pltpu.VMEM((2 * toks, z.req_rows, HEAD_DIM), F32),
            pltpu.VMEM((z.kvs, many, HEAD_DIM), F32),
            pltpu.VMEM((z.kvs, many, HEAD_DIM), F32),
            pltpu.VMEM((z.kvs, many, HEAD_DIM), F32),
            pltpu.VMEM((many, HEAD_DIM), F32),
            pltpu.VMEM((z.kvs * many, HEAD_DIM), F32),
        ],
    )
    pieces = [send] + [swap(send, "col", cols, s) for s in range(1, cols)]
    features, units = gate_weight.shape
    step = min(units // 2, 1024)
    gate_up, kept = call(
        functools.partial(project_kernel, z, step),
        "project",
        [
            (tile_index, SMEM),
            (gate_delta, VMEM),
            (up_delta, VMEM),
            (gate_weight, HBM),
            (up_weight, HBM),
        ]
        + [(p, VMEM) for p in pieces],
        [((z.rows, units + HEAD_DIM), BF16)] * 2,
        [
            pltpu.VMEM((z.rows, features), BF16),
            pltpu.VMEM((z.rows, 2 * units), F32),
            pltpu.VMEM((2 * units // step, features, step), BF16),
            pltpu.SemaphoreType.DMA((2 * units // step,)),
        ],
        limit=48,
    )
    (total,) = call(
        functools.partial(add_kernel, z),
        "chip_sum",
        [(kept, VMEM), (swap(gate_up, "tok", toks, 1), VMEM)],
        [((z.rows, units + HEAD_DIM), BF16)],
    )
    parts = [total] + [swap(total, "tok", toks, 2 * s) for s in range(1, toks // 2)]
    (hidden,) = call(
        functools.partial(hidden_kernel, z, width),
        "hidden",
        [(p, VMEM) for p in parts],
        [((z.rows, units // 2), BF16)],
        limit=16,
    )
    back = [back[0]] + [swap(back[s], "tok", toks, s) for s in range(1, toks)]
    (attended,) = call(
        functools.partial(return_kernel, z),
        "attended",
        [(b, VMEM) for b in back],
        [((cap, width), BF16)],
        [pltpu.VMEM((block, HEAD_DIM), F32)],
    )
    out_width = down_weight.shape[1]
    step = min(out_width, 512)
    parts = call(
        functools.partial(down_kernel, z, step),
        "down",
        [
            (tile_index, SMEM),
            (down_delta, VMEM),
            (down_weight, HBM),
            (hidden, VMEM),
            (swap(hidden, "tok", toks, 1), VMEM),
        ],
        [((2 * z.lane_slots, out_width // 2), BF16)] * cols,
        [
            pltpu.VMEM((z.rows, units), BF16),
            pltpu.VMEM((z.rows, out_width), F32),
            pltpu.VMEM((2 * z.lane_slots, out_width // 2), F32),
            pltpu.VMEM((out_width // step, units, step), BF16),
            pltpu.SemaphoreType.DMA((out_width // step,)),
        ],
        limit=32,
    )
    parts = [parts[0]] + [swap(parts[s], "col", cols, s) for s in range(1, cols)]
    (ffn_out,) = call(
        functools.partial(finish_kernel, z),
        "finish",
        [(p, VMEM) for p in parts],
        [((z.lane_slots, out_width), BF16)],
    )
    return attended, ffn_out


def solution(mesh):
    in_specs = (
        P(("rep", "tok", "col"), None),
        P(("rep", "tok", "col"), None, None),
        P("rep", "col", None),
        P("rep", "col"),
        P(),
        P("tok", "col"),
        P("tok", "col"),
        P("col", "tok"),
        P("tok", "col", None, None, None),
        P("tok", "col", None, None, None),
        P("tok", "col", None, None, None),
        P("tok", "col", None, None, None),
    )
    out_specs = (P(("rep", "tok", "col"), None), P(("rep", "col"), "tok"))
    return jax.shard_map(local, mesh=mesh, in_specs=in_specs, out_specs=out_specs, check_vma=False)
```

```python
import functools

import jax
import jax.numpy as jnp
from jax import lax
from jax.experimental import pallas as pl
from jax.experimental.pallas import tpu as pltpu
from jax.sharding import PartitionSpec as P

HEADS = 64
KV_HEADS = 8
HEAD_DIM = 128
GROUP = HEADS // KV_HEADS
MIB = 1 << 20
FETCH = (5, 7, 13)
DOWN_FIRST = 3
CUTS = (4, 6)
BF16 = jnp.bfloat16
F32 = jnp.float32
VMEM = pltpu.VMEM
HBM = pltpu.HBM


def call(kernel, name, ins, outs, scratch=(), limit=8, cost=None, after=()):
    if cost is None:
        cost = pl.CostEstimate(flops=0, bytes_accessed=1024, transcendentals=0)
    count = len(ins)
    ins = ins + [(a, VMEM) for a in after]

    def body(*refs):
        kernel(*refs[:count], *refs[count + len(after) :])

    return list(
        pl.pallas_call(
            body,
            name=name,
            in_specs=[pl.BlockSpec(memory_space=s) for _, s in ins],
            out_specs=[pl.BlockSpec(memory_space=VMEM) for _ in outs],
            out_shape=[VMEM(shape, dtype) for shape, dtype in outs],
            scratch_shapes=list(scratch),
            cost_estimate=cost,
            compiler_params=pltpu.CompilerParams(vmem_limit_bytes=limit * MIB),
        )(*[pltpu.with_memory_space_constraint(a, space) for a, space in ins])
    )


class Sizes:
    def __init__(self, toks, cols, cap, units):
        self.toks, self.cols, self.cap = toks, cols, cap
        half = units // 2
        cuts = [half * n // 8 for n in CUTS]
        self.parts = list(zip([0] + cuts, [b - a for a, b in zip([0] + cuts, cuts + [half])]))
        self.chunks = len(self.parts)
        self.step = min(512, min(size for _, size in self.parts))
        self.blocks_of = [
            [
                (q, keep, m, first + at)
                for keep in (False, True)
                for m in range(2)
                for at in range(0, size, self.step)
            ]
            for q, (first, size) in enumerate(self.parts)
        ]
        self.downs = [(mine, n * half // 4) for mine in (True, False) for n in range(4)]
        self.tail = 2 * self.parts[0][1]
        self.heads = HEADS // toks
        self.kvs = max(1, self.heads // GROUP)
        self.group = self.heads // self.kvs
        self.lane_slots = toks * cap
        self.rows = toks * cols * cap
        self.req_rows = -(-(self.heads + 2 * self.kvs) // 16) * 16
        self.blocks = 2 * self.kvs
        self.pieces = 2 * self.req_rows // 16

    def first_kv(self, tok):
        return tok * self.heads // GROUP


def pack_kernel(z, ctx, req_ref, cache_ref, *rest):
    outs, (narrow, wide, rows, req_sem, sems) = rest[: z.toks], rest[z.toks :]
    tok = lax.axis_index("tok")
    width = z.kvs * HEAD_DIM
    cache_rows = z.cap * ctx
    pairs = KV_HEADS * HEAD_DIM
    fetch = pltpu.make_async_copy(req_ref, narrow, req_sem)
    fetch.start()
    copies = []
    for s in reversed(range(z.toks)):
        first = pl.multiple_of(z.first_kv(tok ^ s) * HEAD_DIM, HEAD_DIM)
        for half in range(2):
            for k in range(z.cap):
                copy = pltpu.make_async_copy(
                    cache_ref.at[k, :, pl.ds(half * pairs + first, width)],
                    outs[s].at[pl.ds(k * ctx, ctx), pl.ds(half * width, width)],
                    sems.at[s, half, k],
                )
                copy.start()
                copies.append(copy)
    rows[...] = jnp.zeros_like(rows)
    fetch.wait()
    wide[...] = narrow[...].astype(F32)
    for s in range(z.toks):
        to = tok ^ s
        starts = [(to * z.heads + h) * HEAD_DIM for h in range(z.heads)]
        for half in range(2):
            starts += [
                HEADS * HEAD_DIM + half * pairs + (z.first_kv(to) + j) * HEAD_DIM
                for j in range(z.kvs)
            ]
        for r in range(2):
            for n, start in enumerate(starts):
                rows[r * z.req_rows + n : r * z.req_rows + n + 1, :] = wide[
                    r : r + 1, pl.ds(pl.multiple_of(start, HEAD_DIM), HEAD_DIM)
                ]
        for p in range(z.pieces):
            at, lane = cache_rows + p // z.blocks * 16, p % z.blocks * HEAD_DIM
            outs[s][at : at + 16, lane : lane + HEAD_DIM] = rows[p * 16 : p * 16 + 16, :].astype(BF16)
    for copy in copies:
        copy.wait()


def start_copies(pairs, sems):
    copies = [pltpu.make_async_copy(src, dst, sems.at[n]) for n, (src, dst) in enumerate(pairs)]
    for copy in copies:
        copy.start()
    return copies


def after_starts(compute):
    pl.when(lax.axis_index("tok") >= 0)(compute)


def weight_blocks(z, jobs, refs):
    core = lax.axis_index("tok") % 2
    half = refs[0].shape[1] // 2
    found = []
    for job in jobs:
        at = pl.multiple_of((core if job[-3 if len(job) > 2 else 0] else 1 - core) * half, half)
        if len(job) > 2:
            _, _, matrix, first = job
            found.append(refs[matrix].at[:, pl.ds(at + first, z.step)])
        else:
            found.append(refs[2].at[pl.ds(at + job[1], half // 4), :])
    return found


def fetch_kernel(z, jobs, whole, gain_size, *refs):
    weights, rest = refs[:3], refs[3:]
    sources, rest = list(rest[: len(whole)]), rest[len(whole) :]
    outs, sems = rest[:-1], rest[-1]
    if gain_size:
        tok = lax.axis_index("tok")
        at = pl.multiple_of(tok * gain_size, gain_size)
        sources[0] = sources[0].at[:, pl.ds(at, gain_size)]
    sources += weight_blocks(z, jobs, weights)
    for copy in start_copies(list(zip(sources, outs)), sems):
        copy.wait()


def attend_kernel(z, ctx, jobs, list_hbm, count_hbm, *rest):
    weights, pieces, rest = rest[:3], rest[3 : 3 + z.toks], rest[3 + z.toks :]
    send_ref, back_refs, rest = rest[0], rest[1 : 1 + z.toks], rest[1 + z.toks :]
    blocks, rest = rest[: len(jobs)], rest[len(jobs) :]
    cache, req, query, own_key, own_value, alive, mixed_all, list_ref, count_ref, table_sems, sems = rest
    tables = start_copies([(list_hbm, list_ref), (count_hbm, count_ref)], table_sems)
    copies = start_copies(list(zip(weight_blocks(z, jobs, weights), blocks)), sems)
    tok = lax.axis_index("tok")
    cache_rows = z.cap * ctx
    for s in range(z.toks):
        source = tok ^ s
        cache[source] = pieces[s][:cache_rows, :]
        for p in range(z.pieces):
            at, lane = cache_rows + p // z.blocks * 16, p % z.blocks * HEAD_DIM
            r, part = p * 16 // z.req_rows, p * 16 % z.req_rows
            req[source * 2 + r, part : part + 16, :] = pieces[s][
                at : at + 16, lane : lane + HEAD_DIM
            ].astype(F32)
    for table in tables:
        table.wait()
    for g in range(z.toks):
        for k in range(z.cap):
            live = (k < count_ref[0, g]).astype(F32)
            rows = req[list_ref[k, 0, g]] * live
            at = (g * z.cap + k) * z.group
            for j in range(z.kvs):
                query[j, at : at + z.group, :] = rows[j * z.group : (j + 1) * z.group, :]
                key, value = z.heads + j, z.heads + z.kvs + j
                own_key[j, at : at + z.group, :] = jnp.broadcast_to(
                    rows[key : key + 1, :], (z.group, HEAD_DIM)
                )
                own_value[j, at : at + z.group, :] = jnp.broadcast_to(
                    rows[value : value + 1, :], (z.group, HEAD_DIM)
                )
            alive[at : at + z.group, :] = jnp.full((z.group, HEAD_DIM), live, F32)
    many, keys = z.lane_slots * z.group, z.toks * cache_rows
    row_slot = lax.broadcasted_iota(jnp.int32, (many, keys), 0) // z.group
    key_slot = lax.broadcasted_iota(jnp.int32, (many, keys), 1) // ctx
    same = row_slot == key_slot
    scale = HEAD_DIM ** (-0.5)
    for j in range(z.kvs):
        cached_keys = cache[:, :, j * HEAD_DIM : (j + 1) * HEAD_DIM].reshape(keys, HEAD_DIM)
        at = (z.kvs + j) * HEAD_DIM
        cached_values = cache[:, :, at : at + HEAD_DIM].reshape(keys, HEAD_DIM)
        past = (
            lax.dot_general(
                query[j].astype(BF16),
                cached_keys,
                (((1,), (1,)), ((), ())),
                preferred_element_type=F32,
            )
            * scale
        )
        own = jnp.sum(query[j] * own_key[j], axis=-1, keepdims=True) * scale
        top = jnp.maximum(jnp.max(jnp.where(same, past, -jnp.inf), axis=-1, keepdims=True), own)
        past_exp = jnp.where(same, jnp.exp(jnp.where(same, past - top, 0.0)), 0.0)
        own_exp = jnp.exp(own - top)
        total = jnp.sum(past_exp, axis=-1, keepdims=True) + own_exp
        weights = (past_exp / total).astype(BF16)
        own_weight = (own_exp / total).astype(BF16).astype(F32)
        mixed = jnp.dot(weights, cached_values, preferred_element_type=F32)
        mixed = (mixed + own_weight * own_value[j]) * alive[...]
        mixed_all[j * many : (j + 1) * many, :] = mixed.astype(BF16).astype(F32)
    block = z.cap * z.group
    for s in range(z.toks):
        for j in range(z.kvs):
            at = pl.multiple_of(j * many + (tok ^ s) * block, block if block % 8 == 0 else 4)
            back_refs[s][j * block : (j + 1) * block, :] = mixed_all[pl.ds(at, block), :].astype(BF16)
    count = z.kvs * z.lane_slots
    for h in range(z.group):
        send_ref[:, h * HEAD_DIM : (h + 1) * HEAD_DIM] = mixed_all[
            pl.ds(h, count, stride=z.group), :
        ].astype(BF16)
    for copy in copies:
        copy.wait()


def halves(value):
    high = value.astype(BF16).astype(F32)
    return high, value - high


def two_lanes(high, low, rows):
    lane = lax.broadcasted_iota(jnp.int32, (rows, HEAD_DIM), 1)
    return jnp.where(lane == 0, high, jnp.where(lane == 1, low, 0.0)).astype(BF16)


def slot_of_row(z, col, shape):
    row = lax.broadcasted_iota(jnp.int32, shape, 0)
    return ((row // z.lane_slots) ^ col) * z.lane_slots + row % z.lane_slots


def tile_terms(z, source, delta_ref, index_ref, matrix, extra, out_base):
    side = delta_ref.shape[-1]
    col = lax.axis_index("col")
    variant = slot_of_row(z, col, (z.rows, side)) // (2 * z.cols * z.cap)
    for n in range(delta_ref.shape[2]):
        at = pl.multiple_of(index_ref[0, matrix, 1, 0, n] * side, side)
        to = pl.multiple_of(out_base + index_ref[0, matrix, 2, 0, n] * side, side)
        rows = jnp.where(variant == index_ref[0, matrix, 0, 0, n], source[:, pl.ds(at, side)], 0)
        extra[:, pl.ds(to, side)] += jnp.dot(
            rows.astype(BF16), delta_ref[0, 0, n], preferred_element_type=F32
        )


def project_blocks(z, chunk, source, extra, blocks, send_ref, keep_ref):
    core = lax.axis_index("tok") % 2
    units = extra.shape[1] // 2
    first, size = z.parts[chunk]
    for n, (out_ref, side) in enumerate(((send_ref, 1 - core), (keep_ref, core))):
        for m in range(2):
            for p in range(size // z.step):
                block = blocks[(2 * n + m) * (size // z.step) + p]
                at = side * (units // 2) + m * units + first + p * z.step
                value = jnp.dot(source[...], block[...], preferred_element_type=F32)
                value += extra[:, pl.ds(pl.multiple_of(at, HEAD_DIM), z.step)]
                to = m * size + p * z.step
                out_ref[:, to : to + z.step] = value.astype(BF16)


def first_project_kernel(z, jobs, index_hbm, gain_ref, gate_delta, up_delta, *rest):
    pieces, rest = rest[: z.cols], rest[z.cols :]
    odd_backs, rest = rest[: z.toks // 2], rest[z.toks // 2 :]
    count = len(z.blocks_of[0])
    weights, blocks, rest = rest[:3], rest[3 : 3 + count], rest[3 + count :]
    send_ref, keep_ref, source, extra, *fetched = rest[: 4 + len(jobs)]
    index_ref, index_sem, sems = rest[4 + len(jobs) :]
    table = pltpu.make_async_copy(index_hbm, index_ref, index_sem)
    table.start()
    copies = start_copies(list(zip(weight_blocks(z, jobs, weights), fetched)), sems)
    col = lax.axis_index("col")
    units = extra.shape[1] // 2
    extra[...] = jnp.zeros_like(extra)
    count = z.kvs * z.lane_slots
    wide = z.group * HEAD_DIM
    slot = slot_of_row(z, col, (z.rows, count))
    lane_of, owner = slot // z.cap % z.cols, slot // (z.cols * z.cap)
    column = lax.broadcasted_iota(jnp.int32, (z.rows, count), 1)
    squares = jnp.zeros((z.rows, 1), F32)
    for j in range(z.kvs):
        place = j * z.lane_slots + owner * z.cap + slot % z.cap
        found = jnp.zeros((z.rows, wide), F32)
        for s in range(z.cols):
            pick = ((lane_of == (col ^ s)) & (column == place)).astype(F32).astype(BF16)
            found += jnp.dot(pick, pieces[s][...], preferred_element_type=F32)
        squares += jnp.sum(found * found, axis=-1, keepdims=True)
        lanes = slice(j * wide, (j + 1) * wide)
        source[:, lanes] = (found * gain_ref[:, lanes]).astype(BF16)
    tail = z.tail
    for ref in (send_ref, keep_ref):
        ref[:, tail : tail + HEAD_DIM] = two_lanes(*halves(squares), z.rows)
    send_ref[:, tail + HEAD_DIM :] = jnp.zeros((z.rows, z.toks // 2 * HEAD_DIM), BF16)
    for n, ref in enumerate(odd_backs):
        lane = tail + (n + 1) * HEAD_DIM
        send_ref[: ref.shape[0], lane : lane + HEAD_DIM] = ref[...]
    table.wait()
    tile_terms(z, source, gate_delta, index_ref, 0, extra, 0)
    tile_terms(z, source, up_delta, index_ref, 1, extra, units)
    after_starts(lambda: project_blocks(z, 0, source, extra, blocks, send_ref, keep_ref))
    for copy in copies:
        copy.wait()


def next_project_kernel(z, jobs, delta_hbm, *rest):
    count = sum(len(some) for some in z.blocks_of[1:])
    weights, (source, extra), blocks, rest = rest[:3], rest[3:5], rest[5 : 5 + count], rest[5 + count :]
    sums = 2 * (z.chunks - 1)
    outs, (delta_ref, *fetched, sems) = rest[:sums], rest[sums:]
    copies = start_copies(
        list(zip(weight_blocks(z, jobs, weights) + [delta_hbm], fetched + [delta_ref])), sems
    )

    @after_starts
    def _():
        at = 0
        for q in range(1, z.chunks):
            refs = blocks[at : at + len(z.blocks_of[q])]
            at += len(refs)
            project_blocks(z, q, source, extra, refs, outs[2 * q - 2], outs[2 * q - 1])

    for copy in copies:
        copy.wait()


def add_kernel(z, mine, other, *rest):
    chips = z.toks // 2
    evens, outs = rest[: len(rest) - (chips - 1)], rest[len(rest) - (chips - 1) :]
    tail = z.tail if evens else mine.shape[1]
    sums = (mine[:, :tail].astype(F32) + other[:, :tail].astype(F32)).astype(BF16)
    for s, out_ref in enumerate(outs):
        out_ref[:, :tail] = sums
        if not evens:
            continue
        lanes = slice(tail, tail + HEAD_DIM)
        total = mine[:, lanes].astype(F32) + other[:, lanes].astype(F32)
        out_ref[:, lanes] = two_lanes(*halves(jnp.sum(total, axis=-1, keepdims=True)), z.rows)
        block = evens[s].shape[0]
        out_ref[:, tail + HEAD_DIM :] = jnp.zeros((z.rows, 2 * HEAD_DIM), BF16)
        out_ref[:block, tail + HEAD_DIM : tail + 2 * HEAD_DIM] = evens[s][...]
        lane = tail + (s + 2) * HEAD_DIM
        out_ref[:block, tail + 2 * HEAD_DIM :] = other[:block, lane : lane + HEAD_DIM]


def hidden_kernel(z, width, *refs):
    chips = z.toks // 2
    out_ref = refs[-1]
    squares = sum(ref[:, z.tail : z.tail + HEAD_DIM].astype(F32) for ref in refs[:chips])
    squares = jnp.sum(squares, axis=-1, keepdims=True)
    scale = lax.rsqrt(squares * (1.0 / width) + 1e-06)
    for q, (first, size) in enumerate(z.parts):
        parts = refs[q * chips : (q + 1) * chips]
        step = min(size, 256)
        for at in range(0, size, step):
            gate = sum(ref[:, at : at + step].astype(F32) for ref in parts) * scale
            up = sum(ref[:, size + at : size + at + step].astype(F32) for ref in parts) * scale
            out_ref[:, first + at : first + at + step] = (jax.nn.silu(gate) * up).astype(BF16)


def down_kernel(z, index_hbm, delta_ref, mine, other, *rest):
    weights, rest = rest[: len(z.downs)], rest[len(z.downs) :]
    outs, (source, total, fold, index_ref, index_sem) = rest[: z.cols], rest[z.cols :]
    table = pltpu.make_async_copy(index_hbm, index_ref, index_sem)
    table.start()
    core = lax.axis_index("tok") % 2
    half = mine.shape[1]
    source[:, pl.ds(pl.multiple_of(core * half, half), half)] = mine[...]
    source[:, pl.ds(pl.multiple_of((1 - core) * half, half), half)] = other[...]
    width = total.shape[1]
    step = min(width, 512)
    for to in range(0, width, step):
        value = jnp.zeros((z.rows, step), F32)
        for (is_mine, at), weight in zip(z.downs, weights):
            units = (mine if is_mine else other)[:, at : at + weight.shape[0]]
            value += jnp.dot(units, weight[:, to : to + step], preferred_element_type=F32)
        total[:, to : to + step] = value
    table.wait()
    tile_terms(z, source, delta_ref, index_ref, 2, total, 0)
    for s in range(z.cols):
        rows = slice(s * z.lane_slots, (s + 1) * z.lane_slots)
        fold[: z.lane_slots, :] = total[rows, : width // 2]
        fold[z.lane_slots :, :] = total[rows, width // 2 :]
        outs[s][...] = fold[...].astype(BF16)


def finish_kernel(z, *refs):
    parts, out_ref = refs[: z.cols], refs[z.cols]
    total = sum(ref[...].astype(F32) for ref in parts)
    half = total.shape[1]
    out_ref[:, :half] = total[: z.lane_slots].astype(BF16)
    out_ref[:, half:] = total[z.lane_slots :].astype(BF16)


def return_kernel(z, own, from_core, *refs):
    chips = z.toks // 2
    parts, (out_ref, rows) = refs[: chips - 1], refs[chips - 1 :]
    tok = lax.axis_index("tok")
    block = z.cap * z.group
    count = z.kvs * block
    tail = z.tail + HEAD_DIM
    for s in range(z.toks):
        if s == 0:
            rows[...] = own[...].astype(F32)
        elif s == 1:
            rows[...] = from_core[:count, tail : tail + HEAD_DIM].astype(F32)
        else:
            lane = tail + s % 2 * HEAD_DIM
            rows[...] = parts[s // 2 - 1][:count, lane : lane + HEAD_DIM].astype(F32)
        first = pl.multiple_of((tok ^ s) * z.heads * HEAD_DIM, HEAD_DIM)
        for j in range(z.kvs):
            for h in range(z.group):
                to = first + (j * z.group + h) * HEAD_DIM
                out_ref[:, pl.ds(to, HEAD_DIM)] = rows[
                    pl.ds(j * block + h, z.cap, stride=z.group), :
                ].astype(BF16)


def swap(array, axis, size, distance):
    return lax.ppermute(array, axis, [(i, i ^ distance) for i in range(size)])


def local(
    request_rows,
    key_cache,
    route_list,
    route_count,
    norm_gain,
    gate_weight,
    up_weight,
    down_weight,
    gate_delta,
    up_delta,
    down_delta,
    tile_index,
):
    toks, cols = lax.axis_size("tok"), lax.axis_size("col")
    cap, ctx = key_cache.shape[0], key_cache.shape[1]
    features, units = gate_weight.shape
    z = Sizes(toks, cols, cap, units)
    width = norm_gain.shape[0]
    cache_rows = cap * ctx
    lanes = 2 * z.kvs * HEAD_DIM
    piece_rows = cache_rows + -(-z.pieces // z.blocks) * 16
    many = z.lane_slots * z.group
    chips = toks // 2
    gain = norm_gain.reshape(1, width)
    route_list = route_list.transpose(2, 1, 0)
    route_count = route_count.transpose(1, 0)
    tile_index = tile_index.transpose(0, 2, 4, 1, 3)
    dma = pltpu.SemaphoreType.DMA

    jobs = [job for some in z.blocks_of for job in some]
    cuts = [0] + [-(-len(jobs) * n // 16) for n in FETCH]
    early, middle, late, beside = [jobs[a:b] for a, b in zip(cuts, cuts[1:] + [len(jobs)])]
    beside, last = beside + z.downs[:DOWN_FIRST], z.downs[DOWN_FIRST:]
    weights = [(gate_weight, HBM), (up_weight, HBM), (down_weight, HBM)]

    def shapes(some):
        up, down = (features, z.step), (units // 8, down_weight.shape[1])
        return [(up if len(job) > 2 else down, BF16) for job in some]

    def traffic(some):
        moved = sum(a * b * 2 for (a, b), _ in shapes(some))
        return pl.CostEstimate(flops=0, bytes_accessed=moved, transcendentals=0)

    pieces = call(
        functools.partial(pack_kernel, z, ctx),
        "pack",
        [(request_rows, HBM), (key_cache, HBM)],
        [((piece_rows, lanes), BF16)] * toks,
        [
            pltpu.VMEM(request_rows.shape, BF16),
            pltpu.VMEM(request_rows.shape, F32),
            pltpu.VMEM((2 * z.req_rows, HEAD_DIM), F32),
            dma,
            dma((toks, 2, cap)),
        ],
    )
    whole = [gain, gate_delta, up_delta]
    gain, gate_delta, up_delta, *blocks = call(
        functools.partial(fetch_kernel, z, early, whole, features),
        "fetch_early",
        weights + [(a, HBM) for a in whole],
        [((1, features), F32), (gate_delta.shape, BF16), (up_delta.shape, BF16)]
        + shapes(early),
        [dma((len(early) + 3,))],
        after=pieces[:1],
        cost=traffic(early),
    )
    pieces = [pieces[0]] + [swap(pieces[s], "tok", toks, s) for s in range(1, toks)]
    back_rows = z.kvs * cap * z.group
    send, *rest = call(
        functools.partial(attend_kernel, z, ctx, middle),
        "attend",
        [(route_list, HBM), (route_count, HBM)] + weights + [(p, VMEM) for p in pieces],
        [((z.kvs * z.lane_slots, z.group * HEAD_DIM), BF16)]
        + [((back_rows, HEAD_DIM), BF16)] * toks
        + shapes(middle),
        [
            pltpu.VMEM((toks, cache_rows, lanes), BF16),
            pltpu.VMEM((2 * toks, z.req_rows, HEAD_DIM), F32),
            pltpu.VMEM((z.kvs, many, HEAD_DIM), F32),
            pltpu.VMEM((z.kvs, many, HEAD_DIM), F32),
            pltpu.VMEM((z.kvs, many, HEAD_DIM), F32),
            pltpu.VMEM((many, HEAD_DIM), F32),
            pltpu.VMEM((z.kvs * many, HEAD_DIM), F32),
            pltpu.SMEM(route_list.shape, jnp.int32),
            pltpu.SMEM(route_count.shape, jnp.int32),
            dma((2,)),
            dma((max(1, len(middle)),)),
        ],
        after=[gain],
    )
    back = rest[:toks]
    blocks += rest[toks:]
    blocks += call(
        functools.partial(fetch_kernel, z, late, [], 0),
        "fetch_late",
        weights,
        shapes(late),
        [dma((len(late),))],
        after=[send],
        cost=traffic(late),
    )
    pieces = [send] + [swap(send, "col", cols, s) for s in range(1, cols)]
    out_width = down_weight.shape[1]
    table = pltpu.SMEM(tile_index.shape, jnp.int32)
    sent, kept, source, extra, *fetched = call(
        functools.partial(first_project_kernel, z, beside),
        "project_first",
        [
            (tile_index, HBM),
            (gain, VMEM),
            (gate_delta, VMEM),
            (up_delta, VMEM),
        ]
        + [(p, VMEM) for p in pieces + back[1::2]]
        + weights
        + [(p, VMEM) for p in blocks[: len(z.blocks_of[0])]],
        [
            ((z.rows, z.tail + (1 + chips) * HEAD_DIM), BF16),
            ((z.rows, z.tail + HEAD_DIM), BF16),
            ((z.rows, features), BF16),
            ((z.rows, 2 * units), F32),
        ]
        + shapes(beside),
        [table, dma, dma((len(beside),))],
        after=blocks[-1:],
    )
    blocks = blocks[len(z.blocks_of[0]) :] + fetched[: len(beside) - DOWN_FIRST]
    down_blocks = fetched[len(beside) - DOWN_FIRST :]
    from_core = swap(sent, "tok", toks, 1)
    totals = [
        call(
            functools.partial(add_kernel, z),
            "chip_sum_first",
            [(a, VMEM) for a in [kept, from_core] + back[2::2]],
            [((z.rows, z.tail + 3 * HEAD_DIM), BF16)] * (chips - 1),
        )
    ]
    sizes = [2 * size for _, size in z.parts[1:]]
    *sums, down_delta = call(
        functools.partial(next_project_kernel, z, last),
        "project_next",
        [(down_delta, HBM)] + weights + [(a, VMEM) for a in [source, extra] + blocks],
        [((z.rows, size), BF16) for size in sizes for _ in range(2)]
        + [(down_delta.shape, BF16)]
        + shapes(last),
        [dma((len(last) + 1,))],
        cost=pl.CostEstimate(
            flops=4 * z.rows * features * sum(sizes),
            bytes_accessed=4 * features * sum(sizes),
            transcendentals=0,
        ),
        after=totals[0][:1],
    )
    rest = sums[2 * len(sizes) :] + [down_delta]
    down_delta, down_blocks = rest[0], down_blocks + rest[1:]
    for q, size in enumerate(sizes):
        sent, kept = sums[2 * q : 2 * q + 2]
        totals.append(
            call(
                functools.partial(add_kernel, z),
                "chip_sum_next",
                [(kept, VMEM), (swap(sent, "tok", toks, 1), VMEM)],
                [((z.rows, size), BF16)] * (chips - 1),
            )
        )
    parts = [
        total[:1] + [swap(total[s - 1], "tok", toks, 2 * s) for s in range(1, chips)]
        for total in totals
    ]
    (hidden,) = call(
        functools.partial(hidden_kernel, z, width),
        "hidden",
        [(a, VMEM) for part in parts for a in part],
        [((z.rows, units // 2), BF16)],
    )
    firsts = parts[0]
    (attended,) = call(
        functools.partial(return_kernel, z),
        "attended",
        [(a, VMEM) for a in [back[0], from_core] + firsts[1:]],
        [((cap, width), BF16)],
        [pltpu.VMEM((back_rows, HEAD_DIM), F32)],
    )
    parts = call(
        functools.partial(down_kernel, z),
        "down",
        [(tile_index, HBM)]
        + [(a, VMEM) for a in [down_delta, hidden, swap(hidden, "tok", toks, 1)] + down_blocks],
        [((2 * z.lane_slots, out_width // 2), BF16)] * cols,
        [
            pltpu.VMEM((z.rows, units), BF16),
            pltpu.VMEM((z.rows, out_width), F32),
            pltpu.VMEM((2 * z.lane_slots, out_width // 2), F32),
            table,
            dma,
        ],
    )
    parts = [parts[0]] + [swap(parts[s], "col", cols, s) for s in range(1, cols)]
    (ffn_out,) = call(
        functools.partial(finish_kernel, z),
        "finish",
        [(p, VMEM) for p in parts],
        [((z.lane_slots, out_width), BF16)],
    )
    return attended, ffn_out


def solution(mesh):
    in_specs = (
        P(("rep", "tok", "col"), None),
        P(("rep", "tok", "col"), None, None),
        P("rep", "col", None),
        P("rep", "col"),
        P(),
        P("tok", "col"),
        P("tok", "col"),
        P("col", "tok"),
        P("tok", "col", None, None, None),
        P("tok", "col", None, None, None),
        P("tok", "col", None, None, None),
        P("tok", "col", None, None, None),
    )
    out_specs = (P(("rep", "tok", "col"), None), P(("rep", "col"), "tok"))
    return jax.shard_map(local, mesh=mesh, in_specs=in_specs, out_specs=out_specs, check_vma=False)
```

```python
import functools

import jax
import jax.numpy as jnp
from jax import lax
from jax.experimental import pallas as pl
from jax.experimental.pallas import tpu as pltpu
from jax.sharding import PartitionSpec as P

HEADS = 64
KV_HEADS = 8
HEAD_DIM = 128
GROUP = HEADS // KV_HEADS
MIB = 1 << 20
FETCH = (0, 4, 1, 5, 5, 1, 3, 5)
CUTS = (4, 6)
BF16 = jnp.bfloat16
F32 = jnp.float32
VMEM = pltpu.VMEM
HBM = pltpu.HBM


def call(kernel, name, ins, outs, scratch=(), limit=8, cost=None, after=()):
    if cost is None:
        cost = pl.CostEstimate(flops=0, bytes_accessed=1024, transcendentals=0)
    count = len(ins)
    ins = ins + [(a, VMEM) for a in after]

    def body(*refs):
        kernel(*refs[:count], *refs[count + len(after) :])

    return list(
        pl.pallas_call(
            body,
            name=name,
            in_specs=[pl.BlockSpec(memory_space=s) for _, s in ins],
            out_specs=[pl.BlockSpec(memory_space=VMEM) for _ in outs],
            out_shape=[VMEM(shape, dtype) for shape, dtype in outs],
            scratch_shapes=list(scratch),
            cost_estimate=cost,
            compiler_params=pltpu.CompilerParams(vmem_limit_bytes=limit * MIB),
        )(*[pltpu.with_memory_space_constraint(a, space) for a, space in ins])
    )


class Sizes:
    def __init__(self, toks, cols, cap, units):
        self.toks, self.cols, self.cap = toks, cols, cap
        half = units // 2
        cuts = [half * n // 8 for n in CUTS]
        self.parts = list(zip([0] + cuts, [b - a for a, b in zip([0] + cuts, cuts + [half])]))
        self.chunks = len(self.parts)
        self.step = min(512, min(size for _, size in self.parts))
        self.blocks_of = [
            [
                (q, keep, m, first + at)
                for keep in (False, True)
                for m in range(2)
                for at in range(0, size, self.step)
            ]
            for q, (first, size) in enumerate(self.parts)
        ]
        self.downs = [(mine, n * half // 4) for mine in (True, False) for n in range(4)]
        self.tail = 2 * self.parts[0][1]
        self.heads = HEADS // toks
        self.kvs = max(1, self.heads // GROUP)
        self.group = self.heads // self.kvs
        self.lane_slots = toks * cap
        self.rows = toks * cols * cap
        self.req_rows = -(-(self.heads + 2 * self.kvs) // 16) * 16
        self.blocks = 2 * self.kvs
        self.pieces = 2 * self.req_rows // 16

    def first_kv(self, tok):
        return tok * self.heads // GROUP


def pack_kernel(z, ctx, jobs, req_ref, cache_ref, *rest):
    weights, outs, rest = rest[:3], rest[3 : 3 + z.toks], rest[3 + z.toks :]
    blocks, (narrow, wide, rows, req_sem, sems, block_sems) = rest[: len(jobs)], rest[len(jobs) :]
    tok = lax.axis_index("tok")
    width = z.kvs * HEAD_DIM
    pairs = KV_HEADS * HEAD_DIM
    fetch = pltpu.make_async_copy(req_ref, narrow, req_sem)
    fetch.start()
    copies = []
    for s in reversed(range(z.toks)):
        first = pl.multiple_of(z.first_kv(tok ^ s) * HEAD_DIM, HEAD_DIM)
        for half in range(2):
            copy = pltpu.make_async_copy(
                cache_ref.at[:, :, pl.ds(half * pairs + first, width)],
                outs[s].at[: z.cap, :, pl.ds(half * width, width)],
                sems.at[s, half],
            )
            copy.start()
            copies.append(copy)
    copies += start_copies(list(zip(weight_blocks(z, jobs, weights), blocks)), block_sems)
    fetch.wait()

    @after_starts
    def _():
        rows[...] = jnp.zeros_like(rows)
        wide[...] = narrow[...].astype(F32)
        for s in range(z.toks):
            to = tok ^ s
            starts = [(to * z.heads + h) * HEAD_DIM for h in range(z.heads)]
            for half in range(2):
                starts += [
                    HEADS * HEAD_DIM + half * pairs + (z.first_kv(to) + j) * HEAD_DIM
                    for j in range(z.kvs)
                ]
            for r in range(2):
                for n, start in enumerate(starts):
                    at = r * z.req_rows + n
                    rows[s, at : at + 1, :] = wide[
                        r : r + 1, pl.ds(pl.multiple_of(start, HEAD_DIM), HEAD_DIM)
                    ]
            for p in range(z.pieces):
                at, lane = z.cap + p // z.blocks, p % z.blocks * HEAD_DIM
                outs[s][at, :, lane : lane + HEAD_DIM] = rows[s, p * 16 : p * 16 + 16, :].astype(BF16)

    for copy in copies:
        copy.wait()


def start_copies(pairs, sems):
    copies = [pltpu.make_async_copy(src, dst, sems.at[n]) for n, (src, dst) in enumerate(pairs)]
    for copy in copies:
        copy.start()
    return copies


def after_starts(compute):
    pl.when(lax.axis_index("tok") >= 0)(compute)


def weight_blocks(z, jobs, refs):
    core = lax.axis_index("tok") % 2
    half = refs[0].shape[1] // 2
    found = []
    for job in jobs:
        at = pl.multiple_of((core if job[-3 if len(job) > 2 else 0] else 1 - core) * half, half)
        if len(job) > 2:
            _, _, matrix, first = job
            found.append(refs[matrix].at[:, pl.ds(at + first, z.step)])
        else:
            found.append(refs[2].at[pl.ds(at + job[1], half // 4), :])
    return found


def fetch_kernel(z, jobs, whole, gain_size, *refs):
    weights, rest = refs[:3], refs[3:]
    sources, rest = list(rest[: len(whole)]), rest[len(whole) :]
    outs, sems = rest[:-1], rest[-1]
    if gain_size:
        tok = lax.axis_index("tok")
        at = pl.multiple_of(tok * gain_size, gain_size)
        sources[0] = sources[0].at[:, pl.ds(at, gain_size)]
    sources += weight_blocks(z, jobs, weights)
    for copy in start_copies(list(zip(sources, outs)), sems):
        copy.wait()


def attend_kernel(z, ctx, jobs, list_hbm, count_hbm, *rest):
    weights, pieces, rest = rest[:3], rest[3 : 3 + z.toks], rest[3 + z.toks :]
    send_ref, back_refs, rest = rest[0], rest[1 : 1 + z.toks], rest[1 + z.toks :]
    blocks, rest = rest[: len(jobs)], rest[len(jobs) :]
    cache, req, query, own_key, own_value, alive, mixed_all, list_ref, count_ref, table_sems, sems = rest
    tables = start_copies([(list_hbm, list_ref), (count_hbm, count_ref)], table_sems)
    copies = start_copies(list(zip(weight_blocks(z, jobs, weights), blocks)), sems)

    @after_starts
    def _():
        tok = lax.axis_index("tok")
        cache_rows = z.cap * ctx
        for s in range(z.toks):
            source = tok ^ s
            cache[source] = pieces[s][: z.cap].reshape(cache_rows, cache.shape[2])
            for p in range(z.pieces):
                at, lane = z.cap + p // z.blocks, p % z.blocks * HEAD_DIM
                r, part = p * 16 // z.req_rows, p * 16 % z.req_rows
                req[source * 2 + r, part : part + 16, :] = pieces[s][
                    at, :, lane : lane + HEAD_DIM
                ].astype(F32)
        for table in tables:
            table.wait()
        for g in range(z.toks):
            for k in range(z.cap):
                live = (k < count_ref[0, g]).astype(F32)
                rows = req[list_ref[k, 0, g]] * live
                at = (g * z.cap + k) * z.group
                for j in range(z.kvs):
                    query[j, at : at + z.group, :] = rows[j * z.group : (j + 1) * z.group, :]
                    key, value = z.heads + j, z.heads + z.kvs + j
                    own_key[j, at : at + z.group, :] = jnp.broadcast_to(
                        rows[key : key + 1, :], (z.group, HEAD_DIM)
                    )
                    own_value[j, at : at + z.group, :] = jnp.broadcast_to(
                        rows[value : value + 1, :], (z.group, HEAD_DIM)
                    )
                alive[at : at + z.group, :] = jnp.full((z.group, HEAD_DIM), live, F32)
        many, keys = z.lane_slots * z.group, z.toks * cache_rows
        row_slot = lax.broadcasted_iota(jnp.int32, (many, keys), 0) // z.group
        key_slot = lax.broadcasted_iota(jnp.int32, (many, keys), 1) // ctx
        same = row_slot == key_slot
        scale = HEAD_DIM ** (-0.5)
        for j in range(z.kvs):
            cached_keys = cache[:, :, j * HEAD_DIM : (j + 1) * HEAD_DIM].reshape(keys, HEAD_DIM)
            at = (z.kvs + j) * HEAD_DIM
            cached_values = cache[:, :, at : at + HEAD_DIM].reshape(keys, HEAD_DIM)
            past = (
                lax.dot_general(
                    query[j].astype(BF16),
                    cached_keys,
                    (((1,), (1,)), ((), ())),
                    preferred_element_type=F32,
                )
                * scale
            )
            own = jnp.sum(query[j] * own_key[j], axis=-1, keepdims=True) * scale
            top = jnp.maximum(jnp.max(jnp.where(same, past, -jnp.inf), axis=-1, keepdims=True), own)
            past_exp = jnp.where(same, jnp.exp(jnp.where(same, past - top, 0.0)), 0.0)
            own_exp = jnp.exp(own - top)
            total = jnp.sum(past_exp, axis=-1, keepdims=True) + own_exp
            weights = (past_exp / total).astype(BF16)
            own_weight = (own_exp / total).astype(BF16).astype(F32)
            mixed = jnp.dot(weights, cached_values, preferred_element_type=F32)
            mixed = (mixed + own_weight * own_value[j]) * alive[...]
            mixed_all[j * many : (j + 1) * many, :] = mixed.astype(BF16).astype(F32)
        block = z.cap * z.group
        for s in range(z.toks):
            for j in range(z.kvs):
                at = pl.multiple_of(j * many + (tok ^ s) * block, block if block % 8 == 0 else 4)
                back_refs[s][j * block : (j + 1) * block, :] = mixed_all[pl.ds(at, block), :].astype(BF16)
        count = z.kvs * z.lane_slots
        for h in range(z.group):
            send_ref[:, h * HEAD_DIM : (h + 1) * HEAD_DIM] = mixed_all[
                pl.ds(h, count, stride=z.group), :
            ].astype(BF16)

    for copy in copies:
        copy.wait()


def halves(value):
    high = value.astype(BF16).astype(F32)
    return high, value - high


def two_lanes(high, low, rows):
    lane = lax.broadcasted_iota(jnp.int32, (rows, HEAD_DIM), 1)
    return jnp.where(lane == 0, high, jnp.where(lane == 1, low, 0.0)).astype(BF16)


def slot_of_row(z, col, shape):
    row = lax.broadcasted_iota(jnp.int32, shape, 0)
    return ((row // z.lane_slots) ^ col) * z.lane_slots + row % z.lane_slots


def tile_terms(z, source, delta_ref, index_ref, matrix, extra, out_base):
    side = delta_ref.shape[-1]
    col = lax.axis_index("col")
    variant = slot_of_row(z, col, (z.rows, side)) // (2 * z.cols * z.cap)
    for n in range(delta_ref.shape[2]):
        at = pl.multiple_of(index_ref[0, matrix, 1, 0, n] * side, side)
        to = pl.multiple_of(out_base + index_ref[0, matrix, 2, 0, n] * side, side)
        rows = jnp.where(variant == index_ref[0, matrix, 0, 0, n], source[:, pl.ds(at, side)], 0)
        extra[:, pl.ds(to, side)] += jnp.dot(
            rows.astype(BF16), delta_ref[0, 0, n], preferred_element_type=F32
        )


def project_steps(z, chunk, source, extra, blocks, send_ref, keep_ref):
    core = lax.axis_index("tok") % 2
    units = extra.shape[1] // 2
    first, size = z.parts[chunk]
    steps = []
    for n, (out_ref, side) in enumerate(((send_ref, 1 - core), (keep_ref, core))):
        for m in range(2):
            for p in range(size // z.step):
                block = blocks[(2 * n + m) * (size // z.step) + p]
                at = side * (units // 2) + m * units + first + p * z.step
                to = m * size + p * z.step

                def step(block=block, at=pl.multiple_of(at, HEAD_DIM), to=to, out_ref=out_ref):
                    value = jnp.dot(source[...], block[...], preferred_element_type=F32)
                    value += extra[:, pl.ds(at, z.step)]
                    out_ref[:, to : to + z.step] = value.astype(BF16)

                steps.append(step)
    return steps


def first_project_kernel(z, jobs, index_hbm, gain_ref, gate_delta, up_delta, *rest):
    pieces, rest = rest[: z.cols], rest[z.cols :]
    odd_backs, rest = rest[: z.toks // 2], rest[z.toks // 2 :]
    count = len(z.blocks_of[0])
    weights, blocks, rest = rest[:3], rest[3 : 3 + count], rest[3 + count :]
    send_ref, keep_ref, source, extra, *fetched = rest[: 4 + len(jobs)]
    index_ref, index_sem, sems = rest[4 + len(jobs) :]
    table = pltpu.make_async_copy(index_hbm, index_ref, index_sem)
    table.start()
    copies = start_copies(list(zip(weight_blocks(z, jobs, weights), fetched)), sems)
    units = extra.shape[1] // 2

    @after_starts
    def _():
        gather_rows(z, pieces, gain_ref, odd_backs, source, extra, send_ref, keep_ref)

    table.wait()

    @after_starts
    def _():
        tile_terms(z, source, gate_delta, index_ref, 0, extra, 0)
        tile_terms(z, source, up_delta, index_ref, 1, extra, units)
        for step in project_steps(z, 0, source, extra, blocks, send_ref, keep_ref):
            step()

    for copy in copies:
        copy.wait()


def gather_rows(z, pieces, gain_ref, odd_backs, source, extra, send_ref, keep_ref):
    col = lax.axis_index("col")
    extra[...] = jnp.zeros_like(extra)
    count = z.kvs * z.lane_slots
    wide = z.group * HEAD_DIM
    slot = slot_of_row(z, col, (z.rows, count))
    lane_of, owner = slot // z.cap % z.cols, slot // (z.cols * z.cap)
    column = lax.broadcasted_iota(jnp.int32, (z.rows, count), 1)
    squares = jnp.zeros((z.rows, 1), F32)
    for j in range(z.kvs):
        place = j * z.lane_slots + owner * z.cap + slot % z.cap
        found = jnp.zeros((z.rows, wide), F32)
        for s in range(z.cols):
            pick = ((lane_of == (col ^ s)) & (column == place)).astype(F32).astype(BF16)
            found += jnp.dot(pick, pieces[s][...], preferred_element_type=F32)
        squares += jnp.sum(found * found, axis=-1, keepdims=True)
        lanes = slice(j * wide, (j + 1) * wide)
        source[:, lanes] = (found * gain_ref[:, lanes]).astype(BF16)
    tail = z.tail
    for ref in (send_ref, keep_ref):
        ref[:, tail : tail + HEAD_DIM] = two_lanes(*halves(squares), z.rows)
    send_ref[:, tail + HEAD_DIM :] = jnp.zeros((z.rows, z.toks // 2 * HEAD_DIM), BF16)
    for n, ref in enumerate(odd_backs):
        lane = tail + (n + 1) * HEAD_DIM
        send_ref[: ref.shape[0], lane : lane + HEAD_DIM] = ref[...]


def next_project_kernel(z, jobs, delta_hbm, *rest):
    count = sum(len(some) for some in z.blocks_of[1:])
    here = sum(len(job) > 2 for job in jobs)
    weights, (source, extra), rest = rest[:3], rest[3:5], rest[5:]
    blocks, rest = rest[: count - here], rest[count - here :]
    sums = 2 * (z.chunks - 1)
    outs, (delta_ref, *fetched) = rest[:sums], rest[sums:-1]
    copies = start_copies(
        list(zip(weight_blocks(z, jobs, weights) + [delta_hbm], fetched + [delta_ref])), rest[-1]
    )
    blocks = list(blocks) + fetched[:here]
    steps = []
    for q in range(1, z.chunks):
        refs = blocks[len(steps) : len(steps) + len(z.blocks_of[q])]
        steps += project_steps(z, q, source, extra, refs, outs[2 * q - 2], outs[2 * q - 1])

    @after_starts
    def _():
        for step in steps[: count - here]:
            step()

    for n in range(here):
        copies[n].wait()
        after_starts(steps[count - here + n])
    for copy in copies[here:]:
        copy.wait()


def add_kernel(z, mine, other, out_ref):
    size = mine.shape[1] // (2 * HEAD_DIM) * (2 * HEAD_DIM)
    out_ref[:, :size] = (mine[:, :size].astype(F32) + other[:, :size].astype(F32)).astype(BF16)
    if mine.shape[1] > size:
        lanes = slice(size, size + HEAD_DIM)
        total = mine[:, lanes].astype(F32) + other[:, lanes].astype(F32)
        out_ref[:, lanes] = two_lanes(*halves(jnp.sum(total, axis=-1, keepdims=True)), z.rows)


def hidden_kernel(z, width, *refs):
    chips = z.toks // 2
    out_ref = refs[-1]
    squares = sum(ref[:, z.tail : z.tail + HEAD_DIM].astype(F32) for ref in refs[:chips])
    squares = jnp.sum(squares, axis=-1, keepdims=True)
    scale = lax.rsqrt(squares * (1.0 / width) + 1e-06)
    for q, (first, size) in enumerate(z.parts):
        parts = refs[q * chips : (q + 1) * chips]
        step = min(size, 256)
        for at in range(0, size, step):
            gate = sum(ref[:, at : at + step].astype(F32) for ref in parts) * scale
            up = sum(ref[:, size + at : size + at + step].astype(F32) for ref in parts) * scale
            out_ref[:, first + at : first + at + step] = (jax.nn.silu(gate) * up).astype(BF16)


def down_products(z, mine, units_ref, weights, total, before=None):
    width = total.shape[1]
    places = [at for is_mine, at in z.downs if is_mine == mine]
    step = min(width, 512)
    for to in range(0, width, step):
        lanes = slice(to, to + step)
        value = jnp.zeros((z.rows, step), F32) if before is None else before[:, lanes]
        for at, weight in zip(places, weights):
            units = units_ref[:, at : at + weight.shape[0]]
            value += jnp.dot(units, weight[:, lanes], preferred_element_type=F32)
        total[:, lanes] = value


def down_mine_kernel(z, mine, *rest):
    down_products(z, True, mine, rest[:-1], rest[-1])


def down_kernel(z, index_hbm, delta_ref, before, mine, other, from_core, *rest):
    others = z.toks // 2 - 1
    evens, rest = rest[:others], rest[others:]
    weights, rest = rest[: len(z.downs) // 2], rest[len(z.downs) // 2 :]
    outs, backs, rest = rest[: z.cols], rest[z.cols : z.cols + others], rest[z.cols + others :]
    source, total, fold, index_ref, index_sem = rest
    table = pltpu.make_async_copy(index_hbm, index_ref, index_sem)
    table.start()

    @after_starts
    def _():
        core = lax.axis_index("tok") % 2
        half = mine.shape[1]
        source[:, pl.ds(pl.multiple_of(core * half, half), half)] = mine[...]
        source[:, pl.ds(pl.multiple_of((1 - core) * half, half), half)] = other[...]
        down_products(z, False, other, weights, total, before)

    for s, back in enumerate(backs):
        back[:, :HEAD_DIM] = evens[s][...]
        lane = z.tail + (s + 2) * HEAD_DIM
        back[:, HEAD_DIM:] = from_core[: back.shape[0], lane : lane + HEAD_DIM]
    table.wait()
    tile_terms(z, source, delta_ref, index_ref, 2, total, 0)
    width = total.shape[1]
    for s in range(z.cols):
        rows = slice(s * z.lane_slots, (s + 1) * z.lane_slots)
        fold[: z.lane_slots, :] = total[rows, : width // 2]
        fold[z.lane_slots :, :] = total[rows, width // 2 :]
        outs[s][...] = fold[...].astype(BF16)


def finish_kernel(z, *refs):
    parts, out_ref = refs[: z.cols], refs[z.cols]
    total = sum(ref[...].astype(F32) for ref in parts)
    half = total.shape[1]
    out_ref[:, :half] = total[: z.lane_slots].astype(BF16)
    out_ref[:, half:] = total[z.lane_slots :].astype(BF16)


def return_kernel(z, own, from_core, *refs):
    chips = z.toks // 2
    parts, (out_ref, rows) = refs[: chips - 1], refs[chips - 1 :]
    tok = lax.axis_index("tok")
    block = z.cap * z.group
    count = z.kvs * block
    tail = z.tail + HEAD_DIM
    for s in range(z.toks):
        if s == 0:
            rows[...] = own[...].astype(F32)
        elif s == 1:
            rows[...] = from_core[:count, tail : tail + HEAD_DIM].astype(F32)
        else:
            lane = s % 2 * HEAD_DIM
            rows[...] = parts[s // 2 - 1][:, lane : lane + HEAD_DIM].astype(F32)
        first = pl.multiple_of((tok ^ s) * z.heads * HEAD_DIM, HEAD_DIM)
        for j in range(z.kvs):
            for h in range(z.group):
                to = first + (j * z.group + h) * HEAD_DIM
                out_ref[:, pl.ds(to, HEAD_DIM)] = rows[
                    pl.ds(j * block + h, z.cap, stride=z.group), :
                ].astype(BF16)


def swap(array, axis, size, distance):
    return lax.ppermute(array, axis, [(i, i ^ distance) for i in range(size)])


def local(
    request_rows,
    key_cache,
    route_list,
    route_count,
    norm_gain,
    gate_weight,
    up_weight,
    down_weight,
    gate_delta,
    up_delta,
    down_delta,
    tile_index,
):
    toks, cols = lax.axis_size("tok"), lax.axis_size("col")
    cap, ctx = key_cache.shape[0], key_cache.shape[1]
    features, units = gate_weight.shape
    z = Sizes(toks, cols, cap, units)
    width = norm_gain.shape[0]
    cache_rows = cap * ctx
    lanes = 2 * z.kvs * HEAD_DIM
    piece_shape = (cap + -(-z.pieces // z.blocks), ctx, lanes)
    many = z.lane_slots * z.group
    chips = toks // 2
    gain = norm_gain.reshape(1, width)
    route_list = route_list.transpose(2, 1, 0)
    route_count = route_count.transpose(1, 0)
    tile_index = tile_index.transpose(0, 2, 4, 1, 3)
    dma = pltpu.SemaphoreType.DMA

    jobs = [job for some in z.blocks_of for job in some]
    used = len(jobs)
    jobs += z.downs
    cuts = [0]
    for count in FETCH:
        cuts.append(cuts[-1] + count)
    first, early, middle, late, beside, between, last, final = [jobs[a:b] for a, b in zip(cuts, cuts[1:])]
    weights = [(gate_weight, HBM), (up_weight, HBM), (down_weight, HBM)]

    def shapes(some):
        up, down = (features, z.step), (units // 8, down_weight.shape[1])
        return [(up if len(job) > 2 else down, BF16) for job in some]

    def traffic(some):
        moved = sum(a * b * 2 for (a, b), _ in shapes(some))
        return pl.CostEstimate(flops=0, bytes_accessed=moved, transcendentals=0)

    pieces = call(
        functools.partial(pack_kernel, z, ctx, first),
        "pack",
        [(request_rows, HBM), (key_cache, HBM)] + weights,
        [(piece_shape, BF16)] * toks + shapes(first),
        [
            pltpu.VMEM(request_rows.shape, BF16),
            pltpu.VMEM(request_rows.shape, F32),
            pltpu.VMEM((toks, 2 * z.req_rows, HEAD_DIM), F32),
            dma,
            dma((toks, 2)),
            dma((max(1, len(first)),)),
        ],
    )
    pieces, blocks = pieces[:toks], pieces[toks:]
    whole = [gain, gate_delta, up_delta]
    gain, gate_delta, up_delta, *fetched = call(
        functools.partial(fetch_kernel, z, early, whole, features),
        "fetch_early",
        weights + [(a, HBM) for a in whole],
        [((1, features), F32), (gate_delta.shape, BF16), (up_delta.shape, BF16)]
        + shapes(early),
        [dma((len(early) + 3,))],
        after=pieces[:1],
        cost=traffic(early),
    )
    blocks += fetched
    pieces = [pieces[0]] + [swap(pieces[s], "tok", toks, s) for s in range(1, toks)]
    back_rows = z.kvs * cap * z.group
    send, *rest = call(
        functools.partial(attend_kernel, z, ctx, middle),
        "attend",
        [(route_list, HBM), (route_count, HBM)] + weights + [(p, VMEM) for p in pieces],
        [((z.kvs * z.lane_slots, z.group * HEAD_DIM), BF16)]
        + [((back_rows, HEAD_DIM), BF16)] * toks
        + shapes(middle),
        [
            pltpu.VMEM((toks, cache_rows, lanes), BF16),
            pltpu.VMEM((2 * toks, z.req_rows, HEAD_DIM), F32),
            pltpu.VMEM((z.kvs, many, HEAD_DIM), F32),
            pltpu.VMEM((z.kvs, many, HEAD_DIM), F32),
            pltpu.VMEM((z.kvs, many, HEAD_DIM), F32),
            pltpu.VMEM((many, HEAD_DIM), F32),
            pltpu.VMEM((z.kvs * many, HEAD_DIM), F32),
            pltpu.SMEM(route_list.shape, jnp.int32),
            pltpu.SMEM(route_count.shape, jnp.int32),
            dma((2,)),
            dma((max(1, len(middle)),)),
        ],
        after=[gain],
    )
    back = rest[:toks]
    blocks += rest[toks:]
    blocks += call(
        functools.partial(fetch_kernel, z, late, [], 0),
        "fetch_late",
        weights,
        shapes(late),
        [dma((len(late),))],
        after=[send],
        cost=traffic(late),
    )
    pieces = [send] + [swap(send, "col", cols, s) for s in range(1, cols)]
    out_width = down_weight.shape[1]
    table = pltpu.SMEM(tile_index.shape, jnp.int32)
    sent, kept, source, extra, *fetched = call(
        functools.partial(first_project_kernel, z, beside),
        "project_first",
        [
            (tile_index, HBM),
            (gain, VMEM),
            (gate_delta, VMEM),
            (up_delta, VMEM),
        ]
        + [(p, VMEM) for p in pieces + back[1::2]]
        + weights
        + [(p, VMEM) for p in blocks[: len(z.blocks_of[0])]],
        [
            ((z.rows, z.tail + (1 + chips) * HEAD_DIM), BF16),
            ((z.rows, z.tail + HEAD_DIM), BF16),
            ((z.rows, features), BF16),
            ((z.rows, 2 * units), F32),
        ]
        + shapes(beside),
        [table, dma, dma((len(beside),))],
        after=blocks[-1:],
    )
    blocks = blocks[len(z.blocks_of[0]) :] + fetched
    fetched = call(
        functools.partial(fetch_kernel, z, between, [], 0),
        "fetch_between",
        weights,
        shapes(between),
        [dma((len(between),))],
        cost=traffic(between),
        after=[sent],
    )
    blocks += fetched
    from_core = swap(sent, "tok", toks, 1)
    totals = [
        call(
            functools.partial(add_kernel, z),
            "chip_sum_first",
            [(kept, VMEM), (from_core, VMEM)],
            [((z.rows, z.tail + HEAD_DIM), BF16)],
            after=fetched[-1:],
        )
    ]
    sizes = [2 * size for _, size in z.parts[1:]]
    *sums, down_delta = call(
        functools.partial(next_project_kernel, z, last),
        "project_next",
        [(down_delta, HBM)] + weights + [(a, VMEM) for a in [source, extra] + blocks[: used - len(z.blocks_of[0])]],
        [((z.rows, size), BF16) for size in sizes for _ in range(2)]
        + [(down_delta.shape, BF16)]
        + shapes(last),
        [dma((len(last) + 1,))],
        cost=pl.CostEstimate(
            flops=4 * z.rows * features * sum(sizes),
            bytes_accessed=4 * features * sum(sizes),
            transcendentals=0,
        ),
        after=totals[0][:1],
    )
    rest = sums[2 * len(sizes) :] + [down_delta]
    down_delta, blocks = rest[0], blocks + rest[1:]
    for q, size in enumerate(sizes):
        sent, kept = sums[2 * q : 2 * q + 2]
        other = swap(sent, "tok", toks, 1)
        totals.append(
            call(
                functools.partial(add_kernel, z),
                "chip_sum_next",
                [(kept, VMEM), (other, VMEM)],
                [((z.rows, size), BF16)],
            )
        )
    parts = [
        total + [swap(total[0], "tok", toks, 2 * s) for s in range(1, chips)]
        for total in totals
    ]
    fetched = call(
        functools.partial(fetch_kernel, z, final, [], 0),
        "fetch_down",
        weights,
        shapes(final),
        [dma((len(final),))],
        cost=traffic(final),
        after=totals[-1],
    )
    down_blocks = (blocks + fetched)[-len(z.downs) :]
    (hidden,) = call(
        functools.partial(hidden_kernel, z, width),
        "hidden",
        [(a, VMEM) for part in parts for a in part],
        [((z.rows, units // 2), BF16)],
        after=fetched[-1:],
    )
    half = len(z.downs) // 2
    (before,) = call(
        functools.partial(down_mine_kernel, z),
        "down_mine",
        [(a, VMEM) for a in [hidden] + down_blocks[:half]],
        [((z.rows, out_width), F32)],
        cost=pl.CostEstimate(
            flops=z.rows * units * out_width, bytes_accessed=units * out_width, transcendentals=0
        ),
    )
    parts = call(
        functools.partial(down_kernel, z),
        "down",
        [(tile_index, HBM)]
        + [(a, VMEM) for a in [down_delta, before, hidden, swap(hidden, "tok", toks, 1), from_core]]
        + [(a, VMEM) for a in back[2::2] + down_blocks[half:]],
        [((2 * z.lane_slots, out_width // 2), BF16)] * cols
        + [((back_rows, 2 * HEAD_DIM), BF16)] * (chips - 1),
        [
            pltpu.VMEM((z.rows, units), BF16),
            pltpu.VMEM((z.rows, out_width), F32),
            pltpu.VMEM((2 * z.lane_slots, out_width // 2), F32),
            table,
            dma,
        ],
    )
    parts, across = parts[:cols], parts[cols:]
    parts = [parts[0]] + [swap(parts[s], "col", cols, s) for s in range(1, cols)]
    across = [swap(rows, "tok", toks, 2 * s + 2) for s, rows in enumerate(across)]
    (attended,) = call(
        functools.partial(return_kernel, z),
        "attended",
        [(a, VMEM) for a in [back[0], from_core] + across],
        [((cap, width), BF16)],
        [pltpu.VMEM((back_rows, HEAD_DIM), F32)],
    )
    (ffn_out,) = call(
        functools.partial(finish_kernel, z),
        "finish",
        [(p, VMEM) for p in parts],
        [((z.lane_slots, out_width), BF16)],
    )
    return attended, ffn_out


def solution(mesh):
    in_specs = (
        P(("rep", "tok", "col"), None),
        P(("rep", "tok", "col"), None, None),
        P("rep", "col", None),
        P("rep", "col"),
        P(),
        P("tok", "col"),
        P("tok", "col"),
        P("col", "tok"),
        P("tok", "col", None, None, None),
        P("tok", "col", None, None, None),
        P("tok", "col", None, None, None),
        P("tok", "col", None, None, None),
    )
    out_specs = (P(("rep", "tok", "col"), None), P(("rep", "col"), "tok"))
    return jax.shard_map(local, mesh=mesh, in_specs=in_specs, out_specs=out_specs, check_vma=False)
```

```python
import functools

import jax
import jax.numpy as jnp
from jax import lax
from jax.experimental import pallas as pl
from jax.experimental.pallas import tpu as pltpu
from jax.sharding import PartitionSpec as P

HEADS = 64
KV_HEADS = 8
HEAD_DIM = 128
GROUP = HEADS // KV_HEADS
MIB = 1 << 20
FETCH = (0, 3, 1, 4, 5, 1, 2, 1, 6, 1)
CUTS = (4, 6)
BF16 = jnp.bfloat16
F32 = jnp.float32
VMEM = pltpu.VMEM
HBM = pltpu.HBM


def call(kernel, name, ins, outs, scratch=(), limit=8, cost=None, after=(), out=VMEM):
    if cost is None:
        cost = pl.CostEstimate(flops=0, bytes_accessed=1024, transcendentals=0)
    count = len(ins)
    ins = ins + [(a, VMEM) for a in after]

    def body(*refs):
        kernel(*refs[:count], *refs[count + len(after) :])

    return list(
        pl.pallas_call(
            body,
            name=name,
            in_specs=[pl.BlockSpec(memory_space=s) for _, s in ins],
            out_specs=[pl.BlockSpec(memory_space=out) for _ in outs],
            out_shape=[out(shape, dtype) for shape, dtype in outs],
            scratch_shapes=list(scratch),
            cost_estimate=cost,
            compiler_params=pltpu.CompilerParams(vmem_limit_bytes=limit * MIB),
        )(*[pltpu.with_memory_space_constraint(a, space) for a, space in ins])
    )


class Sizes:
    def __init__(self, toks, cols, cap, units):
        self.toks, self.cols, self.cap = toks, cols, cap
        half = units // 2
        cuts = [half * n // 8 for n in CUTS]
        self.parts = list(zip([0] + cuts, [b - a for a, b in zip([0] + cuts, cuts + [half])]))
        self.chunks = len(self.parts)
        self.step = min(512, min(size for _, size in self.parts))
        self.blocks_of = [
            [
                (q, keep, m, first + at)
                for keep in (False, True)
                for m in range(2)
                for at in range(0, size, self.step)
            ]
            for q, (first, size) in enumerate(self.parts)
        ]
        self.downs = [(mine, n * half // 4) for mine in (True, False) for n in range(4)]
        self.tail = 2 * self.parts[0][1]
        self.heads = HEADS // toks
        self.kvs = max(1, self.heads // GROUP)
        self.group = self.heads // self.kvs
        self.lane_slots = toks * cap
        self.rows = toks * cols * cap
        self.req_rows = -(-(self.heads + 2 * self.kvs) // 16) * 16
        self.blocks = 2 * self.kvs
        self.pieces = 2 * self.req_rows // 16

    def first_kv(self, tok):
        return tok * self.heads // GROUP


def pack_kernel(z, ctx, jobs, req_ref, cache_ref, *rest):
    weights, outs, rest = rest[:3], rest[3 : 3 + z.toks], rest[3 + z.toks :]
    blocks, (narrow, wide, rows, req_sem, sems, block_sems) = rest[: len(jobs)], rest[len(jobs) :]
    tok = lax.axis_index("tok")
    width = z.kvs * HEAD_DIM
    pairs = KV_HEADS * HEAD_DIM
    fetch = pltpu.make_async_copy(req_ref, narrow, req_sem)
    fetch.start()
    copies = []
    for s in reversed(range(z.toks)):
        first = pl.multiple_of(z.first_kv(tok ^ s) * HEAD_DIM, HEAD_DIM)
        for half in range(2):
            copy = pltpu.make_async_copy(
                cache_ref.at[:, :, pl.ds(half * pairs + first, width)],
                outs[s].at[: z.cap, :, pl.ds(half * width, width)],
                sems.at[s, half],
            )
            copy.start()
            copies.append(copy)
    copies += start_copies(list(zip(weight_blocks(z, jobs, weights), blocks)), block_sems)
    fetch.wait()

    @after_starts
    def _():
        rows[...] = jnp.zeros_like(rows)
        wide[...] = narrow[...].astype(F32)
        for s in range(z.toks):
            to = tok ^ s
            starts = [(to * z.heads + h) * HEAD_DIM for h in range(z.heads)]
            for half in range(2):
                starts += [
                    HEADS * HEAD_DIM + half * pairs + (z.first_kv(to) + j) * HEAD_DIM
                    for j in range(z.kvs)
                ]
            for r in range(2):
                for n, start in enumerate(starts):
                    at = r * z.req_rows + n
                    rows[s, at : at + 1, :] = wide[
                        r : r + 1, pl.ds(pl.multiple_of(start, HEAD_DIM), HEAD_DIM)
                    ]
            for p in range(z.pieces):
                at, lane = z.cap + p // z.blocks, p % z.blocks * HEAD_DIM
                outs[s][at, :, lane : lane + HEAD_DIM] = rows[s, p * 16 : p * 16 + 16, :].astype(BF16)

    for copy in copies:
        copy.wait()


def start_copies(pairs, sems):
    copies = [pltpu.make_async_copy(src, dst, sems.at[n]) for n, (src, dst) in enumerate(pairs)]
    for copy in copies:
        copy.start()
    return copies


def after_starts(compute):
    pl.when(lax.axis_index("tok") >= 0)(compute)


def weight_blocks(z, jobs, refs):
    core = lax.axis_index("tok") % 2
    half = refs[0].shape[1] // 2
    found = []
    for job in jobs:
        at = pl.multiple_of((core if job[-3 if len(job) > 2 else 0] else 1 - core) * half, half)
        if len(job) > 2:
            _, _, matrix, first = job
            found.append(refs[matrix].at[:, pl.ds(at + first, z.step)])
        else:
            found.append(refs[2].at[pl.ds(at + job[1], half // 4), :])
    return found


def fetch_kernel(z, jobs, whole, gain_size, *refs):
    weights, rest = refs[:3], refs[3:]
    sources, rest = list(rest[: len(whole)]), rest[len(whole) :]
    outs, sems = rest[:-1], rest[-1]
    if gain_size:
        tok = lax.axis_index("tok")
        at = pl.multiple_of(tok * gain_size, gain_size)
        sources[0] = sources[0].at[:, pl.ds(at, gain_size)]
    sources += weight_blocks(z, jobs, weights)
    for copy in start_copies(list(zip(sources, outs)), sems):
        copy.wait()


def attend_kernel(z, ctx, jobs, list_hbm, count_hbm, *rest):
    weights, pieces, rest = rest[:3], rest[3 : 3 + z.toks], rest[3 + z.toks :]
    pieces = pieces[:1] + pieces[-1:] + pieces[1:-1]
    send_ref, back_refs, rest = rest[0], rest[1 : 1 + z.toks], rest[1 + z.toks :]
    blocks, rest = rest[: len(jobs)], rest[len(jobs) :]
    cache, req, query, own_key, own_value, alive, mixed_all, list_ref, count_ref, table_sems, sems = rest
    tables = start_copies([(list_hbm, list_ref), (count_hbm, count_ref)], table_sems)
    copies = start_copies(list(zip(weight_blocks(z, jobs, weights), blocks)), sems)

    @after_starts
    def _():
        tok = lax.axis_index("tok")
        cache_rows = z.cap * ctx
        for s in range(z.toks):
            source = tok ^ s
            cache[source] = pieces[s][: z.cap].reshape(cache_rows, cache.shape[2])
            for p in range(z.pieces):
                at, lane = z.cap + p // z.blocks, p % z.blocks * HEAD_DIM
                r, part = p * 16 // z.req_rows, p * 16 % z.req_rows
                req[source * 2 + r, part : part + 16, :] = pieces[s][
                    at, :, lane : lane + HEAD_DIM
                ].astype(F32)
        for table in tables:
            table.wait()
        for g in range(z.toks):
            for k in range(z.cap):
                live = (k < count_ref[0, g]).astype(F32)
                rows = req[list_ref[k, 0, g]] * live
                at = (g * z.cap + k) * z.group
                for j in range(z.kvs):
                    query[j, at : at + z.group, :] = rows[j * z.group : (j + 1) * z.group, :]
                    key, value = z.heads + j, z.heads + z.kvs + j
                    own_key[j, at : at + z.group, :] = jnp.broadcast_to(
                        rows[key : key + 1, :], (z.group, HEAD_DIM)
                    )
                    own_value[j, at : at + z.group, :] = jnp.broadcast_to(
                        rows[value : value + 1, :], (z.group, HEAD_DIM)
                    )
                alive[at : at + z.group, :] = jnp.full((z.group, HEAD_DIM), live, F32)
        many, keys = z.lane_slots * z.group, z.toks * cache_rows
        row_slot = lax.broadcasted_iota(jnp.int32, (many, keys), 0) // z.group
        key_slot = lax.broadcasted_iota(jnp.int32, (many, keys), 1) // ctx
        same = row_slot == key_slot
        scale = HEAD_DIM ** (-0.5)
        for j in range(z.kvs):
            cached_keys = cache[:, :, j * HEAD_DIM : (j + 1) * HEAD_DIM].reshape(keys, HEAD_DIM)
            at = (z.kvs + j) * HEAD_DIM
            cached_values = cache[:, :, at : at + HEAD_DIM].reshape(keys, HEAD_DIM)
            past = (
                lax.dot_general(
                    query[j].astype(BF16),
                    cached_keys,
                    (((1,), (1,)), ((), ())),
                    preferred_element_type=F32,
                )
                * scale
            )
            own = jnp.sum(query[j] * own_key[j], axis=-1, keepdims=True) * scale
            top = jnp.maximum(jnp.max(jnp.where(same, past, -jnp.inf), axis=-1, keepdims=True), own)
            past_exp = jnp.where(same, jnp.exp(jnp.where(same, past - top, 0.0)), 0.0)
            own_exp = jnp.exp(own - top)
            total = jnp.sum(past_exp, axis=-1, keepdims=True) + own_exp
            weights = (past_exp / total).astype(BF16)
            own_weight = (own_exp / total).astype(BF16).astype(F32)
            mixed = jnp.dot(weights, cached_values, preferred_element_type=F32)
            mixed = (mixed + own_weight * own_value[j]) * alive[...]
            mixed_all[j * many : (j + 1) * many, :] = mixed.astype(BF16).astype(F32)
        block = z.cap * z.group
        for s in range(z.toks):
            for j in range(z.kvs):
                at = pl.multiple_of(j * many + (tok ^ s) * block, block if block % 8 == 0 else 4)
                back_refs[s][j * block : (j + 1) * block, :] = mixed_all[pl.ds(at, block), :].astype(BF16)
        count = z.kvs * z.lane_slots
        for h in range(z.group):
            send_ref[:, h * HEAD_DIM : (h + 1) * HEAD_DIM] = mixed_all[
                pl.ds(h, count, stride=z.group), :
            ].astype(BF16)

    for copy in copies:
        copy.wait()


def halves(value):
    high = value.astype(BF16).astype(F32)
    return high, value - high


def two_lanes(high, low, rows):
    lane = lax.broadcasted_iota(jnp.int32, (rows, HEAD_DIM), 1)
    return jnp.where(lane == 0, high, jnp.where(lane == 1, low, 0.0)).astype(BF16)


def slot_of_row(z, col, shape):
    row = lax.broadcasted_iota(jnp.int32, shape, 0)
    return ((row // z.lane_slots) ^ col) * z.lane_slots + row % z.lane_slots


def tile_terms(z, source, delta_ref, index_ref, matrix, extra, out_base):
    side = delta_ref.shape[-1]
    col = lax.axis_index("col")
    variant = slot_of_row(z, col, (z.rows, side)) // (2 * z.cols * z.cap)
    for n in range(delta_ref.shape[2]):
        at = pl.multiple_of(index_ref[0, matrix, 1, 0, n] * side, side)
        to = pl.multiple_of(out_base + index_ref[0, matrix, 2, 0, n] * side, side)
        rows = jnp.where(variant == index_ref[0, matrix, 0, 0, n], source[:, pl.ds(at, side)], 0)
        extra[:, pl.ds(to, side)] += jnp.dot(
            rows.astype(BF16), delta_ref[0, 0, n], preferred_element_type=F32
        )


def project_steps(z, chunk, source, extra, blocks, send_ref, keep_ref):
    core = lax.axis_index("tok") % 2
    units = extra.shape[1] // 2
    first, size = z.parts[chunk]
    steps = []
    for n, (out_ref, side) in enumerate(((send_ref, 1 - core), (keep_ref, core))):
        for m in range(2):
            for p in range(size // z.step):
                block = blocks[(2 * n + m) * (size // z.step) + p]
                at = side * (units // 2) + m * units + first + p * z.step
                to = m * size + p * z.step

                def step(block=block, at=pl.multiple_of(at, HEAD_DIM), to=to, out_ref=out_ref):
                    value = jnp.dot(source[...], block[...], preferred_element_type=F32)
                    value += extra[:, pl.ds(at, z.step)]
                    out_ref[:, to : to + z.step] = value.astype(BF16)

                steps.append(step)
    return steps


def first_project_kernel(z, jobs, index_hbm, gain_ref, gate_delta, up_delta, *rest):
    pieces, rest = rest[: z.cols], rest[z.cols :]
    odd_backs, rest = rest[: z.toks // 2], rest[z.toks // 2 :]
    count = len(z.blocks_of[0])
    weights, blocks, rest = rest[:3], rest[3 : 3 + count], rest[3 + count :]
    send_ref, keep_ref, source, extra, *fetched = rest[: 4 + len(jobs)]
    index_ref, index_sem, sems = rest[4 + len(jobs) :]
    table = pltpu.make_async_copy(index_hbm, index_ref, index_sem)
    table.start()
    copies = start_copies(list(zip(weight_blocks(z, jobs, weights), fetched)), sems)
    units = extra.shape[1] // 2

    @after_starts
    def _():
        gather_rows(z, pieces, gain_ref, odd_backs, source, extra, send_ref, keep_ref)

    table.wait()

    @after_starts
    def _():
        tile_terms(z, source, gate_delta, index_ref, 0, extra, 0)
        tile_terms(z, source, up_delta, index_ref, 1, extra, units)
        for step in project_steps(z, 0, source, extra, blocks, send_ref, keep_ref):
            step()

    for copy in copies:
        copy.wait()


def gather_rows(z, pieces, gain_ref, odd_backs, source, extra, send_ref, keep_ref):
    col = lax.axis_index("col")
    extra[...] = jnp.zeros_like(extra)
    count = z.kvs * z.lane_slots
    wide = z.group * HEAD_DIM
    slot = slot_of_row(z, col, (z.rows, count))
    lane_of, owner = slot // z.cap % z.cols, slot // (z.cols * z.cap)
    column = lax.broadcasted_iota(jnp.int32, (z.rows, count), 1)
    squares = jnp.zeros((z.rows, 1), F32)
    for j in range(z.kvs):
        place = j * z.lane_slots + owner * z.cap + slot % z.cap
        found = jnp.zeros((z.rows, wide), F32)
        for s in range(z.cols):
            pick = ((lane_of == (col ^ s)) & (column == place)).astype(F32).astype(BF16)
            found += jnp.dot(pick, pieces[s][...], preferred_element_type=F32)
        squares += jnp.sum(found * found, axis=-1, keepdims=True)
        lanes = slice(j * wide, (j + 1) * wide)
        source[:, lanes] = (found * gain_ref[:, lanes]).astype(BF16)
    tail = z.tail
    for ref in (send_ref, keep_ref):
        ref[:, tail : tail + HEAD_DIM] = two_lanes(*halves(squares), z.rows)
    send_ref[:, tail + HEAD_DIM :] = jnp.zeros((z.rows, z.toks // 2 * HEAD_DIM), BF16)
    for n, ref in enumerate(odd_backs):
        lane = tail + (n + 1) * HEAD_DIM
        send_ref[: ref.shape[0], lane : lane + HEAD_DIM] = ref[...]


def next_project_kernel(z, q, jobs, *rest):
    weights, (source, extra), rest = rest[:3], rest[3:5], rest[5:]
    blocks, rest = rest[: len(z.blocks_of[q])], rest[len(z.blocks_of[q]) :]
    send_ref, keep_ref, *fetched, sems = rest
    copies = start_copies(list(zip(weight_blocks(z, jobs, weights), fetched)), sems)

    @after_starts
    def _():
        for step in project_steps(z, q, source, extra, blocks, send_ref, keep_ref):
            step()

    for copy in copies:
        copy.wait()


def add_kernel(z, mine, other, out_ref):
    size = mine.shape[1] // (2 * HEAD_DIM) * (2 * HEAD_DIM)
    out_ref[:, :size] = (mine[:, :size].astype(F32) + other[:, :size].astype(F32)).astype(BF16)
    if mine.shape[1] > size:
        lanes = slice(size, size + HEAD_DIM)
        total = mine[:, lanes].astype(F32) + other[:, lanes].astype(F32)
        out_ref[:, lanes] = two_lanes(*halves(jnp.sum(total, axis=-1, keepdims=True)), z.rows)


def hidden_kernel(z, width, *refs):
    chips = z.toks // 2
    out_ref = refs[-1]
    squares = sum(ref[:, z.tail : z.tail + HEAD_DIM].astype(F32) for ref in refs[:chips])
    squares = jnp.sum(squares, axis=-1, keepdims=True)
    scale = lax.rsqrt(squares * (1.0 / width) + 1e-06)
    for q, (first, size) in enumerate(z.parts):
        parts = refs[q * chips : (q + 1) * chips]
        step = min(size, 256)
        for at in range(0, size, step):
            gate = sum(ref[:, at : at + step].astype(F32) for ref in parts) * scale
            up = sum(ref[:, size + at : size + at + step].astype(F32) for ref in parts) * scale
            out_ref[:, first + at : first + at + step] = (jax.nn.silu(gate) * up).astype(BF16)


def down_products(z, mine, units_ref, weights, total, before=None):
    width = total.shape[1]
    places = [at for is_mine, at in z.downs if is_mine == mine]
    step = min(width, 512)
    for to in range(0, width, step):
        lanes = slice(to, to + step)
        value = jnp.zeros((z.rows, step), F32) if before is None else before[:, lanes]
        for at, weight in zip(places, weights):
            units = units_ref[:, at : at + weight.shape[0]]
            value += jnp.dot(units, weight[:, lanes], preferred_element_type=F32)
        total[:, lanes] = value


def down_mine_kernel(z, jobs, *rest):
    weights, mine, rest = rest[:3], rest[3], rest[4:]
    blocks, rest = rest[: len(z.downs) // 2], rest[len(z.downs) // 2 :]
    total, *fetched, sems = rest
    copies = start_copies(list(zip(weight_blocks(z, jobs, weights), fetched)), sems)
    after_starts(lambda: down_products(z, True, mine, blocks, total))
    for copy in copies:
        copy.wait()


def down_kernel(z, index_hbm, delta_ref, before, mine, other, from_core, *rest):
    others = z.toks // 2 - 1
    evens, rest = rest[:others], rest[others:]
    weights, rest = rest[: len(z.downs) // 2], rest[len(z.downs) // 2 :]
    outs, backs, rest = rest[: z.cols], rest[z.cols : z.cols + others], rest[z.cols + others :]
    source, total, fold, index_ref, index_sem = rest
    table = pltpu.make_async_copy(index_hbm, index_ref, index_sem)
    table.start()

    @after_starts
    def _():
        core = lax.axis_index("tok") % 2
        half = mine.shape[1]
        source[:, pl.ds(pl.multiple_of(core * half, half), half)] = mine[...]
        source[:, pl.ds(pl.multiple_of((1 - core) * half, half), half)] = other[...]
        down_products(z, False, other, weights, total, before)

    for s, back in enumerate(backs):
        back[:, :HEAD_DIM] = evens[s][...]
        lane = z.tail + (s + 2) * HEAD_DIM
        back[:, HEAD_DIM:] = from_core[: back.shape[0], lane : lane + HEAD_DIM]
    table.wait()
    tile_terms(z, source, delta_ref, index_ref, 2, total, 0)
    width = total.shape[1]
    for s in range(z.cols):
        rows = slice(s * z.lane_slots, (s + 1) * z.lane_slots)
        fold[: z.lane_slots, :] = total[rows, : width // 2]
        fold[z.lane_slots :, :] = total[rows, width // 2 :]
        outs[s][...] = fold[...].astype(BF16)


def finish_kernel(z, own, from_core, *refs):
    others = z.toks // 2 - 1
    across, parts, rest = refs[:others], refs[others : others + z.cols], refs[others + z.cols :]
    attended_hbm, out_hbm, attended, out, rows, sems = rest
    tok = lax.axis_index("tok")
    block = z.cap * z.group
    count = z.kvs * block
    tail = z.tail + HEAD_DIM
    for s in range(z.toks):
        if s == 0:
            rows[s] = own[...].astype(F32)
        elif s == 1:
            rows[s] = from_core[:count, tail : tail + HEAD_DIM].astype(F32)
        else:
            lane = s % 2 * HEAD_DIM
            rows[s] = across[s // 2 - 1][:, lane : lane + HEAD_DIM].astype(F32)
        first = pl.multiple_of((tok ^ s) * z.heads * HEAD_DIM, HEAD_DIM)
        for j in range(z.kvs):
            for h in range(z.group):
                to = first + (j * z.group + h) * HEAD_DIM
                attended[:, pl.ds(to, HEAD_DIM)] = rows[
                    s, pl.ds(j * block + h, z.cap, stride=z.group), :
                ].astype(BF16)
    copies = start_copies([(attended, attended_hbm)], sems)

    @after_starts
    def _():
        total = sum(ref[...].astype(F32) for ref in parts)
        half = total.shape[1]
        out[:, :half] = total[: z.lane_slots].astype(BF16)
        out[:, half:] = total[z.lane_slots :].astype(BF16)

    copy = pltpu.make_async_copy(out, out_hbm, sems.at[1])
    copy.start()
    for copy in copies + [copy]:
        copy.wait()


def swap(array, axis, size, distance):
    return lax.ppermute(array, axis, [(i, i ^ distance) for i in range(size)])


def local(
    request_rows,
    key_cache,
    route_list,
    route_count,
    norm_gain,
    gate_weight,
    up_weight,
    down_weight,
    gate_delta,
    up_delta,
    down_delta,
    tile_index,
):
    toks, cols = lax.axis_size("tok"), lax.axis_size("col")
    cap, ctx = key_cache.shape[0], key_cache.shape[1]
    features, units = gate_weight.shape
    z = Sizes(toks, cols, cap, units)
    width = norm_gain.shape[0]
    cache_rows = cap * ctx
    lanes = 2 * z.kvs * HEAD_DIM
    piece_shape = (cap + -(-z.pieces // z.blocks), ctx, lanes)
    many = z.lane_slots * z.group
    chips = toks // 2
    gain = norm_gain.reshape(1, width)
    route_list = route_list.transpose(2, 1, 0)
    route_count = route_count.transpose(1, 0)
    tile_index = tile_index.transpose(0, 2, 4, 1, 3)
    dma = pltpu.SemaphoreType.DMA

    jobs = [job for some in z.blocks_of for job in some]
    used = len(jobs)
    jobs += z.downs
    cuts = [0]
    for count in FETCH:
        cuts.append(cuts[-1] + count)
    first, early, middle, late, beside, between, *lasts, final, ending = [jobs[a:b] for a, b in zip(cuts, cuts[1:])]
    weights = [(gate_weight, HBM), (up_weight, HBM), (down_weight, HBM)]

    def shapes(some):
        up, down = (features, z.step), (units // 8, down_weight.shape[1])
        return [(up if len(job) > 2 else down, BF16) for job in some]

    def traffic(some):
        moved = sum(a * b * 2 for (a, b), _ in shapes(some))
        return pl.CostEstimate(flops=0, bytes_accessed=moved, transcendentals=0)

    pieces = call(
        functools.partial(pack_kernel, z, ctx, first),
        "pack",
        [(request_rows, HBM), (key_cache, HBM)] + weights,
        [(piece_shape, BF16)] * toks + shapes(first),
        [
            pltpu.VMEM(request_rows.shape, BF16),
            pltpu.VMEM(request_rows.shape, F32),
            pltpu.VMEM((toks, 2 * z.req_rows, HEAD_DIM), F32),
            dma,
            dma((toks, 2)),
            dma((max(1, len(first)),)),
        ],
    )
    pieces, blocks = pieces[:toks], pieces[toks:]
    whole = [gain, gate_delta, up_delta]
    gain, gate_delta, up_delta, *fetched = call(
        functools.partial(fetch_kernel, z, early, whole, features),
        "fetch_early",
        weights + [(a, HBM) for a in whole],
        [((1, features), F32), (gate_delta.shape, BF16), (up_delta.shape, BF16)]
        + shapes(early),
        [dma((len(early) + 3,))],
        after=pieces[:1],
        cost=traffic(early),
    )
    blocks += fetched
    pieces = [pieces[0]] + [swap(pieces[s], "tok", toks, s) for s in range(1, toks)]
    back_rows = z.kvs * cap * z.group
    send, *rest = call(
        functools.partial(attend_kernel, z, ctx, middle),
        "attend",
        [(route_list, HBM), (route_count, HBM)] + weights + [(p, VMEM) for p in pieces[:1] + pieces[2:] + pieces[1:2]],
        [((z.kvs * z.lane_slots, z.group * HEAD_DIM), BF16)]
        + [((back_rows, HEAD_DIM), BF16)] * toks
        + shapes(middle),
        [
            pltpu.VMEM((toks, cache_rows, lanes), BF16),
            pltpu.VMEM((2 * toks, z.req_rows, HEAD_DIM), F32),
            pltpu.VMEM((z.kvs, many, HEAD_DIM), F32),
            pltpu.VMEM((z.kvs, many, HEAD_DIM), F32),
            pltpu.VMEM((z.kvs, many, HEAD_DIM), F32),
            pltpu.VMEM((many, HEAD_DIM), F32),
            pltpu.VMEM((z.kvs * many, HEAD_DIM), F32),
            pltpu.SMEM(route_list.shape, jnp.int32),
            pltpu.SMEM(route_count.shape, jnp.int32),
            dma((2,)),
            dma((max(1, len(middle)),)),
        ],
        after=[gain],
    )
    back = rest[:toks]
    blocks += rest[toks:]
    blocks += call(
        functools.partial(fetch_kernel, z, late, [], 0),
        "fetch_late",
        weights,
        shapes(late),
        [dma((len(late),))],
        after=[send],
        cost=traffic(late),
    )
    pieces = [send] + [swap(send, "col", cols, s) for s in range(1, cols)]
    out_width = down_weight.shape[1]
    table = pltpu.SMEM(tile_index.shape, jnp.int32)
    sent, kept, source, extra, *fetched = call(
        functools.partial(first_project_kernel, z, beside),
        "project_first",
        [
            (tile_index, HBM),
            (gain, VMEM),
            (gate_delta, VMEM),
            (up_delta, VMEM),
        ]
        + [(p, VMEM) for p in pieces + back[1::2]]
        + weights
        + [(p, VMEM) for p in blocks[: len(z.blocks_of[0])]],
        [
            ((z.rows, z.tail + (1 + chips) * HEAD_DIM), BF16),
            ((z.rows, z.tail + HEAD_DIM), BF16),
            ((z.rows, features), BF16),
            ((z.rows, 2 * units), F32),
        ]
        + shapes(beside),
        [table, dma, dma((len(beside),))],
        after=blocks[-1:],
    )
    blocks = blocks[len(z.blocks_of[0]) :] + fetched
    fetched = call(
        functools.partial(fetch_kernel, z, between, [], 0),
        "fetch_between",
        weights,
        shapes(between),
        [dma((len(between),))],
        cost=traffic(between),
        after=[sent],
    )
    blocks += fetched
    from_core = swap(sent, "tok", toks, 1)
    totals = [
        call(
            functools.partial(add_kernel, z),
            "chip_sum_first",
            [(kept, VMEM), (from_core, VMEM)],
            [((z.rows, z.tail + HEAD_DIM), BF16)],
            after=fetched[-1:],
        )
    ]
    for q, jobs in enumerate(lasts, 1):
        size = 2 * z.parts[q][1]
        place = sum(len(some) for some in z.blocks_of[1:q])
        sent, kept, *fetched = call(
            functools.partial(next_project_kernel, z, q, jobs),
            "project_next",
            weights
            + [(a, VMEM) for a in [source, extra] + blocks[place : place + len(z.blocks_of[q])]],
            [((z.rows, size), BF16)] * 2 + shapes(jobs),
            [dma((len(jobs),))],
            cost=pl.CostEstimate(
                flops=4 * z.rows * features * size,
                bytes_accessed=4 * features * size,
                transcendentals=0,
            ),
            after=totals[0],
        )
        blocks += fetched
        other = swap(sent, "tok", toks, 1)
        totals.append(
            call(
                functools.partial(add_kernel, z),
                "chip_sum_next",
                [(kept, VMEM), (other, VMEM)],
                [((z.rows, size), BF16)],
            )
        )
    parts = [
        total + [swap(total[0], "tok", toks, 2 * s) for s in range(1, chips)]
        for total in totals
    ]
    down_delta, *fetched = call(
        functools.partial(fetch_kernel, z, final, [down_delta], 0),
        "fetch_down",
        weights + [(down_delta, HBM)],
        [(down_delta.shape, BF16)] + shapes(final),
        [dma((len(final) + 1,))],
        cost=traffic(final),
        after=totals[-1],
    )
    blocks += fetched
    down_blocks = blocks[used - len(z.blocks_of[0]) :]
    (hidden,) = call(
        functools.partial(hidden_kernel, z, width),
        "hidden",
        [(a, VMEM) for part in parts for a in part],
        [((z.rows, units // 2), BF16)],
        after=fetched[-1:],
    )
    half = len(z.downs) // 2
    before, *fetched = call(
        functools.partial(down_mine_kernel, z, ending),
        "down_mine",
        weights + [(a, VMEM) for a in [hidden] + down_blocks[:half]],
        [((z.rows, out_width), F32)] + shapes(ending),
        [dma((max(1, len(ending)),))],
        cost=pl.CostEstimate(
            flops=z.rows * units * out_width, bytes_accessed=units * out_width, transcendentals=0
        ),
    )
    down_blocks += fetched
    parts = call(
        functools.partial(down_kernel, z),
        "down",
        [(tile_index, HBM)]
        + [(a, VMEM) for a in [down_delta, before, hidden, swap(hidden, "tok", toks, 1), from_core]]
        + [(a, VMEM) for a in back[2::2] + down_blocks[half:]],
        [((2 * z.lane_slots, out_width // 2), BF16)] * cols
        + [((back_rows, 2 * HEAD_DIM), BF16)] * (chips - 1),
        [
            pltpu.VMEM((z.rows, units), BF16),
            pltpu.VMEM((z.rows, out_width), F32),
            pltpu.VMEM((2 * z.lane_slots, out_width // 2), F32),
            table,
            dma,
        ],
    )
    parts, across = parts[:cols], parts[cols:]
    parts = [parts[0]] + [swap(parts[s], "col", cols, s) for s in range(1, cols)]
    across = [swap(rows, "tok", toks, 2 * s + 2) for s, rows in enumerate(across)]
    attended, ffn_out = call(
        functools.partial(finish_kernel, z),
        "finish",
        [(a, VMEM) for a in [back[0], from_core] + across + parts[::-1]],
        [((cap, width), BF16), ((z.lane_slots, out_width), BF16)],
        [
            pltpu.VMEM((cap, width), BF16),
            pltpu.VMEM((z.lane_slots, out_width), BF16),
            pltpu.VMEM((toks, back_rows, HEAD_DIM), F32),
            dma((2,)),
        ],
        out=HBM,
    )
    return attended, ffn_out


def solution(mesh):
    in_specs = (
        P(("rep", "tok", "col"), None),
        P(("rep", "tok", "col"), None, None),
        P("rep", "col", None),
        P("rep", "col"),
        P(),
        P("tok", "col"),
        P("tok", "col"),
        P("col", "tok"),
        P("tok", "col", None, None, None),
        P("tok", "col", None, None, None),
        P("tok", "col", None, None, None),
        P("tok", "col", None, None, None),
    )
    out_specs = (P(("rep", "tok", "col"), None), P(("rep", "col"), "tok"))
    return jax.shard_map(local, mesh=mesh, in_specs=in_specs, out_specs=out_specs, check_vma=False)
```

```python
import functools

import jax
import jax.numpy as jnp
from jax import lax
from jax.experimental import pallas as pl
from jax.experimental.pallas import tpu as pltpu
from jax.sharding import PartitionSpec as P

HEADS = 64
KV_HEADS = 8
HEAD_DIM = 128
GROUP = HEADS // KV_HEADS
MIB = 1 << 20
FETCH = (3, 1, 4)
BF16 = jnp.bfloat16
F32 = jnp.float32
VMEM = pltpu.VMEM
HBM = pltpu.HBM


def call(kernel, name, ins, outs, scratch=(), limit=8, cost=None, after=(), out=VMEM):
    if cost is None:
        cost = pl.CostEstimate(flops=0, bytes_accessed=1024, transcendentals=0)
    count = len(ins)
    ins = ins + [(a, VMEM) for a in after]

    def body(*refs):
        kernel(*refs[:count], *refs[count + len(after) :])

    return list(
        pl.pallas_call(
            body,
            name=name,
            in_specs=[pl.BlockSpec(memory_space=s) for _, s in ins],
            out_specs=[pl.BlockSpec(memory_space=out) for _ in outs],
            out_shape=[out(shape, dtype) for shape, dtype in outs],
            scratch_shapes=list(scratch),
            cost_estimate=cost,
            compiler_params=pltpu.CompilerParams(vmem_limit_bytes=limit * MIB),
        )(*[pltpu.with_memory_space_constraint(a, space) for a, space in ins])
    )


class Sizes:
    def __init__(self, toks, cols, cap, units):
        self.toks, self.cols, self.cap = toks, cols, cap
        half = units // 2
        self.ups = [(0, half // 2), (half // 2, half // 2)]
        self.tail = half
        self.step = min(512, half // 4)
        self.jobs = [(keep, at) for keep in (False, True) for at in range(0, half, half // 4)]
        self.heads = HEADS // toks
        self.kvs = max(1, self.heads // GROUP)
        self.group = self.heads // self.kvs
        self.lane_slots = toks * cap
        self.rows = toks * cols * cap
        self.req_rows = -(-(self.heads + 2 * self.kvs) // 16) * 16
        self.blocks = 2 * self.kvs
        self.pieces = 2 * self.req_rows // 16

    def first_kv(self, tok):
        return tok * self.heads // GROUP


def pack_kernel(z, ctx, req_ref, cache_ref, *rest):
    outs, (narrow, wide, rows, req_sem, sems) = rest[: z.toks], rest[z.toks :]
    tok = lax.axis_index("tok")
    width = z.kvs * HEAD_DIM
    pairs = KV_HEADS * HEAD_DIM
    fetch = pltpu.make_async_copy(req_ref, narrow, req_sem)
    fetch.start()
    copies = []
    for s in reversed(range(z.toks)):
        first = pl.multiple_of(z.first_kv(tok ^ s) * HEAD_DIM, HEAD_DIM)
        for half in range(2):
            copy = pltpu.make_async_copy(
                cache_ref.at[:, :, pl.ds(half * pairs + first, width)],
                outs[s].at[: z.cap, :, pl.ds(half * width, width)],
                sems.at[s, half],
            )
            copy.start()
            copies.append(copy)
    fetch.wait()

    @after_starts
    def _():
        rows[...] = jnp.zeros_like(rows)
        wide[...] = narrow[...].astype(F32)
        for s in range(z.toks):
            to = tok ^ s
            starts = [(to * z.heads + h) * HEAD_DIM for h in range(z.heads)]
            for half in range(2):
                starts += [
                    HEADS * HEAD_DIM + half * pairs + (z.first_kv(to) + j) * HEAD_DIM
                    for j in range(z.kvs)
                ]
            for r in range(2):
                for n, start in enumerate(starts):
                    at = r * z.req_rows + n
                    rows[s, at : at + 1, :] = wide[
                        r : r + 1, pl.ds(pl.multiple_of(start, HEAD_DIM), HEAD_DIM)
                    ]
            for p in range(z.pieces):
                at, lane = z.cap + p // z.blocks, p % z.blocks * HEAD_DIM
                outs[s][at, :, lane : lane + HEAD_DIM] = rows[s, p * 16 : p * 16 + 16, :].astype(BF16)

    for copy in copies:
        copy.wait()


def start_copies(pairs, sems):
    copies = [pltpu.make_async_copy(src, dst, sems.at[n]) for n, (src, dst) in enumerate(pairs)]
    for copy in copies:
        copy.start()
    return copies


def after_starts(compute):
    pl.when(lax.axis_index("tok") >= 0)(compute)


def weight_blocks(jobs, gate_ref):
    core = lax.axis_index("tok") % 2
    half = gate_ref.shape[1] // 2
    found = []
    for keep, first in jobs:
        at = pl.multiple_of((core if keep else 1 - core) * half, half)
        found.append(gate_ref.at[:, pl.ds(at + first, half // 4)])
    return found


def fetch_kernel(jobs, whole, gain_size, gate_ref, *rest):
    sources, rest = list(rest[: len(whole)]), rest[len(whole) :]
    outs, sems = rest[:-1], rest[-1]
    if gain_size:
        tok = lax.axis_index("tok")
        at = pl.multiple_of(tok * gain_size, gain_size)
        sources[0] = sources[0].at[:, pl.ds(at, gain_size)]
    sources += weight_blocks(jobs, gate_ref)
    for copy in start_copies(list(zip(sources, outs)), sems):
        copy.wait()


def attend_kernel(z, ctx, jobs, list_hbm, count_hbm, *rest):
    gate_ref, pieces, rest = rest[0], rest[1 : 1 + z.toks], rest[1 + z.toks :]
    pieces = pieces[:1] + pieces[-1:] + pieces[1:-1]
    send_ref, back_refs, rest = rest[0], rest[1 : 1 + z.toks], rest[1 + z.toks :]
    blocks, rest = rest[: len(jobs)], rest[len(jobs) :]
    cache, req, query, own_key, own_value, alive, mixed_all, list_ref, count_ref, table_sems, sems = rest
    tables = start_copies([(list_hbm, list_ref), (count_hbm, count_ref)], table_sems)
    copies = start_copies(list(zip(weight_blocks(jobs, gate_ref), blocks)), sems)

    @after_starts
    def _():
        tok = lax.axis_index("tok")
        cache_rows = z.cap * ctx
        for s in range(z.toks):
            source = tok ^ s
            cache[source] = pieces[s][: z.cap].reshape(cache_rows, cache.shape[2])
            for p in range(z.pieces):
                at, lane = z.cap + p // z.blocks, p % z.blocks * HEAD_DIM
                r, part = p * 16 // z.req_rows, p * 16 % z.req_rows
                req[source * 2 + r, part : part + 16, :] = pieces[s][
                    at, :, lane : lane + HEAD_DIM
                ].astype(F32)
        for table in tables:
            table.wait()
        for g in range(z.toks):
            for k in range(z.cap):
                live = (k < count_ref[0, g]).astype(F32)
                rows = req[list_ref[k, 0, g]] * live
                at = (g * z.cap + k) * z.group
                for j in range(z.kvs):
                    query[j, at : at + z.group, :] = rows[j * z.group : (j + 1) * z.group, :]
                    key, value = z.heads + j, z.heads + z.kvs + j
                    own_key[j, at : at + z.group, :] = jnp.broadcast_to(
                        rows[key : key + 1, :], (z.group, HEAD_DIM)
                    )
                    own_value[j, at : at + z.group, :] = jnp.broadcast_to(
                        rows[value : value + 1, :], (z.group, HEAD_DIM)
                    )
                alive[at : at + z.group, :] = jnp.full((z.group, HEAD_DIM), live, F32)
        many, keys = z.lane_slots * z.group, z.toks * cache_rows
        row_slot = lax.broadcasted_iota(jnp.int32, (many, keys), 0) // z.group
        key_slot = lax.broadcasted_iota(jnp.int32, (many, keys), 1) // ctx
        same = row_slot == key_slot
        scale = HEAD_DIM ** (-0.5)
        for j in range(z.kvs):
            cached_keys = cache[:, :, j * HEAD_DIM : (j + 1) * HEAD_DIM].reshape(keys, HEAD_DIM)
            at = (z.kvs + j) * HEAD_DIM
            cached_values = cache[:, :, at : at + HEAD_DIM].reshape(keys, HEAD_DIM)
            past = (
                lax.dot_general(
                    query[j].astype(BF16),
                    cached_keys,
                    (((1,), (1,)), ((), ())),
                    preferred_element_type=F32,
                )
                * scale
            )
            own = jnp.sum(query[j] * own_key[j], axis=-1, keepdims=True) * scale
            top = jnp.maximum(jnp.max(jnp.where(same, past, -jnp.inf), axis=-1, keepdims=True), own)
            past_exp = jnp.where(same, jnp.exp(jnp.where(same, past - top, 0.0)), 0.0)
            own_exp = jnp.exp(own - top)
            total = jnp.sum(past_exp, axis=-1, keepdims=True) + own_exp
            weights = (past_exp / total).astype(BF16)
            own_weight = (own_exp / total).astype(BF16).astype(F32)
            mixed = jnp.dot(weights, cached_values, preferred_element_type=F32)
            mixed = (mixed + own_weight * own_value[j]) * alive[...]
            mixed_all[j * many : (j + 1) * many, :] = mixed.astype(BF16).astype(F32)
        block = z.cap * z.group
        for s in range(z.toks):
            for j in range(z.kvs):
                at = pl.multiple_of(j * many + (tok ^ s) * block, block if block % 8 == 0 else 4)
                back_refs[s][j * block : (j + 1) * block, :] = mixed_all[pl.ds(at, block), :].astype(BF16)
        count = z.kvs * z.lane_slots
        for h in range(z.group):
            send_ref[:, h * HEAD_DIM : (h + 1) * HEAD_DIM] = mixed_all[
                pl.ds(h, count, stride=z.group), :
            ].astype(BF16)

    for copy in copies:
        copy.wait()


def halves(value):
    high = value.astype(BF16).astype(F32)
    return high, value - high


def two_lanes(high, low, rows):
    lane = lax.broadcasted_iota(jnp.int32, (rows, HEAD_DIM), 1)
    return jnp.where(lane == 0, high, jnp.where(lane == 1, low, 0.0)).astype(BF16)


def slot_of_row(z, col, shape):
    row = lax.broadcasted_iota(jnp.int32, shape, 0)
    return ((row // z.lane_slots) ^ col) * z.lane_slots + row % z.lane_slots


def tile_terms(z, source, delta_ref, index_ref, matrix, extra, out_base):
    side = delta_ref.shape[-1]
    col = lax.axis_index("col")
    variant = slot_of_row(z, col, (z.rows, side)) // (2 * z.cols * z.cap)
    for n in range(delta_ref.shape[2]):
        at = pl.multiple_of(index_ref[0, matrix, 1, 0, n] * side, side)
        to = pl.multiple_of(out_base + index_ref[0, matrix, 2, 0, n] * side, side)
        rows = jnp.where(variant == index_ref[0, matrix, 0, 0, n], source[:, pl.ds(at, side)], 0)
        extra[:, pl.ds(to, side)] += jnp.dot(
            rows.astype(BF16), delta_ref[0, 0, n], preferred_element_type=F32
        )


def first_project_kernel(z, index_hbm, gain_ref, delta_ref, *rest):
    pieces, rest = rest[: z.cols], rest[z.cols :]
    odd_backs, rest = rest[: z.toks // 2], rest[z.toks // 2 :]
    blocks, rest = rest[: len(z.jobs)], rest[len(z.jobs) :]
    send_ref, keep_ref, source, extra, index_ref, index_sem = rest
    table = pltpu.make_async_copy(index_hbm, index_ref, index_sem)
    table.start()

    @after_starts
    def _():
        gather_rows(z, pieces, gain_ref, odd_backs, source, extra, send_ref, keep_ref)

    table.wait()
    tile_terms(z, source, delta_ref, index_ref, 0, extra, 0)
    core = lax.axis_index("tok") % 2
    half = z.tail
    for (keep, first), block in zip(z.jobs, blocks):
        out_ref, side = (keep_ref, core) if keep else (send_ref, 1 - core)
        for p in range(0, half // 4, z.step):
            at = pl.multiple_of(side * half + first + p, HEAD_DIM)
            value = jnp.dot(source[...], block[:, p : p + z.step], preferred_element_type=F32)
            value += extra[:, pl.ds(at, z.step)]
            out_ref[:, first + p : first + p + z.step] = value.astype(BF16)


def up_kernel(z, part, source, extra, up_ref, send_ref, keep_ref):
    core = lax.axis_index("tok") % 2
    first, size = part
    for out_ref, side in ((send_ref, 1 - core), (keep_ref, core)):
        for p in range(0, size, z.step):
            lanes = pl.ds(pl.multiple_of(side * z.tail + first + p, HEAD_DIM), z.step)
            value = jnp.dot(source[...], up_ref[:, lanes], preferred_element_type=F32)
            out_ref[:, p : p + z.step] = (value + extra[:, lanes]).astype(BF16)


def up_tiles_kernel(z, index_hbm, delta_ref, source, extra, index_ref, index_sem):
    table = pltpu.make_async_copy(index_hbm, index_ref, index_sem)
    table.start()
    extra[...] = jnp.zeros_like(extra)
    table.wait()
    tile_terms(z, source, delta_ref, index_ref, 1, extra, 0)


def gather_rows(z, pieces, gain_ref, odd_backs, source, extra, send_ref, keep_ref):
    col = lax.axis_index("col")
    extra[...] = jnp.zeros_like(extra)
    count = z.kvs * z.lane_slots
    wide = z.group * HEAD_DIM
    slot = slot_of_row(z, col, (z.rows, count))
    lane_of, owner = slot // z.cap % z.cols, slot // (z.cols * z.cap)
    column = lax.broadcasted_iota(jnp.int32, (z.rows, count), 1)
    squares = jnp.zeros((z.rows, 1), F32)
    for j in range(z.kvs):
        place = j * z.lane_slots + owner * z.cap + slot % z.cap
        found = jnp.zeros((z.rows, wide), F32)
        for s in range(z.cols):
            pick = ((lane_of == (col ^ s)) & (column == place)).astype(F32).astype(BF16)
            found += jnp.dot(pick, pieces[s][...], preferred_element_type=F32)
        squares += jnp.sum(found * found, axis=-1, keepdims=True)
        lanes = slice(j * wide, (j + 1) * wide)
        source[:, lanes] = (found * gain_ref[:, lanes]).astype(BF16)
    tail = z.tail
    for ref in (send_ref, keep_ref):
        ref[:, tail : tail + HEAD_DIM] = two_lanes(*halves(squares), z.rows)
    send_ref[:, tail + HEAD_DIM :] = jnp.zeros((z.rows, z.toks // 2 * HEAD_DIM), BF16)
    for n, ref in enumerate(odd_backs):
        lane = tail + (n + 1) * HEAD_DIM
        send_ref[: ref.shape[0], lane : lane + HEAD_DIM] = ref[...]


def add_kernel(z, mine, other, out_ref):
    size = mine.shape[1] // (2 * HEAD_DIM) * (2 * HEAD_DIM)
    out_ref[:, :size] = (mine[:, :size].astype(F32) + other[:, :size].astype(F32)).astype(BF16)
    if mine.shape[1] > size:
        lanes = slice(size, size + HEAD_DIM)
        total = mine[:, lanes].astype(F32) + other[:, lanes].astype(F32)
        out_ref[:, lanes] = two_lanes(*halves(jnp.sum(total, axis=-1, keepdims=True)), z.rows)


def hidden_kernel(z, width, *refs):
    chips = z.toks // 2
    gates, out_ref = refs[:chips], refs[-1]
    squares = sum(ref[:, z.tail : z.tail + HEAD_DIM].astype(F32) for ref in gates)
    squares = jnp.sum(squares, axis=-1, keepdims=True)
    scale = lax.rsqrt(squares * (1.0 / width) + 1e-06)
    for q, (first, size) in enumerate(z.ups):
        ups = refs[(q + 1) * chips : (q + 2) * chips]
        step = min(size, 256)
        for at in range(0, size, step):
            lanes = slice(first + at, first + at + step)
            gate = sum(ref[:, lanes].astype(F32) for ref in gates) * scale
            up = sum(ref[:, at : at + step].astype(F32) for ref in ups) * scale
            out_ref[:, lanes] = (jax.nn.silu(gate) * up).astype(BF16)


def down_products(mine, units_ref, weight_ref, total, before=None):
    core = lax.axis_index("tok") % 2
    half, width = units_ref.shape[1], total.shape[1]
    at = pl.multiple_of((core if mine else 1 - core) * half, half)
    step = min(width, 512)
    for to in range(0, width, step):
        lanes = slice(to, to + step)
        value = jnp.dot(
            units_ref[...], weight_ref[pl.ds(at, half), lanes], preferred_element_type=F32
        )
        total[:, lanes] = value if before is None else value + before[:, lanes]


def down_mine_kernel(mine, weight, total):
    down_products(True, mine, weight, total)


def down_kernel(z, index_hbm, delta_ref, before, mine, other, from_core, *rest):
    others = z.toks // 2 - 1
    evens, rest = rest[:others], rest[others:]
    weight, rest = rest[0], rest[1:]
    outs, backs, rest = rest[: z.cols], rest[z.cols : z.cols + others], rest[z.cols + others :]
    source, total, fold, index_ref, index_sem = rest
    table = pltpu.make_async_copy(index_hbm, index_ref, index_sem)
    table.start()

    @after_starts
    def _():
        core = lax.axis_index("tok") % 2
        half = mine.shape[1]
        source[:, pl.ds(pl.multiple_of(core * half, half), half)] = mine[...]
        source[:, pl.ds(pl.multiple_of((1 - core) * half, half), half)] = other[...]
        down_products(False, other, weight, total, before)

    for s, back in enumerate(backs):
        back[:, :HEAD_DIM] = evens[s][...]
        lane = z.tail + (s + 2) * HEAD_DIM
        back[:, HEAD_DIM:] = from_core[: back.shape[0], lane : lane + HEAD_DIM]
    table.wait()
    tile_terms(z, source, delta_ref, index_ref, 2, total, 0)
    width = total.shape[1]
    for s in range(z.cols):
        rows = slice(s * z.lane_slots, (s + 1) * z.lane_slots)
        fold[: z.lane_slots, :] = total[rows, : width // 2]
        fold[z.lane_slots :, :] = total[rows, width // 2 :]
        outs[s][...] = fold[...].astype(BF16)


def finish_kernel(z, own, from_core, *refs):
    others = z.toks // 2 - 1
    across, parts, rest = refs[:others], refs[others : others + z.cols], refs[others + z.cols :]
    attended_hbm, out_hbm, attended, out, rows, sems = rest
    tok = lax.axis_index("tok")
    block = z.cap * z.group
    count = z.kvs * block
    tail = z.tail + HEAD_DIM
    for s in range(z.toks):
        if s == 0:
            rows[s] = own[...].astype(F32)
        elif s == 1:
            rows[s] = from_core[:count, tail : tail + HEAD_DIM].astype(F32)
        else:
            lane = s % 2 * HEAD_DIM
            rows[s] = across[s // 2 - 1][:, lane : lane + HEAD_DIM].astype(F32)
        first = pl.multiple_of((tok ^ s) * z.heads * HEAD_DIM, HEAD_DIM)
        for j in range(z.kvs):
            for h in range(z.group):
                to = first + (j * z.group + h) * HEAD_DIM
                attended[:, pl.ds(to, HEAD_DIM)] = rows[
                    s, pl.ds(j * block + h, z.cap, stride=z.group), :
                ].astype(BF16)
    copies = start_copies([(attended, attended_hbm)], sems)

    @after_starts
    def _():
        total = sum(ref[...].astype(F32) for ref in parts)
        half = total.shape[1]
        out[:, :half] = total[: z.lane_slots].astype(BF16)
        out[:, half:] = total[z.lane_slots :].astype(BF16)

    copy = pltpu.make_async_copy(out, out_hbm, sems.at[1])
    copy.start()
    for copy in copies + [copy]:
        copy.wait()


def swap(array, axis, size, distance):
    return lax.ppermute(array, axis, [(i, i ^ distance) for i in range(size)])


def local(
    request_rows,
    key_cache,
    route_list,
    route_count,
    norm_gain,
    gate_weight,
    up_weight,
    down_weight,
    gate_delta,
    up_delta,
    down_delta,
    tile_index,
):
    toks, cols = lax.axis_size("tok"), lax.axis_size("col")
    cap, ctx = key_cache.shape[0], key_cache.shape[1]
    features, units = gate_weight.shape
    z = Sizes(toks, cols, cap, units)
    width = norm_gain.shape[0]
    cache_rows = cap * ctx
    lanes = 2 * z.kvs * HEAD_DIM
    piece_shape = (cap + -(-z.pieces // z.blocks), ctx, lanes)
    many = z.lane_slots * z.group
    chips = toks // 2
    gain = norm_gain.reshape(1, width)
    route_list = route_list.transpose(2, 1, 0)
    route_count = route_count.transpose(1, 0)
    tile_index = tile_index.transpose(0, 2, 4, 1, 3)
    dma = pltpu.SemaphoreType.DMA

    cuts = [0]
    for count in FETCH:
        cuts.append(cuts[-1] + count)
    early, middle, late = [z.jobs[a:b] for a, b in zip(cuts, cuts[1:])]

    def shapes(some):
        return [((features, units // 8), BF16) for _ in some]

    def traffic(some):
        moved = sum(a * b * 2 for (a, b), _ in shapes(some))
        return pl.CostEstimate(flops=0, bytes_accessed=moved, transcendentals=0)

    def product(share):
        return pl.CostEstimate(
            flops=int(2 * z.rows * features * units * share),
            bytes_accessed=int(2 * features * units * share),
            transcendentals=0,
        )

    pieces = call(
        functools.partial(pack_kernel, z, ctx),
        "pack",
        [(request_rows, HBM), (key_cache, HBM)],
        [(piece_shape, BF16)] * toks,
        [
            pltpu.VMEM(request_rows.shape, BF16),
            pltpu.VMEM(request_rows.shape, F32),
            pltpu.VMEM((toks, 2 * z.req_rows, HEAD_DIM), F32),
            dma,
            dma((toks, 2)),
        ],
    )
    whole = [gain, gate_delta, up_delta]
    gain, gate_delta, up_delta, *blocks = call(
        functools.partial(fetch_kernel, early, whole, features),
        "fetch_early",
        [(a, HBM) for a in [gate_weight] + whole],
        [((1, features), F32), (gate_delta.shape, BF16), (up_delta.shape, BF16)]
        + shapes(early),
        [dma((len(early) + 3,))],
        after=pieces[:1],
        cost=traffic(early),
    )
    pieces = [pieces[0]] + [swap(pieces[s], "tok", toks, s) for s in range(1, toks)]
    back_rows = z.kvs * cap * z.group
    send, *rest = call(
        functools.partial(attend_kernel, z, ctx, middle),
        "attend",
        [(a, HBM) for a in [route_list, route_count, gate_weight]] + [(p, VMEM) for p in pieces[:1] + pieces[2:] + pieces[1:2]],
        [((z.kvs * z.lane_slots, z.group * HEAD_DIM), BF16)]
        + [((back_rows, HEAD_DIM), BF16)] * toks
        + shapes(middle),
        [
            pltpu.VMEM((toks, cache_rows, lanes), BF16),
            pltpu.VMEM((2 * toks, z.req_rows, HEAD_DIM), F32),
            pltpu.VMEM((z.kvs, many, HEAD_DIM), F32),
            pltpu.VMEM((z.kvs, many, HEAD_DIM), F32),
            pltpu.VMEM((z.kvs, many, HEAD_DIM), F32),
            pltpu.VMEM((many, HEAD_DIM), F32),
            pltpu.VMEM((z.kvs * many, HEAD_DIM), F32),
            pltpu.SMEM(route_list.shape, jnp.int32),
            pltpu.SMEM(route_count.shape, jnp.int32),
            dma((2,)),
            dma((max(1, len(middle)),)),
        ],
        after=[gain],
    )
    back = rest[:toks]
    blocks += rest[toks:]
    blocks += call(
        functools.partial(fetch_kernel, late, [], 0),
        "fetch_late",
        [(gate_weight, HBM)],
        shapes(late),
        [dma((len(late),))],
        after=[send],
        cost=traffic(late),
    )
    pieces = [send] + [swap(send, "col", cols, s) for s in range(1, cols)]
    out_width = down_weight.shape[1]
    table = pltpu.SMEM(tile_index.shape, jnp.int32)
    sent, kept, source = call(
        functools.partial(first_project_kernel, z),
        "gate",
        [(tile_index, HBM), (gain, VMEM), (gate_delta, VMEM)]
        + [(p, VMEM) for p in pieces + back[1::2] + blocks],
        [
            ((z.rows, z.tail + (1 + chips) * HEAD_DIM), BF16),
            ((z.rows, z.tail + HEAD_DIM), BF16),
            ((z.rows, features), BF16),
        ],
        [pltpu.VMEM((z.rows, units), F32), table, dma],
        cost=product(1),
    )
    from_core = swap(sent, "tok", toks, 1)
    (extra,) = call(
        functools.partial(up_tiles_kernel, z),
        "up_tiles",
        [(tile_index, HBM), (up_delta, VMEM), (source, VMEM)],
        [((z.rows, units), F32)],
        [table, dma],
        cost=product(1 / 8),
    )
    totals = [
        call(
            functools.partial(add_kernel, z),
            "chip_sum_first",
            [(kept, VMEM), (from_core, VMEM)],
            [((z.rows, z.tail + HEAD_DIM), BF16)],
            after=[extra],
        )
    ]
    for part in z.ups:
        size = part[1]
        sent, kept = call(
            functools.partial(up_kernel, z, part),
            "up",
            [(a, VMEM) for a in [source, extra, up_weight]],
            [((z.rows, size), BF16)] * 2,
            cost=product(size / units * 2),
            after=totals[0],
        )
        totals.append(
            call(
                functools.partial(add_kernel, z),
                "chip_sum_next",
                [(kept, VMEM), (swap(sent, "tok", toks, 1), VMEM)],
                [((z.rows, size), BF16)],
            )
        )
    parts = [
        total + [swap(total[0], "tok", toks, 2 * s) for s in range(1, chips)]
        for total in totals
    ]
    (hidden,) = call(
        functools.partial(hidden_kernel, z, width),
        "hidden",
        [(a, VMEM) for part in parts for a in part],
        [((z.rows, units // 2), BF16)],
    )
    (before,) = call(
        down_mine_kernel,
        "down_mine",
        [(hidden, VMEM), (down_weight, VMEM)],
        [((z.rows, out_width), F32)],
        cost=pl.CostEstimate(
            flops=z.rows * units * out_width, bytes_accessed=units * out_width, transcendentals=0
        ),
    )
    parts = call(
        functools.partial(down_kernel, z),
        "down",
        [(tile_index, HBM)]
        + [(a, VMEM) for a in [down_delta, before, hidden, swap(hidden, "tok", toks, 1), from_core]]
        + [(a, VMEM) for a in back[2::2] + [down_weight]],
        [((2 * z.lane_slots, out_width // 2), BF16)] * cols
        + [((back_rows, 2 * HEAD_DIM), BF16)] * (chips - 1),
        [
            pltpu.VMEM((z.rows, units), BF16),
            pltpu.VMEM((z.rows, out_width), F32),
            pltpu.VMEM((2 * z.lane_slots, out_width // 2), F32),
            table,
            dma,
        ],
    )
    parts, across = parts[:cols], parts[cols:]
    parts = [parts[0]] + [swap(parts[s], "col", cols, s) for s in range(1, cols)]
    across = [swap(rows, "tok", toks, 2 * s + 2) for s, rows in enumerate(across)]
    attended, ffn_out = call(
        functools.partial(finish_kernel, z),
        "finish",
        [(a, VMEM) for a in [back[0], from_core] + across + parts[::-1]],
        [((cap, width), BF16), ((z.lane_slots, out_width), BF16)],
        [
            pltpu.VMEM((cap, width), BF16),
            pltpu.VMEM((z.lane_slots, out_width), BF16),
            pltpu.VMEM((toks, back_rows, HEAD_DIM), F32),
            dma((2,)),
        ],
        out=HBM,
    )
    return attended, ffn_out


def solution(mesh):
    in_specs = (
        P(("rep", "tok", "col"), None),
        P(("rep", "tok", "col"), None, None),
        P("rep", "col", None),
        P("rep", "col"),
        P(),
        P("tok", "col"),
        P("tok", "col"),
        P("col", "tok"),
        P("tok", "col", None, None, None),
        P("tok", "col", None, None, None),
        P("tok", "col", None, None, None),
        P("tok", "col", None, None, None),
    )
    out_specs = (P(("rep", "tok", "col"), None), P(("rep", "col"), "tok"))
    return jax.shard_map(local, mesh=mesh, in_specs=in_specs, out_specs=out_specs, check_vma=False)
```

```python
import functools

import jax
import jax.numpy as jnp
from jax import lax
from jax.experimental import pallas as pl
from jax.experimental.pallas import tpu as pltpu
from jax.sharding import PartitionSpec as P

HEADS = 64
KV_HEADS = 8
HEAD_DIM = 128
GROUP = HEADS // KV_HEADS
MIB = 1 << 20
FETCH = (1, 1, 6)
BF16 = jnp.bfloat16
F32 = jnp.float32
VMEM = pltpu.VMEM
HBM = pltpu.HBM


def call(kernel, name, ins, outs, scratch=(), limit=8, cost=None, after=(), out=VMEM):
    if cost is None:
        cost = pl.CostEstimate(flops=0, bytes_accessed=1024, transcendentals=0)
    count = len(ins)
    ins = ins + [(a, VMEM) for a in after]

    def body(*refs):
        kernel(*refs[:count], *refs[count + len(after) :])

    return list(
        pl.pallas_call(
            body,
            name=name,
            in_specs=[pl.BlockSpec(memory_space=s) for _, s in ins],
            out_specs=[pl.BlockSpec(memory_space=out) for _ in outs],
            out_shape=[out(shape, dtype) for shape, dtype in outs],
            scratch_shapes=list(scratch),
            cost_estimate=cost,
            compiler_params=pltpu.CompilerParams(vmem_limit_bytes=limit * MIB),
        )(*[pltpu.with_memory_space_constraint(a, space) for a, space in ins])
    )


class Sizes:
    def __init__(self, toks, cols, cap, units):
        self.toks, self.cols, self.cap = toks, cols, cap
        half = units // 2
        self.ups = [(0, half // 2), (half // 2, half // 2)]
        self.tail = half
        self.step = min(512, half // 4)
        self.jobs = [(mine, at) for mine in (True, False) for at in range(0, half, half // 4)]
        self.heads = HEADS // toks
        self.kvs = max(1, self.heads // GROUP)
        self.group = self.heads // self.kvs
        self.lane_slots = toks * cap
        self.rows = toks * cols * cap
        self.req_rows = -(-(self.heads + 2 * self.kvs) // 16) * 16
        self.blocks = 2 * self.kvs
        self.pieces = 2 * self.req_rows // 16

    def first_kv(self, tok):
        return tok * self.heads // GROUP


def pack_kernel(z, ctx, req_ref, cache_ref, *rest):
    outs, (narrow, wide, rows, req_sem, sems) = rest[: z.toks], rest[z.toks :]
    tok = lax.axis_index("tok")
    width = z.kvs * HEAD_DIM
    pairs = KV_HEADS * HEAD_DIM
    fetch = pltpu.make_async_copy(req_ref, narrow, req_sem)
    fetch.start()
    copies = []
    for s in reversed(range(z.toks)):
        first = pl.multiple_of(z.first_kv(tok ^ s) * HEAD_DIM, HEAD_DIM)
        for half in range(2):
            copy = pltpu.make_async_copy(
                cache_ref.at[:, :, pl.ds(half * pairs + first, width)],
                outs[s].at[: z.cap, :, pl.ds(half * width, width)],
                sems.at[s, half],
            )
            copy.start()
            copies.append(copy)
    fetch.wait()

    @after_starts
    def _():
        rows[...] = jnp.zeros_like(rows)
        wide[...] = narrow[...].astype(F32)
        for s in range(z.toks):
            to = tok ^ s
            starts = [(to * z.heads + h) * HEAD_DIM for h in range(z.heads)]
            for half in range(2):
                starts += [
                    HEADS * HEAD_DIM + half * pairs + (z.first_kv(to) + j) * HEAD_DIM
                    for j in range(z.kvs)
                ]
            for r in range(2):
                for n, start in enumerate(starts):
                    at = r * z.req_rows + n
                    rows[s, at : at + 1, :] = wide[
                        r : r + 1, pl.ds(pl.multiple_of(start, HEAD_DIM), HEAD_DIM)
                    ]
            for p in range(z.pieces):
                at, lane = z.cap + p // z.blocks, p % z.blocks * HEAD_DIM
                outs[s][at, :, lane : lane + HEAD_DIM] = rows[s, p * 16 : p * 16 + 16, :].astype(BF16)

    for copy in copies:
        copy.wait()


def start_copies(pairs, sems):
    copies = [pltpu.make_async_copy(src, dst, sems.at[n]) for n, (src, dst) in enumerate(pairs)]
    for copy in copies:
        copy.start()
    return copies


def after_starts(compute):
    pl.when(lax.axis_index("tok") >= 0)(compute)


def weight_blocks(jobs, down_ref):
    core = lax.axis_index("tok") % 2
    half = down_ref.shape[0] // 2
    found = []
    for mine, first in jobs:
        at = pl.multiple_of((core if mine else 1 - core) * half, half)
        found.append(down_ref.at[pl.ds(at + first, half // 4), :])
    return found


def fetch_kernel(jobs, down_ref, delta_hbm, *rest):
    outs, sems = rest[:-1], rest[-1]
    for copy in start_copies(list(zip([delta_hbm] + weight_blocks(jobs, down_ref), outs)), sems):
        copy.wait()


def first_fetch_kernel(z, list_hbm, count_hbm, gain_ref, gate_delta, up_delta, _, *rest):
    place_ref, *outs = rest[:-4]
    list_ref, count_ref, table_sems, sems = rest[-4:]
    tables = start_copies([(list_hbm, list_ref), (count_hbm, count_ref)], table_sems)
    features = outs[0].shape[1]
    at = pl.multiple_of(lax.axis_index("tok") * features, features)
    sources = [gain_ref.at[:, pl.ds(at, features)], gate_delta, up_delta]
    copies = start_copies(list(zip(sources, outs)), sems)
    for table in tables:
        table.wait()

    @after_starts
    def _():
        for g in range(z.toks):
            for k in range(z.cap):
                row = jnp.where(k < count_ref[0, g], list_ref[k, 0, g], -1)
                at = (g * z.cap + k) * z.group
                place_ref[at : at + z.group, :] = jnp.full((z.group, HEAD_DIM), row, jnp.int32)

    for copy in copies:
        copy.wait()


def attend_kernel(z, ctx, place_ref, _, *rest):
    pieces, rest = rest[: z.toks], rest[z.toks :]
    pieces = pieces[:1] + pieces[-1:] + pieces[1:-1]
    send_ref, back_refs, rest = rest[0], rest[1 : 1 + z.toks], rest[1 + z.toks :]
    cache, req, mixed_all = rest

    @after_starts
    def _():
        tok = lax.axis_index("tok")
        cache_rows = z.cap * ctx
        for s in range(z.toks):
            source = tok ^ s
            cache[source] = pieces[s][: z.cap].reshape(cache_rows, cache.shape[2])
            for p in range(z.pieces):
                at, lane = z.cap + p // z.blocks, p % z.blocks * HEAD_DIM
                r, part = p * 16 // z.req_rows, p * 16 % z.req_rows
                req[source * 2 + r, part : part + 16, :] = pieces[s][at, :, lane : lane + HEAD_DIM]
        many, keys = z.lane_slots * z.group, z.toks * cache_rows
        held = 2 * z.toks * z.req_rows
        requests = req[...].reshape(held, HEAD_DIM)
        first = place_ref[:, :1]
        alive = (first >= 0).astype(F32)
        first = first * z.req_rows
        head = lax.broadcasted_iota(jnp.int32, (many, 1), 0) % z.group
        column = lax.broadcasted_iota(jnp.int32, (many, held), 1)

        def rows_at(at):
            pick = (column == first + at).astype(F32).astype(BF16)
            return jnp.dot(pick, requests, preferred_element_type=F32)

        row_slot = lax.broadcasted_iota(jnp.int32, (many, keys), 0) // z.group
        key_slot = lax.broadcasted_iota(jnp.int32, (many, keys), 1) // ctx
        same = row_slot == key_slot
        scale = HEAD_DIM ** (-0.5)
        for j in range(z.kvs):
            cached_keys = cache[:, :, j * HEAD_DIM : (j + 1) * HEAD_DIM].reshape(keys, HEAD_DIM)
            at = (z.kvs + j) * HEAD_DIM
            cached_values = cache[:, :, at : at + HEAD_DIM].reshape(keys, HEAD_DIM)
            query = rows_at(head + j * z.group)
            own_key, own_value = rows_at(z.heads + j), rows_at(z.heads + z.kvs + j)
            past = (
                lax.dot_general(
                    query.astype(BF16),
                    cached_keys,
                    (((1,), (1,)), ((), ())),
                    preferred_element_type=F32,
                )
                * scale
            )
            own = jnp.sum(query * own_key, axis=-1, keepdims=True) * scale
            top = jnp.maximum(jnp.max(jnp.where(same, past, -jnp.inf), axis=-1, keepdims=True), own)
            past_exp = jnp.where(same, jnp.exp(jnp.where(same, past - top, 0.0)), 0.0)
            own_exp = jnp.exp(own - top)
            total = jnp.sum(past_exp, axis=-1, keepdims=True) + own_exp
            weights = (past_exp / total).astype(BF16)
            own_weight = (own_exp / total).astype(BF16).astype(F32)
            mixed = jnp.dot(weights, cached_values, preferred_element_type=F32)
            mixed = (mixed + own_weight * own_value) * alive
            mixed_all[j * many : (j + 1) * many, :] = mixed.astype(BF16).astype(F32)
        block = z.cap * z.group
        for s in range(z.toks):
            for j in range(z.kvs):
                at = pl.multiple_of(j * many + (tok ^ s) * block, block if block % 8 == 0 else 4)
                back_refs[s][j * block : (j + 1) * block, :] = mixed_all[pl.ds(at, block), :].astype(BF16)
        count = z.kvs * z.lane_slots
        for h in range(z.group):
            send_ref[:, h * HEAD_DIM : (h + 1) * HEAD_DIM] = mixed_all[
                pl.ds(h, count, stride=z.group), :
            ].astype(BF16)


def halves(value):
    high = value.astype(BF16).astype(F32)
    return high, value - high


def two_lanes(high, low, rows):
    lane = lax.broadcasted_iota(jnp.int32, (rows, HEAD_DIM), 1)
    return jnp.where(lane == 0, high, jnp.where(lane == 1, low, 0.0)).astype(BF16)


def slot_of_row(z, col, shape):
    row = lax.broadcasted_iota(jnp.int32, shape, 0)
    return ((row // z.lane_slots) ^ col) * z.lane_slots + row % z.lane_slots


def tile_terms(z, source, delta_ref, index_ref, matrix, extra, out_base):
    side = delta_ref.shape[-1]
    col = lax.axis_index("col")
    variant = slot_of_row(z, col, (z.rows, side)) // (2 * z.cols * z.cap)
    for n in range(delta_ref.shape[2]):
        at = pl.multiple_of(index_ref[0, matrix, 1, 0, n] * side, side)
        to = pl.multiple_of(out_base + index_ref[0, matrix, 2, 0, n] * side, side)
        rows = jnp.where(variant == index_ref[0, matrix, 0, 0, n], source[:, pl.ds(at, side)], 0)
        extra[:, pl.ds(to, side)] += jnp.dot(
            rows.astype(BF16), delta_ref[0, 0, n], preferred_element_type=F32
        )


def first_project_kernel(z, index_hbm, gain_ref, delta_ref, *rest):
    pieces, rest = rest[: z.cols], rest[z.cols :]
    odd_backs, rest = rest[: z.toks // 2], rest[z.toks // 2 :]
    weight, rest = rest[0], rest[1:]
    send_ref, keep_ref, source, extra, stack, index_ref, index_sem = rest
    table = pltpu.make_async_copy(index_hbm, index_ref, index_sem)
    table.start()

    @after_starts
    def _():
        gather_rows(z, pieces, gain_ref, odd_backs, stack, source, send_ref, keep_ref)

    core = lax.axis_index("tok") % 2
    half = z.tail

    @after_starts
    def _():
        for at in range(0, 2 * half, z.step):
            lanes = slice(at, at + z.step)
            extra[:, lanes] = jnp.dot(source[...], weight[:, lanes], preferred_element_type=F32)

    table.wait()
    tile_terms(z, source, delta_ref, index_ref, 0, extra, 0)
    for out_ref, side in ((send_ref, 1 - core), (keep_ref, core)):
        for p in range(0, half, z.step):
            at = pl.multiple_of(side * half + p, HEAD_DIM)
            out_ref[:, p : p + z.step] = extra[:, pl.ds(at, z.step)].astype(BF16)


def up_kernel(z, part, jobs, source, extra, up_ref, down_ref, send_ref, keep_ref, *rest):
    copies = start_copies(list(zip(weight_blocks(jobs, down_ref), rest[:-1])), rest[-1])

    @after_starts
    def _():
        core = lax.axis_index("tok") % 2
        first, size = part
        for out_ref, side in ((send_ref, 1 - core), (keep_ref, core)):
            for p in range(0, size, z.step):
                lanes = pl.ds(pl.multiple_of(side * z.tail + first + p, HEAD_DIM), z.step)
                value = jnp.dot(source[...], up_ref[:, lanes], preferred_element_type=F32)
                out_ref[:, p : p + z.step] = (value + extra[:, lanes]).astype(BF16)

    for copy in copies:
        copy.wait()


def up_tiles_kernel(z, index_hbm, delta_ref, source, extra, index_ref, index_sem):
    table = pltpu.make_async_copy(index_hbm, index_ref, index_sem)
    table.start()
    extra[...] = jnp.zeros_like(extra)
    table.wait()
    tile_terms(z, source, delta_ref, index_ref, 1, extra, 0)


def gather_rows(z, pieces, gain_ref, odd_backs, stack, source, send_ref, keep_ref):
    col = lax.axis_index("col")
    count = z.kvs * z.lane_slots
    wide = z.group * HEAD_DIM
    deep = stack.shape[0] // z.cols
    for s in range(z.cols):
        piece = pieces[s][...].astype(F32)
        if deep > count:
            piece = jnp.concatenate([piece, jnp.zeros((deep - count, wide), F32)], axis=0)
        stack[s * deep : (s + 1) * deep, :] = piece.astype(BF16)
    shape = (z.rows, z.cols * deep)
    slot = slot_of_row(z, col, shape)
    lane_of, owner = slot // z.cap % z.cols, slot // (z.cols * z.cap)
    column = lax.broadcasted_iota(jnp.int32, shape, 1)
    first = (lane_of ^ col) * deep + owner * z.cap + slot % z.cap
    squares = jnp.zeros((z.rows, 1), F32)
    for j in range(z.kvs):
        pick = (column == first + j * z.lane_slots).astype(F32).astype(BF16)
        found = jnp.dot(pick, stack[...], preferred_element_type=F32)
        squares += jnp.sum(found * found, axis=-1, keepdims=True)
        lanes = slice(j * wide, (j + 1) * wide)
        source[:, lanes] = (found * gain_ref[:, lanes]).astype(BF16)
    tail = z.tail
    for ref in (send_ref, keep_ref):
        ref[:, tail : tail + HEAD_DIM] = two_lanes(*halves(squares), z.rows)
    send_ref[:, tail + HEAD_DIM :] = jnp.zeros((z.rows, z.toks // 2 * HEAD_DIM), BF16)
    for n, ref in enumerate(odd_backs):
        lane = tail + (n + 1) * HEAD_DIM
        send_ref[: ref.shape[0], lane : lane + HEAD_DIM] = ref[...]


def add_kernel(z, mine, other, out_ref):
    size = mine.shape[1] // (2 * HEAD_DIM) * (2 * HEAD_DIM)
    out_ref[:, :size] = (mine[:, :size].astype(F32) + other[:, :size].astype(F32)).astype(BF16)
    if mine.shape[1] > size:
        lanes = slice(size, size + HEAD_DIM)
        total = mine[:, lanes].astype(F32) + other[:, lanes].astype(F32)
        out_ref[:, lanes] = two_lanes(*halves(jnp.sum(total, axis=-1, keepdims=True)), z.rows)


def hidden_kernel(z, width, *refs):
    chips = z.toks // 2
    gates, out_ref = refs[:chips], refs[-1]
    squares = sum(ref[:, z.tail : z.tail + HEAD_DIM].astype(F32) for ref in gates)
    squares = jnp.sum(squares, axis=-1, keepdims=True)
    scale = lax.rsqrt(squares * (1.0 / width) + 1e-06)
    for q, (first, size) in enumerate(z.ups):
        ups = refs[(q + 1) * chips : (q + 2) * chips]
        step = min(size, 256)
        for at in range(0, size, step):
            lanes = slice(first + at, first + at + step)
            gate = sum(ref[:, lanes].astype(F32) for ref in gates) * scale
            up = sum(ref[:, at : at + step].astype(F32) for ref in ups) * scale
            out_ref[:, lanes] = (jax.nn.silu(gate) * up).astype(BF16)


def down_products(units_ref, blocks, total, before=None):
    width = total.shape[1]
    deep = blocks[0].shape[0]
    step = min(width, 512)
    for to in range(0, width, step):
        lanes = slice(to, to + step)
        value = jnp.zeros((total.shape[0], step), F32) if before is None else before[:, lanes]
        for n, block in enumerate(blocks):
            units = units_ref[:, n * deep : (n + 1) * deep]
            value += jnp.dot(units, block[:, lanes], preferred_element_type=F32)
        total[:, lanes] = value


def down_mine_kernel(mine, *rest):
    down_products(mine, rest[:-1], rest[-1])


def down_kernel(z, index_hbm, delta_ref, before, mine, other, from_core, *rest):
    others = z.toks // 2 - 1
    evens, rest = rest[:others], rest[others:]
    blocks, rest = rest[: len(z.jobs) // 2], rest[len(z.jobs) // 2 :]
    outs, backs, rest = rest[: z.cols], rest[z.cols : z.cols + others], rest[z.cols + others :]
    source, total, fold, index_ref, index_sem = rest
    table = pltpu.make_async_copy(index_hbm, index_ref, index_sem)
    table.start()

    @after_starts
    def _():
        core = lax.axis_index("tok") % 2
        half = mine.shape[1]
        source[:, pl.ds(pl.multiple_of(core * half, half), half)] = mine[...]
        source[:, pl.ds(pl.multiple_of((1 - core) * half, half), half)] = other[...]
        down_products(other, blocks, total, before)

    for s, back in enumerate(backs):
        back[:, :HEAD_DIM] = evens[s][...]
        lane = z.tail + (s + 2) * HEAD_DIM
        back[:, HEAD_DIM:] = from_core[: back.shape[0], lane : lane + HEAD_DIM]
    table.wait()
    tile_terms(z, source, delta_ref, index_ref, 2, total, 0)
    width = total.shape[1]
    for s in range(z.cols):
        rows = slice(s * z.lane_slots, (s + 1) * z.lane_slots)
        fold[: z.lane_slots, :] = total[rows, : width // 2]
        fold[z.lane_slots :, :] = total[rows, width // 2 :]
        outs[s][...] = fold[...].astype(BF16)


def finish_kernel(z, own, from_core, *refs):
    others = z.toks // 2 - 1
    across, parts, rest = refs[:others], refs[others : others + z.cols], refs[others + z.cols :]
    attended_hbm, out_hbm, attended, out, rows, sems = rest
    tok = lax.axis_index("tok")
    block = z.cap * z.group
    count = z.kvs * block
    tail = z.tail + HEAD_DIM
    for s in range(z.toks):
        if s == 0:
            rows[s] = own[...].astype(F32)
        elif s == 1:
            rows[s] = from_core[:count, tail : tail + HEAD_DIM].astype(F32)
        else:
            lane = s % 2 * HEAD_DIM
            rows[s] = across[s // 2 - 1][:, lane : lane + HEAD_DIM].astype(F32)
        first = pl.multiple_of((tok ^ s) * z.heads * HEAD_DIM, HEAD_DIM)
        for j in range(z.kvs):
            for h in range(z.group):
                to = first + (j * z.group + h) * HEAD_DIM
                attended[:, pl.ds(to, HEAD_DIM)] = rows[
                    s, pl.ds(j * block + h, z.cap, stride=z.group), :
                ].astype(BF16)
    copies = start_copies([(attended, attended_hbm)], sems)

    @after_starts
    def _():
        total = sum(ref[...].astype(F32) for ref in parts)
        half = total.shape[1]
        out[:, :half] = total[: z.lane_slots].astype(BF16)
        out[:, half:] = total[z.lane_slots :].astype(BF16)

    copy = pltpu.make_async_copy(out, out_hbm, sems.at[1])
    copy.start()
    for copy in copies + [copy]:
        copy.wait()


def swap(array, axis, size, distance):
    return lax.ppermute(array, axis, [(i, i ^ distance) for i in range(size)])


def local(
    request_rows,
    key_cache,
    route_list,
    route_count,
    norm_gain,
    gate_weight,
    up_weight,
    down_weight,
    gate_delta,
    up_delta,
    down_delta,
    tile_index,
):
    toks, cols = lax.axis_size("tok"), lax.axis_size("col")
    cap, ctx = key_cache.shape[0], key_cache.shape[1]
    features, units = gate_weight.shape
    z = Sizes(toks, cols, cap, units)
    width = norm_gain.shape[0]
    cache_rows = cap * ctx
    lanes = 2 * z.kvs * HEAD_DIM
    piece_shape = (cap + -(-z.pieces // z.blocks), ctx, lanes)
    many = z.lane_slots * z.group
    chips = toks // 2
    gain = norm_gain.reshape(1, width)
    route_list = route_list.transpose(2, 1, 0)
    route_count = route_count.transpose(1, 0)
    tile_index = tile_index.transpose(0, 2, 4, 1, 3)
    dma = pltpu.SemaphoreType.DMA

    cuts = [0]
    for count in FETCH:
        cuts.append(cuts[-1] + count)
    *beside, final = [z.jobs[a:b] for a, b in zip(cuts, cuts[1:])]

    def shapes(some):
        return [((units // 8, down_weight.shape[1]), BF16) for _ in some]

    def traffic(some):
        moved = sum(a * b * 2 for (a, b), _ in shapes(some))
        return pl.CostEstimate(flops=0, bytes_accessed=moved, transcendentals=0)

    def product(share):
        return pl.CostEstimate(
            flops=int(2 * z.rows * features * units * share),
            bytes_accessed=int(2 * features * units * share),
            transcendentals=0,
        )

    pieces = call(
        functools.partial(pack_kernel, z, ctx),
        "pack",
        [(request_rows, HBM), (key_cache, HBM)],
        [(piece_shape, BF16)] * toks,
        [
            pltpu.VMEM(request_rows.shape, BF16),
            pltpu.VMEM(request_rows.shape, F32),
            pltpu.VMEM((toks, 2 * z.req_rows, HEAD_DIM), F32),
            dma,
            dma((toks, 2)),
        ],
        cost=product(1),
    )
    place, gain, gate_delta, up_delta = call(
        functools.partial(first_fetch_kernel, z),
        "fetch_early",
        [(a, HBM) for a in [route_list, route_count, gain, gate_delta, up_delta, gate_weight]],
        [((many, HEAD_DIM), jnp.int32), ((1, features), F32)]
        + [(gate_delta.shape, BF16), (up_delta.shape, BF16)],
        [
            pltpu.SMEM(route_list.shape, jnp.int32),
            pltpu.SMEM(route_count.shape, jnp.int32),
            dma((2,)),
            dma((3,)),
        ],
        cost=traffic([]),
        after=pieces[:1],
    )
    pieces = [pieces[0]] + [swap(pieces[s], "tok", toks, s) for s in range(1, toks)]
    back_rows = z.kvs * cap * z.group
    send, *back = call(
        functools.partial(attend_kernel, z, ctx),
        "attend",
        [(place, VMEM), (gate_weight, HBM)] + [(p, VMEM) for p in pieces[:1] + pieces[2:] + pieces[1:2]],
        [((z.kvs * z.lane_slots, z.group * HEAD_DIM), BF16)]
        + [((back_rows, HEAD_DIM), BF16)] * toks,
        [
            pltpu.VMEM((toks, cache_rows, lanes), BF16),
            pltpu.VMEM((2 * toks, z.req_rows, HEAD_DIM), BF16),
            pltpu.VMEM((z.kvs * many, HEAD_DIM), F32),
        ],
        cost=product(1),
        after=[gain],
    )
    pieces = [send] + [swap(send, "col", cols, s) for s in range(1, cols)]
    out_width = down_weight.shape[1]
    table = pltpu.SMEM(tile_index.shape, jnp.int32)
    sent, kept, source = call(
        functools.partial(first_project_kernel, z),
        "gate",
        [(tile_index, HBM), (gain, VMEM), (gate_delta, VMEM)]
        + [(p, VMEM) for p in pieces + back[1::2] + [gate_weight]],
        [
            ((z.rows, z.tail + (1 + chips) * HEAD_DIM), BF16),
            ((z.rows, z.tail + HEAD_DIM), BF16),
            ((z.rows, features), BF16),
        ],
        [
            pltpu.VMEM((z.rows, units), F32),
            pltpu.VMEM((cols * -(-z.kvs * z.lane_slots // 16) * 16, z.group * HEAD_DIM), BF16),
            table,
            dma,
        ],
        cost=product(1),
    )
    from_core = swap(sent, "tok", toks, 1)
    (extra,) = call(
        functools.partial(up_tiles_kernel, z),
        "up_tiles",
        [(tile_index, HBM), (up_delta, VMEM), (source, VMEM)],
        [((z.rows, units), F32)],
        [table, dma],
        cost=product(1 / 8),
    )
    totals = [
        call(
            functools.partial(add_kernel, z),
            "chip_sum_first",
            [(kept, VMEM), (from_core, VMEM)],
            [((z.rows, z.tail + HEAD_DIM), BF16)],
            after=[extra],
        )
    ]
    blocks = []
    for part, jobs in zip(z.ups, beside):
        size = part[1]
        sent, kept, *fetched = call(
            functools.partial(up_kernel, z, part, jobs),
            "up",
            [(a, VMEM) for a in [source, extra, up_weight]] + [(down_weight, HBM)],
            [((z.rows, size), BF16)] * 2 + shapes(jobs),
            [dma((len(jobs),))],
            cost=product(size / units * 2),
            after=totals[0],
        )
        blocks += fetched
        totals.append(
            call(
                functools.partial(add_kernel, z),
                "chip_sum_next",
                [(kept, VMEM), (swap(sent, "tok", toks, 1), VMEM)],
                [((z.rows, size), BF16)],
            )
        )
    parts = [
        total + [swap(total[0], "tok", toks, 2 * s) for s in range(1, chips)]
        for total in totals
    ]
    down_delta, *fetched = call(
        functools.partial(fetch_kernel, final),
        "fetch_down",
        [(down_weight, HBM), (down_delta, HBM)],
        [(down_delta.shape, BF16)] + shapes(final),
        [dma((len(final) + 1,))],
        cost=traffic(final),
        after=totals[-1],
    )
    blocks += fetched
    half = len(blocks) // 2
    (hidden,) = call(
        functools.partial(hidden_kernel, z, width),
        "hidden",
        [(a, VMEM) for part in parts for a in part],
        [((z.rows, units // 2), BF16)],
        after=fetched[-1:],
    )
    (before,) = call(
        down_mine_kernel,
        "down_mine",
        [(a, VMEM) for a in [hidden] + blocks[:half]],
        [((z.rows, out_width), F32)],
        cost=pl.CostEstimate(
            flops=z.rows * units * out_width, bytes_accessed=units * out_width, transcendentals=0
        ),
    )
    parts = call(
        functools.partial(down_kernel, z),
        "down",
        [(tile_index, HBM)]
        + [(a, VMEM) for a in [down_delta, before, hidden, swap(hidden, "tok", toks, 1), from_core]]
        + [(a, VMEM) for a in back[2::2] + blocks[half:]],
        [((2 * z.lane_slots, out_width // 2), BF16)] * cols
        + [((back_rows, 2 * HEAD_DIM), BF16)] * (chips - 1),
        [
            pltpu.VMEM((z.rows, units), BF16),
            pltpu.VMEM((z.rows, out_width), F32),
            pltpu.VMEM((2 * z.lane_slots, out_width // 2), F32),
            table,
            dma,
        ],
    )
    parts, across = parts[:cols], parts[cols:]
    parts = [parts[0]] + [swap(parts[s], "col", cols, s) for s in range(1, cols)]
    across = [swap(rows, "tok", toks, 2 * s + 2) for s, rows in enumerate(across)]
    attended, ffn_out = call(
        functools.partial(finish_kernel, z),
        "finish",
        [(a, VMEM) for a in [back[0], from_core] + across + parts[::-1]],
        [((cap, width), BF16), ((z.lane_slots, out_width), BF16)],
        [
            pltpu.VMEM((cap, width), BF16),
            pltpu.VMEM((z.lane_slots, out_width), BF16),
            pltpu.VMEM((toks, back_rows, HEAD_DIM), F32),
            dma((2,)),
        ],
        out=HBM,
    )
    return attended, ffn_out


def solution(mesh):
    in_specs = (
        P(("rep", "tok", "col"), None),
        P(("rep", "tok", "col"), None, None),
        P("rep", "col", None),
        P("rep", "col"),
        P(),
        P("tok", "col"),
        P("tok", "col"),
        P("col", "tok"),
        P("tok", "col", None, None, None),
        P("tok", "col", None, None, None),
        P("tok", "col", None, None, None),
        P("tok", "col", None, None, None),
    )
    out_specs = (P(("rep", "tok", "col"), None), P(("rep", "col"), "tok"))
    return jax.shard_map(local, mesh=mesh, in_specs=in_specs, out_specs=out_specs, check_vma=False)
```

```python
import functools

import jax
import jax.numpy as jnp
from jax import lax
from jax.experimental import pallas as pl
from jax.experimental.pallas import tpu as pltpu
from jax.sharding import PartitionSpec as P

HEADS = 64
KV_HEADS = 8
HEAD_DIM = 128
GROUP = HEADS // KV_HEADS
MIB = 1 << 20
FETCH = (1, 1, 5, 1)
BF16 = jnp.bfloat16
F32 = jnp.float32
VMEM = pltpu.VMEM
HBM = pltpu.HBM


def call(kernel, name, ins, outs, scratch=(), limit=8, cost=None, after=(), out=VMEM):
    if cost is None:
        cost = pl.CostEstimate(flops=0, bytes_accessed=1024, transcendentals=0)
    count = len(ins)
    ins = ins + [(a, VMEM) for a in after]

    def body(*refs):
        kernel(*refs[:count], *refs[count + len(after) :])

    return list(
        pl.pallas_call(
            body,
            name=name,
            in_specs=[pl.BlockSpec(memory_space=s) for _, s in ins],
            out_specs=[pl.BlockSpec(memory_space=out) for _ in outs],
            out_shape=[out(shape, dtype) for shape, dtype in outs],
            scratch_shapes=list(scratch),
            cost_estimate=cost,
            compiler_params=pltpu.CompilerParams(vmem_limit_bytes=limit * MIB),
        )(*[pltpu.with_memory_space_constraint(a, space) for a, space in ins])
    )


class Sizes:
    def __init__(self, toks, cols, cap, units):
        self.toks, self.cols, self.cap = toks, cols, cap
        half = units // 2
        self.ups = [(0, half // 2), (half // 2, half // 2)]
        self.tail = half
        self.step = min(512, half // 4)
        self.jobs = [(mine, at) for mine in (True, False) for at in range(0, half, half // 4)]
        self.heads = HEADS // toks
        self.kvs = max(1, self.heads // GROUP)
        self.group = self.heads // self.kvs
        self.lane_slots = toks * cap
        self.rows = toks * cols * cap
        self.req_rows = -(-(self.heads + 2 * self.kvs) // 16) * 16
        self.blocks = 2 * self.kvs
        self.pieces = 2 * self.req_rows // 16

    def first_kv(self, tok):
        return tok * self.heads // GROUP


def pack_kernel(z, ctx, req_ref, cache_ref, *rest):
    outs, (narrow, wide, rows, req_sem, sems) = rest[: z.toks], rest[z.toks :]
    tok = lax.axis_index("tok")
    width = z.kvs * HEAD_DIM
    pairs = KV_HEADS * HEAD_DIM
    fetch = pltpu.make_async_copy(req_ref, narrow, req_sem)
    fetch.start()
    copies = []
    for s in reversed(range(z.toks)):
        first = pl.multiple_of(z.first_kv(tok ^ s) * HEAD_DIM, HEAD_DIM)
        for half in range(2):
            copy = pltpu.make_async_copy(
                cache_ref.at[:, :, pl.ds(half * pairs + first, width)],
                outs[s].at[: z.cap, :, pl.ds(half * width, width)],
                sems.at[s, half],
            )
            copy.start()
            copies.append(copy)
    fetch.wait()

    @after_starts
    def _():
        rows[...] = jnp.zeros_like(rows)
        wide[...] = narrow[...].astype(F32)
        for s in range(z.toks):
            to = tok ^ s
            starts = [(to * z.heads + h) * HEAD_DIM for h in range(z.heads)]
            for half in range(2):
                starts += [
                    HEADS * HEAD_DIM + half * pairs + (z.first_kv(to) + j) * HEAD_DIM
                    for j in range(z.kvs)
                ]
            for r in range(2):
                for n, start in enumerate(starts):
                    at = r * z.req_rows + n
                    rows[s, at : at + 1, :] = wide[
                        r : r + 1, pl.ds(pl.multiple_of(start, HEAD_DIM), HEAD_DIM)
                    ]
            for p in range(z.pieces):
                at, lane = z.cap + p // z.blocks, p % z.blocks * HEAD_DIM
                outs[s][at, :, lane : lane + HEAD_DIM] = rows[s, p * 16 : p * 16 + 16, :].astype(BF16)

    for copy in copies:
        copy.wait()


def start_copies(pairs, sems):
    copies = [pltpu.make_async_copy(src, dst, sems.at[n]) for n, (src, dst) in enumerate(pairs)]
    for copy in copies:
        copy.start()
    return copies


def after_starts(compute):
    pl.when(lax.axis_index("tok") >= 0)(compute)


def weight_blocks(jobs, down_ref):
    core = lax.axis_index("tok") % 2
    half = down_ref.shape[0] // 2
    found = []
    for mine, first in jobs:
        at = pl.multiple_of((core if mine else 1 - core) * half, half)
        found.append(down_ref.at[pl.ds(at + first, half // 4), :])
    return found


def fetch_kernel(jobs, down_ref, delta_hbm, *rest):
    outs, sems = rest[:-1], rest[-1]
    for copy in start_copies(list(zip([delta_hbm] + weight_blocks(jobs, down_ref), outs)), sems):
        copy.wait()


def first_fetch_kernel(z, list_hbm, count_hbm, gain_ref, gate_delta, up_delta, _, *rest):
    place_ref, *outs = rest[:-4]
    list_ref, count_ref, table_sems, sems = rest[-4:]
    tables = start_copies([(list_hbm, list_ref), (count_hbm, count_ref)], table_sems)
    features = outs[0].shape[1]
    at = pl.multiple_of(lax.axis_index("tok") * features, features)
    sources = [gain_ref.at[:, pl.ds(at, features)], gate_delta, up_delta]
    copies = start_copies(list(zip(sources, outs)), sems)
    for table in tables:
        table.wait()

    @after_starts
    def _():
        for g in range(z.toks):
            for k in range(z.cap):
                row = jnp.where(k < count_ref[0, g], list_ref[k, 0, g], -1)
                at = (g * z.cap + k) * z.group
                place_ref[at : at + z.group, :] = jnp.full((z.group, HEAD_DIM), row, jnp.int32)

    for copy in copies:
        copy.wait()


def attend_kernel(z, ctx, place_ref, _, *rest):
    pieces, rest = rest[: z.toks], rest[z.toks :]
    pieces = pieces[:1] + pieces[-1:] + pieces[1:-1]
    send_ref, back_refs, rest = rest[0], rest[1 : 1 + z.toks], rest[1 + z.toks :]
    cache, req, mixed_all = rest

    @after_starts
    def _():
        tok = lax.axis_index("tok")
        cache_rows = z.cap * ctx
        for s in range(z.toks):
            source = tok ^ s
            cache[source] = pieces[s][: z.cap].reshape(cache_rows, cache.shape[2])
            for p in range(z.pieces):
                at, lane = z.cap + p // z.blocks, p % z.blocks * HEAD_DIM
                r, part = p * 16 // z.req_rows, p * 16 % z.req_rows
                req[source * 2 + r, part : part + 16, :] = pieces[s][at, :, lane : lane + HEAD_DIM]
        many, keys = z.lane_slots * z.group, z.toks * cache_rows
        held = 2 * z.toks * z.req_rows
        requests = req[...].reshape(held, HEAD_DIM)
        first = place_ref[:, :1]
        alive = (first >= 0).astype(F32)
        first = first * z.req_rows
        head = lax.broadcasted_iota(jnp.int32, (many, 1), 0) % z.group
        column = lax.broadcasted_iota(jnp.int32, (many, held), 1)

        def rows_at(at):
            pick = (column == first + at).astype(F32).astype(BF16)
            return jnp.dot(pick, requests, preferred_element_type=F32)

        row_slot = lax.broadcasted_iota(jnp.int32, (many, keys), 0) // z.group
        key_slot = lax.broadcasted_iota(jnp.int32, (many, keys), 1) // ctx
        same = row_slot == key_slot
        scale = HEAD_DIM ** (-0.5)
        for j in range(z.kvs):
            cached_keys = cache[:, :, j * HEAD_DIM : (j + 1) * HEAD_DIM].reshape(keys, HEAD_DIM)
            at = (z.kvs + j) * HEAD_DIM
            cached_values = cache[:, :, at : at + HEAD_DIM].reshape(keys, HEAD_DIM)
            query = rows_at(head + j * z.group)
            own_key, own_value = rows_at(z.heads + j), rows_at(z.heads + z.kvs + j)
            past = (
                lax.dot_general(
                    query.astype(BF16),
                    cached_keys,
                    (((1,), (1,)), ((), ())),
                    preferred_element_type=F32,
                )
                * scale
            )
            own = jnp.sum(query * own_key, axis=-1, keepdims=True) * scale
            top = jnp.maximum(jnp.max(jnp.where(same, past, -jnp.inf), axis=-1, keepdims=True), own)
            past_exp = jnp.where(same, jnp.exp(jnp.where(same, past - top, 0.0)), 0.0)
            own_exp = jnp.exp(own - top)
            total = jnp.sum(past_exp, axis=-1, keepdims=True) + own_exp
            weights = (past_exp / total).astype(BF16)
            own_weight = (own_exp / total).astype(BF16).astype(F32)
            mixed = jnp.dot(weights, cached_values, preferred_element_type=F32)
            mixed = (mixed + own_weight * own_value) * alive
            mixed_all[j * many : (j + 1) * many, :] = mixed.astype(BF16).astype(F32)
        block = z.cap * z.group
        for s in range(z.toks):
            for j in range(z.kvs):
                at = pl.multiple_of(j * many + (tok ^ s) * block, block if block % 8 == 0 else 4)
                back_refs[s][j * block : (j + 1) * block, :] = mixed_all[pl.ds(at, block), :].astype(BF16)
        count = z.kvs * z.lane_slots
        for h in range(z.group):
            send_ref[:, h * HEAD_DIM : (h + 1) * HEAD_DIM] = mixed_all[
                pl.ds(h, count, stride=z.group), :
            ].astype(BF16)


def halves(value):
    high = value.astype(BF16).astype(F32)
    return high, value - high


def two_lanes(high, low, rows):
    lane = lax.broadcasted_iota(jnp.int32, (rows, HEAD_DIM), 1)
    return jnp.where(lane == 0, high, jnp.where(lane == 1, low, 0.0)).astype(BF16)


def slot_of_row(z, col, shape):
    row = lax.broadcasted_iota(jnp.int32, shape, 0)
    return ((row // z.lane_slots) ^ col) * z.lane_slots + row % z.lane_slots


def tile_terms(z, source, delta_ref, index_ref, matrix, extra, out_base):
    side = delta_ref.shape[-1]
    col = lax.axis_index("col")
    variant = slot_of_row(z, col, (z.rows, side)) // (2 * z.cols * z.cap)
    for n in range(delta_ref.shape[2]):
        at = pl.multiple_of(index_ref[0, matrix, 1, 0, n] * side, side)
        to = pl.multiple_of(out_base + index_ref[0, matrix, 2, 0, n] * side, side)
        rows = jnp.where(variant == index_ref[0, matrix, 0, 0, n], source[:, pl.ds(at, side)], 0)
        extra[:, pl.ds(to, side)] += jnp.dot(
            rows.astype(BF16), delta_ref[0, 0, n], preferred_element_type=F32
        )


def first_project_kernel(z, index_hbm, gain_ref, delta_ref, *rest):
    pieces, rest = rest[: z.cols], rest[z.cols :]
    odd_backs, rest = rest[: z.toks // 2], rest[z.toks // 2 :]
    weight, rest = rest[0], rest[1:]
    send_ref, keep_ref, source, extra, stack, index_ref, index_sem = rest
    table = pltpu.make_async_copy(index_hbm, index_ref, index_sem)
    table.start()

    @after_starts
    def _():
        gather_rows(z, pieces, gain_ref, odd_backs, stack, source, send_ref, keep_ref)

    core = lax.axis_index("tok") % 2
    half = z.tail

    @after_starts
    def _():
        for at in range(0, 2 * half, z.step):
            lanes = slice(at, at + z.step)
            extra[:, lanes] = jnp.dot(source[...], weight[:, lanes], preferred_element_type=F32)

    table.wait()
    tile_terms(z, source, delta_ref, index_ref, 0, extra, 0)
    for out_ref, side in ((send_ref, 1 - core), (keep_ref, core)):
        for p in range(0, half, z.step):
            at = pl.multiple_of(side * half + p, HEAD_DIM)
            out_ref[:, p : p + z.step] = extra[:, pl.ds(at, z.step)].astype(BF16)


def up_kernel(z, part, jobs, source, extra, up_ref, down_ref, send_ref, keep_ref, *rest):
    copies = start_copies(list(zip(weight_blocks(jobs, down_ref), rest[:-1])), rest[-1])

    @after_starts
    def _():
        core = lax.axis_index("tok") % 2
        first, size = part
        for out_ref, side in ((send_ref, 1 - core), (keep_ref, core)):
            for p in range(0, size, z.step):
                lanes = pl.ds(pl.multiple_of(side * z.tail + first + p, HEAD_DIM), z.step)
                value = jnp.dot(source[...], up_ref[:, lanes], preferred_element_type=F32)
                out_ref[:, p : p + z.step] = (value + extra[:, lanes]).astype(BF16)

    for copy in copies:
        copy.wait()


def up_tiles_kernel(z, index_hbm, delta_ref, source, extra, index_ref, index_sem):
    table = pltpu.make_async_copy(index_hbm, index_ref, index_sem)
    table.start()
    extra[...] = jnp.zeros_like(extra)
    table.wait()
    tile_terms(z, source, delta_ref, index_ref, 1, extra, 0)


def gather_rows(z, pieces, gain_ref, odd_backs, stack, source, send_ref, keep_ref):
    col = lax.axis_index("col")
    count = z.kvs * z.lane_slots
    wide = z.group * HEAD_DIM
    deep = stack.shape[0] // z.cols
    for s in range(z.cols):
        piece = pieces[s][...].astype(F32)
        if deep > count:
            piece = jnp.concatenate([piece, jnp.zeros((deep - count, wide), F32)], axis=0)
        stack[s * deep : (s + 1) * deep, :] = piece.astype(BF16)
    shape = (z.rows, z.cols * deep)
    slot = slot_of_row(z, col, shape)
    lane_of, owner = slot // z.cap % z.cols, slot // (z.cols * z.cap)
    column = lax.broadcasted_iota(jnp.int32, shape, 1)
    first = (lane_of ^ col) * deep + owner * z.cap + slot % z.cap
    squares = jnp.zeros((z.rows, 1), F32)
    for j in range(z.kvs):
        pick = (column == first + j * z.lane_slots).astype(F32).astype(BF16)
        found = jnp.dot(pick, stack[...], preferred_element_type=F32)
        squares += jnp.sum(found * found, axis=-1, keepdims=True)
        lanes = slice(j * wide, (j + 1) * wide)
        source[:, lanes] = (found * gain_ref[:, lanes]).astype(BF16)
    tail = z.tail
    for ref in (send_ref, keep_ref):
        ref[:, tail : tail + HEAD_DIM] = two_lanes(*halves(squares), z.rows)
    send_ref[:, tail + HEAD_DIM :] = jnp.zeros((z.rows, z.toks // 2 * HEAD_DIM), BF16)
    for n, ref in enumerate(odd_backs):
        lane = tail + (n + 1) * HEAD_DIM
        send_ref[: ref.shape[0], lane : lane + HEAD_DIM] = ref[...]


def add_kernel(z, mine, other, out_ref):
    size = mine.shape[1] // (2 * HEAD_DIM) * (2 * HEAD_DIM)
    out_ref[:, :size] = (mine[:, :size].astype(F32) + other[:, :size].astype(F32)).astype(BF16)
    if mine.shape[1] > size:
        lanes = slice(size, size + HEAD_DIM)
        total = mine[:, lanes].astype(F32) + other[:, lanes].astype(F32)
        out_ref[:, lanes] = two_lanes(*halves(jnp.sum(total, axis=-1, keepdims=True)), z.rows)


def hidden_kernel(z, width, *refs):
    chips = z.toks // 2
    gates, out_ref = refs[:chips], refs[-1]
    squares = sum(ref[:, z.tail : z.tail + HEAD_DIM].astype(F32) for ref in gates)
    squares = jnp.sum(squares, axis=-1, keepdims=True)
    scale = lax.rsqrt(squares * (1.0 / width) + 1e-06)
    for q, (first, size) in enumerate(z.ups):
        ups = refs[(q + 1) * chips : (q + 2) * chips]
        step = min(size, 256)
        for at in range(0, size, step):
            lanes = slice(first + at, first + at + step)
            gate = sum(ref[:, lanes].astype(F32) for ref in gates) * scale
            up = sum(ref[:, at : at + step].astype(F32) for ref in ups) * scale
            out_ref[:, lanes] = (jax.nn.silu(gate) * up).astype(BF16)


def down_products(units_ref, blocks, total, before=None):
    width = total.shape[1]
    deep = blocks[0].shape[0]
    step = min(width, 512)
    for to in range(0, width, step):
        lanes = slice(to, to + step)
        value = jnp.zeros((total.shape[0], step), F32) if before is None else before[:, lanes]
        for n, block in enumerate(blocks):
            units = units_ref[:, n * deep : (n + 1) * deep]
            value += jnp.dot(units, block[:, lanes], preferred_element_type=F32)
        total[:, lanes] = value


def down_mine_kernel(z, jobs, down_ref, mine, *rest):
    blocks, (total, *fetched, sems) = rest[: len(z.jobs) // 2], rest[len(z.jobs) // 2 :]
    copies = start_copies(list(zip(weight_blocks(jobs, down_ref), fetched)), sems)
    after_starts(lambda: down_products(mine, blocks, total))
    for copy in copies:
        copy.wait()


def down_kernel(z, index_hbm, delta_ref, before, mine, other, from_core, *rest):
    others = z.toks // 2 - 1
    evens, rest = rest[:others], rest[others:]
    blocks, rest = rest[: len(z.jobs) // 2], rest[len(z.jobs) // 2 :]
    outs, backs, rest = rest[: z.cols], rest[z.cols : z.cols + others], rest[z.cols + others :]
    source, total, fold, index_ref, index_sem = rest
    table = pltpu.make_async_copy(index_hbm, index_ref, index_sem)
    table.start()

    @after_starts
    def _():
        core = lax.axis_index("tok") % 2
        half = mine.shape[1]
        source[:, pl.ds(pl.multiple_of(core * half, half), half)] = mine[...]
        source[:, pl.ds(pl.multiple_of((1 - core) * half, half), half)] = other[...]
        down_products(other, blocks, total, before)

    for s, back in enumerate(backs):
        back[:, :HEAD_DIM] = evens[s][...]
        lane = z.tail + (s + 2) * HEAD_DIM
        back[:, HEAD_DIM:] = from_core[: back.shape[0], lane : lane + HEAD_DIM]
    table.wait()
    tile_terms(z, source, delta_ref, index_ref, 2, total, 0)
    width = total.shape[1]
    for s in range(z.cols):
        rows = slice(s * z.lane_slots, (s + 1) * z.lane_slots)
        fold[: z.lane_slots, :] = total[rows, : width // 2]
        fold[z.lane_slots :, :] = total[rows, width // 2 :]
        outs[s][...] = fold[...].astype(BF16)


def finish_kernel(z, own, from_core, *refs):
    others = z.toks // 2 - 1
    across, parts, rest = refs[:others], refs[others : others + z.cols], refs[others + z.cols :]
    attended_hbm, out_hbm, attended, out, rows, sems = rest
    tok = lax.axis_index("tok")
    block = z.cap * z.group
    count = z.kvs * block
    tail = z.tail + HEAD_DIM
    for s in range(z.toks):
        if s == 0:
            rows[s] = own[...].astype(F32)
        elif s == 1:
            rows[s] = from_core[:count, tail : tail + HEAD_DIM].astype(F32)
        else:
            lane = s % 2 * HEAD_DIM
            rows[s] = across[s // 2 - 1][:, lane : lane + HEAD_DIM].astype(F32)
        first = pl.multiple_of((tok ^ s) * z.heads * HEAD_DIM, HEAD_DIM)
        for j in range(z.kvs):
            for h in range(z.group):
                to = first + (j * z.group + h) * HEAD_DIM
                attended[:, pl.ds(to, HEAD_DIM)] = rows[
                    s, pl.ds(j * block + h, z.cap, stride=z.group), :
                ].astype(BF16)
    copies = start_copies([(attended, attended_hbm)], sems)

    @after_starts
    def _():
        total = sum(ref[...].astype(F32) for ref in parts)
        half = total.shape[1]
        out[:, :half] = total[: z.lane_slots].astype(BF16)
        out[:, half:] = total[z.lane_slots :].astype(BF16)

    copy = pltpu.make_async_copy(out, out_hbm, sems.at[1])
    copy.start()
    for copy in copies + [copy]:
        copy.wait()


def swap(array, axis, size, distance):
    return lax.ppermute(array, axis, [(i, i ^ distance) for i in range(size)])


def local(
    request_rows,
    key_cache,
    route_list,
    route_count,
    norm_gain,
    gate_weight,
    up_weight,
    down_weight,
    gate_delta,
    up_delta,
    down_delta,
    tile_index,
):
    toks, cols = lax.axis_size("tok"), lax.axis_size("col")
    cap, ctx = key_cache.shape[0], key_cache.shape[1]
    features, units = gate_weight.shape
    z = Sizes(toks, cols, cap, units)
    width = norm_gain.shape[0]
    cache_rows = cap * ctx
    lanes = 2 * z.kvs * HEAD_DIM
    piece_shape = (cap + -(-z.pieces // z.blocks), ctx, lanes)
    many = z.lane_slots * z.group
    chips = toks // 2
    gain = norm_gain.reshape(1, width)
    route_list = route_list.transpose(2, 1, 0)
    route_count = route_count.transpose(1, 0)
    tile_index = tile_index.transpose(0, 2, 4, 1, 3)
    dma = pltpu.SemaphoreType.DMA

    cuts = [0]
    for count in FETCH:
        cuts.append(cuts[-1] + count)
    *beside, final, ending = [z.jobs[a:b] for a, b in zip(cuts, cuts[1:])]

    def shapes(some):
        return [((units // 8, down_weight.shape[1]), BF16) for _ in some]

    def traffic(some):
        moved = sum(a * b * 2 for (a, b), _ in shapes(some))
        return pl.CostEstimate(flops=0, bytes_accessed=moved, transcendentals=0)

    def product(share):
        return pl.CostEstimate(
            flops=int(2 * z.rows * features * units * share),
            bytes_accessed=int(2 * features * units * share),
            transcendentals=0,
        )

    pieces = call(
        functools.partial(pack_kernel, z, ctx),
        "pack",
        [(request_rows, HBM), (key_cache, HBM)],
        [(piece_shape, BF16)] * toks,
        [
            pltpu.VMEM(request_rows.shape, BF16),
            pltpu.VMEM(request_rows.shape, F32),
            pltpu.VMEM((toks, 2 * z.req_rows, HEAD_DIM), F32),
            dma,
            dma((toks, 2)),
        ],
        cost=product(1),
    )
    place, gain, gate_delta, up_delta = call(
        functools.partial(first_fetch_kernel, z),
        "fetch_early",
        [(a, HBM) for a in [route_list, route_count, gain, gate_delta, up_delta, gate_weight]],
        [((many, HEAD_DIM), jnp.int32), ((1, features), F32)]
        + [(gate_delta.shape, BF16), (up_delta.shape, BF16)],
        [
            pltpu.SMEM(route_list.shape, jnp.int32),
            pltpu.SMEM(route_count.shape, jnp.int32),
            dma((2,)),
            dma((3,)),
        ],
        cost=traffic([]),
        after=pieces[:1],
    )
    pieces = [pieces[0]] + [swap(pieces[s], "tok", toks, s) for s in range(1, toks)]
    back_rows = z.kvs * cap * z.group
    send, *back = call(
        functools.partial(attend_kernel, z, ctx),
        "attend",
        [(place, VMEM), (gate_weight, HBM)] + [(p, VMEM) for p in pieces[:1] + pieces[2:] + pieces[1:2]],
        [((z.kvs * z.lane_slots, z.group * HEAD_DIM), BF16)]
        + [((back_rows, HEAD_DIM), BF16)] * toks,
        [
            pltpu.VMEM((toks, cache_rows, lanes), BF16),
            pltpu.VMEM((2 * toks, z.req_rows, HEAD_DIM), BF16),
            pltpu.VMEM((z.kvs * many, HEAD_DIM), F32),
        ],
        cost=product(1),
        after=[gain],
    )
    pieces = [send] + [swap(send, "col", cols, s) for s in range(1, cols)]
    out_width = down_weight.shape[1]
    table = pltpu.SMEM(tile_index.shape, jnp.int32)
    sent, kept, source = call(
        functools.partial(first_project_kernel, z),
        "gate",
        [(tile_index, HBM), (gain, VMEM), (gate_delta, VMEM)]
        + [(p, VMEM) for p in pieces + back[1::2] + [gate_weight]],
        [
            ((z.rows, z.tail + (1 + chips) * HEAD_DIM), BF16),
            ((z.rows, z.tail + HEAD_DIM), BF16),
            ((z.rows, features), BF16),
        ],
        [
            pltpu.VMEM((z.rows, units), F32),
            pltpu.VMEM((cols * -(-z.kvs * z.lane_slots // 16) * 16, z.group * HEAD_DIM), BF16),
            table,
            dma,
        ],
        cost=product(1),
    )
    from_core = swap(sent, "tok", toks, 1)
    (extra,) = call(
        functools.partial(up_tiles_kernel, z),
        "up_tiles",
        [(tile_index, HBM), (up_delta, VMEM), (source, VMEM)],
        [((z.rows, units), F32)],
        [table, dma],
        cost=product(1 / 8),
    )
    totals = [
        call(
            functools.partial(add_kernel, z),
            "chip_sum_first",
            [(kept, VMEM), (from_core, VMEM)],
            [((z.rows, z.tail + HEAD_DIM), BF16)],
            after=[extra],
        )
    ]
    blocks = []
    for part, jobs in zip(z.ups, beside):
        size = part[1]
        sent, kept, *fetched = call(
            functools.partial(up_kernel, z, part, jobs),
            "up",
            [(a, VMEM) for a in [source, extra, up_weight]] + [(down_weight, HBM)],
            [((z.rows, size), BF16)] * 2 + shapes(jobs),
            [dma((len(jobs),))],
            cost=product(size / units * 2),
            after=totals[0],
        )
        blocks += fetched
        totals.append(
            call(
                functools.partial(add_kernel, z),
                "chip_sum_next",
                [(kept, VMEM), (swap(sent, "tok", toks, 1), VMEM)],
                [((z.rows, size), BF16)],
            )
        )
    parts = [
        total + [swap(total[0], "tok", toks, 2 * s) for s in range(1, chips)]
        for total in totals
    ]
    down_delta, *fetched = call(
        functools.partial(fetch_kernel, final),
        "fetch_down",
        [(down_weight, HBM), (down_delta, HBM)],
        [(down_delta.shape, BF16)] + shapes(final),
        [dma((len(final) + 1,))],
        cost=traffic(final),
        after=totals[-1],
    )
    blocks += fetched
    half = len(z.jobs) // 2
    (hidden,) = call(
        functools.partial(hidden_kernel, z, width),
        "hidden",
        [(a, VMEM) for part in parts for a in part],
        [((z.rows, units // 2), BF16)],
        after=fetched[-1:],
    )
    before, *fetched = call(
        functools.partial(down_mine_kernel, z, ending),
        "down_mine",
        [(down_weight, HBM)] + [(a, VMEM) for a in [hidden] + blocks[:half]],
        [((z.rows, out_width), F32)] + shapes(ending),
        [dma((len(ending),))],
        cost=pl.CostEstimate(
            flops=z.rows * units * out_width, bytes_accessed=units * out_width, transcendentals=0
        ),
    )
    blocks += fetched
    parts = call(
        functools.partial(down_kernel, z),
        "down",
        [(tile_index, HBM)]
        + [(a, VMEM) for a in [down_delta, before, hidden, swap(hidden, "tok", toks, 1), from_core]]
        + [(a, VMEM) for a in back[2::2] + blocks[half:]],
        [((2 * z.lane_slots, out_width // 2), BF16)] * cols
        + [((back_rows, 2 * HEAD_DIM), BF16)] * (chips - 1),
        [
            pltpu.VMEM((z.rows, units), BF16),
            pltpu.VMEM((z.rows, out_width), F32),
            pltpu.VMEM((2 * z.lane_slots, out_width // 2), F32),
            table,
            dma,
        ],
    )
    parts, across = parts[:cols], parts[cols:]
    parts = [parts[0]] + [swap(parts[s], "col", cols, s) for s in range(1, cols)]
    across = [swap(rows, "tok", toks, 2 * s + 2) for s, rows in enumerate(across)]
    attended, ffn_out = call(
        functools.partial(finish_kernel, z),
        "finish",
        [(a, VMEM) for a in [back[0], from_core] + across + parts[::-1]],
        [((cap, width), BF16), ((z.lane_slots, out_width), BF16)],
        [
            pltpu.VMEM((cap, width), BF16),
            pltpu.VMEM((z.lane_slots, out_width), BF16),
            pltpu.VMEM((toks, back_rows, HEAD_DIM), F32),
            dma((2,)),
        ],
        out=HBM,
    )
    return attended, ffn_out


def solution(mesh):
    in_specs = (
        P(("rep", "tok", "col"), None),
        P(("rep", "tok", "col"), None, None),
        P("rep", "col", None),
        P("rep", "col"),
        P(),
        P("tok", "col"),
        P("tok", "col"),
        P("col", "tok"),
        P("tok", "col", None, None, None),
        P("tok", "col", None, None, None),
        P("tok", "col", None, None, None),
        P("tok", "col", None, None, None),
    )
    out_specs = (P(("rep", "tok", "col"), None), P(("rep", "col"), "tok"))
    return jax.shard_map(local, mesh=mesh, in_specs=in_specs, out_specs=out_specs, check_vma=False)
```
